32 devices in a mesh: users: 32 (over z, y, x, core).
Axes of the slice: x: 2, y: 2, z: 4, core: 2. Of those that a mesh axis runs over, the one named last changes fastest.
Arguments:
- tile_owner: int32 [2048, 1], P('users'), may hold values from 0 to 31; in each aligned block of 64 rows (0 to 63, 64 to 127, ...) at most 2 rows name the same one
- tile_slot: int32 [2048], P('users'), may hold values from 0 to 15
- tile_cblock: int32 [2048], P('users'), may hold values from 0 to 63
- tile_context: int32 [2048, 512], P('users'), may hold values from 0 to 7
- tile_weights: bfloat16 [2048, 128, 512], P('users'), as said below
- item_factors: bfloat16 [512, 64, 128], P('users'), may hold values from -0.5 to 0.5
- context_factors: bfloat16 [8, 512], replicated, may hold values from -0.75 to 0.75
- user_basis: float32 [16384, 128], P('users'), may hold values from -6 to 6
- user_counts: int32 [32], P('users'), may hold values from 256 to 512, as said below
Outputs:
- basis: float32 [16384, 128], P('users')
- core_out: float32 [128, 512], replicated
The draws below stay inside these ranges and needn't reach their ends.
Inputs may be any that keep to these rules, and one draw needn't show every extreme that they name: `tile_owner`: among the 64 tiles of one device (aligned blocks of 64 rows), at most 2 name the same owner, and this is reached. `user_counts`: rows of a device at and beyond its count carry no events; some device has 512 live rows and some 512 // 2. tile_weights[t, :, u] is zero for u >= user_counts[t // 64].
All inputs are finite; a program needn't handle non-finite values.
Results may differ from the reference program's by a relative error of at most 0.006.
Values may be sent and summed in bfloat16 or wider, within the bound.
No kernel may reach another device: no remote copies, remote signals or barrier semaphores. Data moves between devices by JAX's collectives and lax.ppermute only.
A program may use at most 128 MiB of HBM per device.

```python
import math
import jax
import jax.numpy as jnp
import numpy as np
from jax import lax

RU = 128
RI = 64
RC = 8
CTX = 512
CB = 8
IBLK = 128
U_DEV = 512
SLOTS = 2
TD = 64
IBD = 16
USERS = 16384
TILES = 2048
ITEM_BLOCKS = 512
N_USERS = 32


def counts_common(key):
    base_key = jax.random.fold_in(key, 7301)
    first_key, second_key, third_key = jax.random.split(base_key, 3)
    counts = jax.random.randint(first_key, (N_USERS,), U_DEV // 2, U_DEV + 1)
    fullest = jax.random.randint(second_key, (), 0, N_USERS)
    counts = counts.at[fullest].set(U_DEV)
    emptiest = (fullest + 1 + jax.random.randint(third_key, (), 0, N_USERS - 1)) % N_USERS
    counts = counts.at[emptiest].set(U_DEV // 2)
    return counts.astype(jnp.int32)


def draw_user_counts(key, part):
    return counts_common(key)


def draw_tile_weights(key, part):
    counts = counts_common(key)
    value_key = jax.random.fold_in(key, 9157)
    values = jnp.clip(jax.random.normal(value_key, (TILES, IBLK, U_DEV), jnp.float32), -6.0, 6.0)
    owner_of = jnp.arange(TILES, dtype=jnp.int32) // TD
    limit = counts[owner_of]
    living = jnp.arange(U_DEV, dtype=jnp.int32)[None, :] < limit[:, None]
    values = jnp.where(living[:, None, :], values, jnp.zeros_like(values))
    return values.astype(jnp.bfloat16)


def plant(entries, rng, smallest, largest):
    dims = entries.shape
    index_at = [jax.random.randint(jax.random.fold_in(rng, axis), (), 0, dims[axis]) for axis in range(len(dims))]
    entries = entries.at[tuple(index_at)].set(smallest)
    longest = dims.index(max(dims))
    index_at[longest] = (index_at[longest] + 1) % dims[longest]
    return entries.at[tuple(index_at)].set(largest)


def block_scale(key, extent, cuts, smallest, high):
    gain, own = 1.0, jax.random.fold_in(key, 6)
    for position, shards_of in cuts:
        steps = jnp.exp(jax.random.uniform(jax.random.fold_in(own, position), (shards_of,), jnp.float32, smallest / len(cuts), high / len(cuts)))
        gain = gain * jnp.repeat(steps, extent[position] // shards_of).reshape([-1 if axis == position else 1 for axis in range(len(extent))])
    return gain


def assign_block(own_key, own, number, rows, count, top, most, slope):
    order = jax.random.permutation(own_key, count)
    packed, ordinary = shares(count, rows * top, most, slope, True), shares(count, rows * top, most, slope, False)
    places = jnp.arange(count)

    def named(lengths, offset_by):
        used = int((lengths > 0).sum())
        fixed = max(1, used // 4)
        shifted = fixed + (places - fixed + offset_by * (used - fixed)) % max(1, count - fixed)
        return jnp.zeros((count,), jnp.int32).at[order[jnp.where(places < fixed, places, shifted)]].set(jnp.asarray(lengths, jnp.int32))

    lengths = jnp.where(number % 4 == 0, named(packed, number // 4), named(ordinary, number - number // 4 - 1))
    mixed = jax.random.permutation(jax.random.fold_in(own, 3), count)
    donor, taker = mixed[0:count // 2 * 2:2], mixed[1:count // 2 * 2:2]
    slack = jnp.minimum(lengths[donor] - 1, most - lengths[taker]) // 2
    slack = jnp.where((donor == order[0]) | (taker == order[0]) | (lengths[taker] == 0), 0, jnp.maximum(slack, 0))
    shifted = jax.random.randint(jax.random.fold_in(own, 4), (count // 2,), 0, 1 << 20) % (slack + 1)
    lengths = lengths.at[donor].add(-shifted).at[taker].add(shifted)
    labels = jnp.searchsorted(jnp.cumsum(lengths), jnp.arange(rows * top), side="right").astype(jnp.int32)
    table = labels.reshape(top, rows).T
    table = table[jax.random.permutation(jax.random.fold_in(own, 1), rows)]
    offset_by = jax.random.randint(jax.random.fold_in(own, 2), (rows, 1), 0, top)
    return jnp.take_along_axis(table, (jnp.arange(top)[None, :] + offset_by) % top, axis=1)


def shares(count, total, reach, skew, full):
    weights = [(1 << 20) // math.isqrt(grade ** skew) + 1 for grade in range(1, count + 1)]
    largest = reach if full else min(reach, max(-(-total // count), total * weights[0] // sum(weights)))
    least = 1 if total - largest >= count - 1 else 0
    given, surplus = [largest] + [least] * (count - 1), total - largest - least * (count - 1)
    while surplus > 0:
        candidates = [i for i in range(1, count) if given[i] < largest] or [i for i in range(1, count) if given[i] < reach]
        mass, left = sum([weights[i] for i in candidates]), surplus
        for i in candidates:
            extra = min(reach - given[i], max(1, left * weights[i] // mass), surplus)
            given[i] = given[i] + extra
            surplus = surplus - extra
    return np.array(given)


def scatter_about(own_key, dims, width, most, cuts=(), kind=jnp.bfloat16):
    loudness = block_scale(own_key, dims, cuts, -0.22, 0.18) if cuts else 1.0
    result = jax.random.normal(own_key, dims, jnp.float32) * width * loudness
    return jnp.minimum(jnp.maximum(result, -most), most).astype(kind)


def setup_inputs(seed: int = 0) -> dict:
    seeds = jax.random.split(jax.random.key(seed), 10)
    tile_owner_keys = jax.random.split(jax.random.fold_in(seeds[0], 1), TILES // TD)
    tile_owner_turns = jax.random.permutation(jax.random.fold_in(seeds[0], 3), TILES // TD)
    tile_owner = jax.vmap(lambda own, number: assign_block(jax.random.fold_in(seeds[0], 2), own, number, TD, N_USERS, 1, SLOTS, 2))(tile_owner_keys, tile_owner_turns).reshape((TILES, 1))
    tile_slot = plant(jax.random.randint(seeds[1], (TILES,), 0, IBD), jax.random.fold_in(seeds[1], 1), 0, IBD - 1).astype(jnp.int32)
    tile_cblock = plant(jax.random.randint(seeds[2], (TILES,), 0, CTX // CB), jax.random.fold_in(seeds[2], 1), 0, (CTX // CB) - 1).astype(jnp.int32)
    tile_context = plant(jax.random.randint(seeds[3], (TILES, U_DEV), 0, CB), jax.random.fold_in(seeds[3], 1), 0, CB - 1).astype(jnp.int32)
    tile_weights = draw_tile_weights(jax.random.fold_in(seeds[9], 71), 0)
    item_factors = scatter_about(seeds[5], (ITEM_BLOCKS, RI, IBLK), IBLK ** -0.5, 0.5, ((0, 32),))
    context_factors = scatter_about(seeds[6], (RC, CTX), TD ** -0.5, 0.75)
    user_basis = scatter_about(seeds[7], (USERS, RU), 1.0, 6.0, ((0, 32),), jnp.float32)
    user_counts = draw_user_counts(jax.random.fold_in(seeds[9], 71), 0)
    return dict(tile_owner=tile_owner, tile_slot=tile_slot, tile_cblock=tile_cblock, tile_context=tile_context, tile_weights=tile_weights, item_factors=item_factors, context_factors=context_factors, user_basis=user_basis, user_counts=user_counts)


def reference(tile_owner, tile_slot, tile_cblock, tile_context, tile_weights, item_factors, context_factors, user_basis, user_counts):
    lookup = context_factors.astype(jnp.float32)
    factors_all = item_factors

    def device_rows(device_pack):
        owners, slots_of, cblocks, contexts, weights, count = device_pack
        blocks = factors_all[owners * IBD + slots_of].astype(jnp.float32)
        products = jnp.einsum('tai,tiu->tau', blocks, weights.astype(jnp.float32)).astype(jnp.bfloat16)
        columns = cblocks[:, None] * CB + contexts
        context_values = lookup[:, columns]
        rows_out = jnp.einsum('rtu,tau->rau', context_values, products.astype(jnp.float32))
        rows_out = rows_out.reshape(RC * RI, U_DEV)
        living = jnp.arange(U_DEV) < count
        rows_out = jnp.where(living[None, :], rows_out, jnp.zeros_like(rows_out))
        return rows_out.T
    device_pack = (tile_owner[:, 0].reshape(N_USERS, TD), tile_slot.reshape(N_USERS, TD), tile_cblock.reshape(N_USERS, TD), tile_context.reshape(N_USERS, TD, U_DEV), tile_weights.reshape(N_USERS, TD, IBLK, U_DEV), user_counts)
    ydata = lax.map(device_rows, device_pack).reshape(USERS, RC * RI)
    projection = jnp.dot(ydata.T, user_basis, precision=lax.Precision.HIGHEST)
    projected = jnp.dot(ydata, projection, precision=lax.Precision.HIGHEST)
    factor_q, factor_r = jnp.linalg.qr(projected)
    sign_fix = jnp.sign(jnp.diagonal(factor_r))
    basis = factor_q * sign_fix[None, :] * jnp.sqrt(jnp.float32(USERS))
    core_out = jnp.dot(basis.T, ydata, precision=lax.Precision.HIGHEST) / jnp.float32(USERS)
    return (basis, core_out)
```

```python
import functools

import jax
import jax.numpy as jnp
from jax import lax
from jax.experimental import pallas as pl
from jax.experimental.pallas import tpu as pltpu
from jax.sharding import PartitionSpec as P

CB = 8
SLOTS = 2
HIGH = lax.Precision.HIGHEST
LANES = 128
ROWS = 8


def dot_f32(lhs, rhs, contract):
    return lax.dot_general(
        lhs, rhs, ((contract[:1], contract[1:]), ((), ())),
        precision=HIGH, preferred_element_type=jnp.float32,
    )


def route_kernel(tiles, devices, owner_ref, slot_ref, request_ref, where_ref, used_ref):
    def clear(place, _):
        used_ref[place] = 0
        for slot in range(SLOTS):
            request_ref[place * SLOTS + slot] = 0
        return 0

    lax.fori_loop(0, devices, clear, 0)

    def assign(tile, _):
        owner = owner_ref[tile]
        taken = used_ref[owner]
        used_ref[owner] = taken + 1
        place = owner * SLOTS + taken
        request_ref[place] = slot_ref[tile]
        where_ref[tile] = place
        return 0

    lax.fori_loop(0, tiles, assign, 0)


def route(owners, slots, devices):
    tiles = owners.shape[0]
    smem = pl.BlockSpec(memory_space=pltpu.SMEM)
    return pl.pallas_call(
        functools.partial(route_kernel, tiles, devices),
        out_shape=(
            jax.ShapeDtypeStruct((devices * SLOTS,), jnp.int32),
            jax.ShapeDtypeStruct((tiles,), jnp.int32),
        ),
        in_specs=[smem, smem],
        out_specs=(smem, smem),
        scratch_shapes=[pltpu.SMEM((devices,), jnp.int32)],
        name="route",
    )(owners, slots)


def context_kernel(tiles, cblock_ref, table_ref, context_ref, out_ref):
    users = context_ref.shape[1]

    def one(tile, _):
        table = table_ref[cblock_ref[tile]]
        marks = jnp.broadcast_to(context_ref[pl.ds(tile, 1), :], (ROWS, users))
        total = jnp.zeros((ROWS, users), jnp.float32)
        for k in range(CB):
            column = jnp.broadcast_to(table[:, k : k + 1], (ROWS, users))
            total = jnp.where(marks == k, column, total)
        out_ref[tile] = total
        return 0

    lax.fori_loop(0, tiles, one, 0)


def context_values(cblock, table, context):
    tiles, users = context.shape
    vmem = pl.BlockSpec(memory_space=pltpu.VMEM)
    return pl.pallas_call(
        functools.partial(context_kernel, tiles),
        out_shape=jax.ShapeDtypeStruct((tiles, ROWS, users), jnp.float32),
        in_specs=[pl.BlockSpec(memory_space=pltpu.SMEM), vmem, vmem],
        out_specs=vmem,
        name="contexts",
    )(cblock, table, context)


def tiles_kernel(
    step_tiles, where_ref, count_ref, core_ref,
    blocks_ref, weights_ref, context_ref, basis_ref,
    y_ref, keep_ref, send_ref, product_ref, pack_ref,
):
    step = pl.program_id(0)
    rank_i = blocks_ref.shape[1]
    users = weights_ref.shape[2]
    rank_c = context_ref.shape[1]

    @pl.when(step == 0)
    def _():
        y_ref[...] = jnp.zeros_like(y_ref)

    for tile in range(step_tiles):
        block = blocks_ref[where_ref[step * step_tiles + tile]]
        product = jnp.dot(block, weights_ref[tile], preferred_element_type=jnp.float32)
        product_ref[tile] = product.astype(jnp.bfloat16).astype(jnp.float32)

    half = rank_i // 2
    for lane in range(users // LANES):
        lanes = slice(lane * LANES, (lane + 1) * LANES)
        for part in range(2):
            rows = slice(part * half, (part + 1) * half)
            total = y_ref[:, rows, lanes]
            for tile in range(step_tiles):
                values = context_ref[tile, :, lanes]
                total = total + values[:, None, :] * product_ref[tile, rows, lanes][None]
            y_ref[:, rows, lanes] = total

    @pl.when(step == pl.num_programs(0) - 1)
    def _():
        living = lax.broadcasted_iota(jnp.int32, (rank_i, users), 1) < count_ref[0]
        for r in range(rank_c):
            y_ref[r] = jnp.where(living, y_ref[r], 0.0)
        ytrans = y_ref[...].reshape(rank_c * rank_i, users)
        groups = ytrans.shape[0] // LANES
        place = 0
        for i in range(groups):
            upper = ytrans[i * LANES : (i + 1) * LANES]
            for j in range(i, groups):
                pack_ref[place] = dot_f32(upper, ytrans[j * LANES : (j + 1) * LANES], (1, 1))
                place += 1
        for i in range(groups):
            pack_ref[place] = dot_f32(ytrans[i * LANES : (i + 1) * LANES], basis_ref[...], (1, 0))
            place += 1
        core = core_ref[0]
        part = place // 2
        for i in range(part):
            keep_ref[i] = pack_ref[core * part + i]
            send_ref[i] = pack_ref[(1 - core) * part + i]


def tile_sums(where, count, core, blocks, weights, contexts, user_basis):
    tiles, block_len, users = weights.shape
    rank_i = blocks.shape[1]
    rank_c = contexts.shape[1]
    rank_u = user_basis.shape[1]
    step_tiles = 8
    groups = rank_c * rank_i // LANES
    pack = groups * (groups + 1) // 2 + groups
    whole = lambda *shape: pl.BlockSpec(shape, lambda s, *_: (0,) * len(shape))
    return pl.pallas_call(
        functools.partial(tiles_kernel, step_tiles),
        out_shape=(
            jax.ShapeDtypeStruct((rank_c, rank_i, users), jnp.float32),
            jax.ShapeDtypeStruct((pack // 2, LANES, rank_u), jnp.float32),
            jax.ShapeDtypeStruct((pack // 2, LANES, rank_u), jnp.float32),
        ),
        grid_spec=pltpu.PrefetchScalarGridSpec(
            num_scalar_prefetch=3,
            grid=(tiles // step_tiles,),
            in_specs=[
                whole(*blocks.shape),
                pl.BlockSpec((step_tiles, block_len, users), lambda s, *_: (s, 0, 0)),
                pl.BlockSpec((step_tiles, rank_c, users), lambda s, *_: (s, 0, 0)),
                whole(*user_basis.shape),
            ],
            out_specs=(
                whole(rank_c, rank_i, users),
                whole(pack // 2, LANES, rank_u),
                whole(pack // 2, LANES, rank_u),
            ),
            scratch_shapes=[
                pltpu.VMEM((step_tiles, rank_i, users), jnp.float32),
                pltpu.VMEM((pack, LANES, rank_u), jnp.float32),
            ],
        ),
        compiler_params=pltpu.CompilerParams(vmem_limit_bytes=28 * 2**20),
        cost_estimate=pl.CostEstimate(flops=2 * 10**9, bytes_accessed=12 * 10**6, transcendentals=0),
        name="tile_sums",
    )(where, count, core, blocks, weights, contexts, user_basis)


def inverse_factor(gram):
    order = gram.shape[0]
    panels = order // ROWS
    sub = lax.broadcasted_iota(jnp.int32, (ROWS, order), 0)
    lane = lax.broadcasted_iota(jnp.int32, (ROWS, order), 1)
    left = [gram[ROWS * i : ROWS * (i + 1)] for i in range(panels)]
    right = [jnp.where(lane == sub + ROWS * i, 1.0, 0.0) for i in range(panels)]
    for k in range(panels):
        columns = {
            i: [
                jnp.broadcast_to(left[i][:, ROWS * k + j : ROWS * k + j + 1], (ROWS, order))
                for j in range(ROWS)
            ]
            for i in range(k, panels)
        }
        row, tail = left[k], right[k]
        scale = jnp.zeros((ROWS, order), jnp.float32)
        rows, tails = [], []
        for j in range(ROWS):
            head = columns[k][j]
            pivot = jnp.broadcast_to(head[j : j + 1], (ROWS, order))
            inverse = pl.reciprocal(pivot, approx=True)
            inverse = inverse * (2.0 - pivot * inverse)
            scale = jnp.where(sub == j, pivot, scale)
            rows.append(jnp.broadcast_to(row[j : j + 1], (ROWS, order)))
            tails.append(jnp.broadcast_to(tail[j : j + 1], (ROWS, order)))
            below = jnp.where(sub > j, head, 0.0) * inverse
            row = row - below * rows[j]
            tail = tail - below * tails[j]
            facts = {k: below}
            for i in range(k + 1, panels):
                facts[i] = columns[i][j] * inverse
            for c in range(j + 1, ROWS):
                crossing = jnp.broadcast_to(head[c : c + 1], (ROWS, order))
                for i in range(k, panels):
                    columns[i][c] = columns[i][c] - facts[i] * crossing
            for i in range(k + 1, panels):
                left[i] = left[i] - facts[i] * rows[j]
                right[i] = right[i] - facts[i] * tails[j]
        right[k] = tail * lax.rsqrt(scale)
    return jnp.concatenate(right, axis=0)


def finish_kernel(total_users, core_ref, mine_ref, other_ref, y_ref, basis_ref, core_out_ref, pack_ref, full_ref):
    core = core_ref[0]
    part = mine_ref.shape[0]
    for i in range(part):
        pack_ref[core * part + i] = mine_ref[i]
        pack_ref[(1 - core) * part + i] = other_ref[i]
    groups = full_ref.shape[0] // LANES
    place = 0
    for i in range(groups):
        for j in range(i, groups):
            block = pack_ref[place]
            full_ref[i * LANES : (i + 1) * LANES, j * LANES : (j + 1) * LANES] = block
            if i != j:
                full_ref[j * LANES : (j + 1) * LANES, i * LANES : (i + 1) * LANES] = block.T
            place += 1
    projection = pack_ref[place : place + groups].reshape(groups * LANES, LANES)
    crossed = dot_f32(full_ref[...], projection, (1, 0))
    gram = dot_f32(projection, crossed, (0, 0))
    projected = dot_f32(y_ref[...].reshape(full_ref.shape[0], -1), projection, (0, 0))
    inverse = inverse_factor(gram)
    root = total_users ** 0.5
    basis_ref[...] = dot_f32(projected, inverse, (1, 1)) * root
    core_out_ref[...] = dot_f32(inverse, crossed, (1, 1)) * (1.0 / root)


def finish(core, mine, other, ytrans, total_users):
    rank_c, rank_i, users = ytrans.shape
    ranks = rank_c * rank_i
    vmem = pl.BlockSpec(memory_space=pltpu.VMEM)
    return pl.pallas_call(
        functools.partial(finish_kernel, total_users),
        out_shape=(
            jax.ShapeDtypeStruct((users, LANES), jnp.float32),
            jax.ShapeDtypeStruct((LANES, ranks), jnp.float32),
        ),
        in_specs=[pl.BlockSpec(memory_space=pltpu.SMEM), vmem, vmem, vmem],
        out_specs=(vmem, vmem),
        scratch_shapes=[
            pltpu.VMEM((2 * mine.shape[0], LANES, LANES), jnp.float32),
            pltpu.VMEM((ranks, ranks), jnp.float32),
        ],
        compiler_params=pltpu.CompilerParams(vmem_limit_bytes=28 * 2**20),
        name="finish",
    )(core, mine, other, ytrans)


def body(
    tile_owner, tile_slot, tile_cblock, tile_context, tile_weights,
    item_factors, context_factors, user_basis, user_counts,
):
    devices = lax.axis_size("users")
    chips = devices // 2
    rank_c = context_factors.shape[0]
    rank_i, block_len = item_factors.shape[1:]
    users = tile_weights.shape[2]
    core = (lax.axis_index("users") % 2).astype(jnp.int32).reshape(1)

    requests, where = route(tile_owner[:, 0], tile_slot, devices)
    asked = lax.all_to_all(requests, "users", split_axis=0, concat_axis=0, tiled=True)
    found = item_factors[asked]
    blocks = lax.all_to_all(found, "users", split_axis=0, concat_axis=0, tiled=True)

    table = context_factors.astype(jnp.float32).reshape(rank_c, -1, CB).transpose(1, 0, 2)
    contexts = context_values(tile_cblock, table, tile_context)
    ytrans, keep, send = tile_sums(where, user_counts, core, blocks, tile_weights, contexts, user_basis)

    pairs = [(i, i ^ 1) for i in range(devices)]
    groups = [[2 * chip + c for chip in range(chips)] for c in range(2)]
    part, wide = keep.shape[0] * keep.shape[1], keep.shape[2]
    halved = (keep + lax.ppermute(send, "users", pairs)).reshape(chips, part // chips, wide)
    pieces = lax.all_to_all(halved, "users", 0, 0, axis_index_groups=groups, tiled=True)
    piece = jnp.sum(pieces, axis=0, keepdims=True)
    spread = jnp.broadcast_to(piece, pieces.shape)
    mine = lax.all_to_all(spread, "users", 0, 0, axis_index_groups=groups, tiled=True)
    mine = mine.reshape(keep.shape)
    other = lax.ppermute(mine, "users", pairs)
    return finish(core, mine, other, ytrans, users * devices)


def solution(mesh):
    return jax.shard_map(
        body,
        mesh=mesh,
        in_specs=(
            P("users", None), P("users"), P("users"), P("users", None), P("users", None, None),
            P("users", None, None), P(), P("users", None), P("users"),
        ),
        out_specs=(P("users", None), P()),
        check_vma=False,
    )
```

```python
import functools

import jax
import jax.numpy as jnp
from jax import lax
from jax.experimental import pallas as pl
from jax.experimental.pallas import tpu as pltpu
from jax.sharding import PartitionSpec as P

CB = 8
SLOTS = 2
HIGH = lax.Precision.HIGHEST
LANES = 128
ROWS = 8
VMEM_LIMIT = 56 * 2**20


def dot_f32(lhs, rhs, contract):
    return lax.dot_general(
        lhs, rhs, ((contract[:1], contract[1:]), ((), ())),
        precision=HIGH, preferred_element_type=jnp.float32,
    )


def route_kernel(half, me_ref, owner_ref, slot_ref, request_ref, where_ref, used_ref):
    side = me_ref[0] // half
    lane = lax.broadcasted_iota(jnp.int32, (1, LANES), 1)

    def clear(place, _):
        used_ref[place] = 0
        return 0

    lax.fori_loop(0, 2 * half, clear, 0)
    request_ref[...] = jnp.zeros_like(request_ref)

    def assign(tile, _):
        owner = owner_ref[tile]
        taken = used_ref[owner]
        used_ref[owner] = taken + 1
        low = lax.rem(owner, half)
        mirrored = jnp.where(owner // half == side, 0, 1)
        place = mirrored * SLOTS + taken
        request_ref[low] = jnp.where(lane == place, slot_ref[tile], request_ref[low])
        where_ref[tile] = low * 2 * SLOTS + place
        return 0

    lax.fori_loop(0, owner_ref.shape[0], assign, 0)


def route(me, owners, slots, half):
    tiles = owners.shape[0]
    smem = pl.BlockSpec(memory_space=pltpu.SMEM)
    return pl.pallas_call(
        functools.partial(route_kernel, half),
        out_shape=(
            jax.ShapeDtypeStruct((half, 1, LANES), jnp.int32),
            jax.ShapeDtypeStruct((tiles,), jnp.int32),
        ),
        in_specs=[smem, smem, smem],
        out_specs=(pl.BlockSpec(memory_space=pltpu.VMEM), smem),
        scratch_shapes=[pltpu.SMEM((2 * half,), jnp.int32)],
        name="route",
    )(me, owners, slots)


def collect_kernel(asked_ref, own_ref, mirror_ref, out_ref):
    def one(peer, _):
        for place in range(2 * SLOTS):
            block = asked_ref[peer, 0, place]
            source = own_ref if place < SLOTS else mirror_ref
            out_ref[peer * 2 * SLOTS + place] = source[block]
        return 0

    lax.fori_loop(0, asked_ref.shape[0], one, 0)


def collect(asked, own, mirror):
    vmem = pl.BlockSpec(memory_space=pltpu.VMEM)
    peers = asked.shape[0]
    return pl.pallas_call(
        collect_kernel,
        out_shape=jax.ShapeDtypeStruct((peers * 2 * SLOTS,) + own.shape[1:], own.dtype),
        in_specs=[pl.BlockSpec(memory_space=pltpu.SMEM), vmem, vmem],
        out_specs=vmem,
        name="collect",
    )(asked, own, mirror)


def context_kernel(tiles, cblock_ref, table_ref, context_ref, out_ref):
    users = context_ref.shape[1]

    def one(tile, _):
        table = table_ref[cblock_ref[tile]]
        marks = jnp.broadcast_to(context_ref[pl.ds(tile, 1), :], (ROWS, users))
        total = jnp.zeros((ROWS, users), jnp.float32)
        for k in range(CB):
            column = jnp.broadcast_to(table[:, k : k + 1], (ROWS, users))
            total = jnp.where(marks == k, column, total)
        out_ref[tile] = total
        return 0

    lax.fori_loop(0, tiles, one, 0)


def context_values(cblock, table, context):
    tiles, users = context.shape
    vmem = pl.BlockSpec(memory_space=pltpu.VMEM)
    return pl.pallas_call(
        functools.partial(context_kernel, tiles),
        out_shape=jax.ShapeDtypeStruct((tiles, ROWS, users), jnp.float32),
        in_specs=[pl.BlockSpec(memory_space=pltpu.SMEM), vmem, vmem],
        out_specs=vmem,
        name="contexts",
    )(cblock, table, context)


def piece_places(devices):
    bits = devices.bit_length() - 1
    rest = [r << 3 for r in range(1 << (bits - 4))]
    places = {}
    for top in range(2):
        second, third = (1, 2) if top == 0 else (2, 1)
        for second_set in range(2):
            for core in range(2):
                places[core, top, second_set] = [
                    core + (top << (bits - 1)) + (second_set << second) + (third_set << third) + others
                    for third_set in range(2)
                    for others in rest
                ]
    return places


PIECES = [(core, top, second) for core in (1, 0) for second in (1, 0) for top in (0, 1)]


def tiles_kernel(
    step_tiles, places, where_ref, count_ref, me_ref,
    blocks_ref, weights_ref, context_ref, basis_ref, *rest,
):
    y_ref, piece_refs, product_ref, pack_ref = rest[0], rest[1:-2], rest[-2], rest[-1]
    step = pl.program_id(0)
    rank_i = blocks_ref.shape[1]
    users = weights_ref.shape[2]
    rank_c = context_ref.shape[1]
    chunk = piece_refs[0].shape[1]

    @pl.when(step == 0)
    def _():
        y_ref[...] = jnp.zeros_like(y_ref)

    for tile in range(step_tiles):
        block = blocks_ref[where_ref[step * step_tiles + tile]]
        product = jnp.dot(block, weights_ref[tile], preferred_element_type=jnp.float32)
        product_ref[tile] = product.astype(jnp.bfloat16).astype(jnp.float32)

    half = rank_i // 2
    for lane in range(users // LANES):
        lanes = slice(lane * LANES, (lane + 1) * LANES)
        for part in range(2):
            rows = slice(part * half, (part + 1) * half)
            total = y_ref[:, rows, lanes]
            for tile in range(step_tiles):
                values = context_ref[tile, :, lanes]
                total = total + values[:, None, :] * product_ref[tile, rows, lanes][None]
            y_ref[:, rows, lanes] = total

    @pl.when(step == pl.num_programs(0) - 1)
    def _():
        living = lax.broadcasted_iota(jnp.int32, (rank_i, users), 1) < count_ref[0]
        for r in range(rank_c):
            y_ref[r] = jnp.where(living, y_ref[r], 0.0)
        ytrans = y_ref[...].reshape(rank_c * rank_i, users)
        groups = ytrans.shape[0] // LANES
        place = 0
        for i in range(groups):
            upper = ytrans[i * LANES : (i + 1) * LANES]
            for j in range(i, groups):
                pack_ref[place * LANES : (place + 1) * LANES] = dot_f32(
                    upper, ytrans[j * LANES : (j + 1) * LANES], (1, 1)
                )
                place += 1
        for i in range(groups):
            pack_ref[place * LANES : (place + 1) * LANES] = dot_f32(
                ytrans[i * LANES : (i + 1) * LANES], basis_ref[...], (1, 0)
            )
            place += 1
        if place * LANES < pack_ref.shape[0]:
            pack_ref[place * LANES :] = jnp.zeros((pack_ref.shape[0] - place * LANES, LANES), jnp.float32)
        me = me_ref[0]
        for piece, ref in zip(PIECES, piece_refs):
            for i, position in enumerate(places[piece]):
                start = pl.multiple_of(jnp.bitwise_xor(me, position) * chunk, ROWS)
                ref[i] = pack_ref[pl.ds(start, chunk)]


def pack_rows(ranks, devices):
    groups = ranks // LANES
    rows = (groups * (groups + 1) // 2 + groups) * LANES
    return -(-rows // (devices * ROWS)) * ROWS


def tile_sums(where, count, me, blocks, weights, contexts, user_basis, devices):
    tiles, block_len, users = weights.shape
    rank_i = blocks.shape[1]
    rank_c = contexts.shape[1]
    step_tiles = 8
    chunk = pack_rows(rank_c * rank_i, devices)
    places = piece_places(devices)
    piece_shape = (devices // 8, chunk, LANES)
    whole = lambda *shape: pl.BlockSpec(shape, lambda s, *_: (0,) * len(shape))
    out = pl.pallas_call(
        functools.partial(tiles_kernel, step_tiles, places),
        out_shape=(jax.ShapeDtypeStruct((rank_c, rank_i, users), jnp.float32),)
        + (jax.ShapeDtypeStruct(piece_shape, jnp.float32),) * len(PIECES),
        grid_spec=pltpu.PrefetchScalarGridSpec(
            num_scalar_prefetch=3,
            grid=(tiles // step_tiles,),
            in_specs=[
                whole(*blocks.shape),
                pl.BlockSpec((step_tiles, block_len, users), lambda s, *_: (s, 0, 0)),
                pl.BlockSpec((step_tiles, rank_c, users), lambda s, *_: (s, 0, 0)),
                whole(*user_basis.shape),
            ],
            out_specs=(whole(rank_c, rank_i, users),) + (whole(*piece_shape),) * len(PIECES),
            scratch_shapes=[
                pltpu.VMEM((step_tiles, rank_i, users), jnp.float32),
                pltpu.VMEM((devices * chunk, LANES), jnp.float32),
            ],
        ),
        compiler_params=pltpu.CompilerParams(vmem_limit_bytes=VMEM_LIMIT),
        cost_estimate=pl.CostEstimate(flops=2 * 10**9, bytes_accessed=12 * 10**6, transcendentals=0),
        name="tile_sums",
    )(where, count, me, blocks, weights, contexts, user_basis)
    return out[0], dict(zip(PIECES, out[1:]))


def inverse_factor(gram):
    order = gram.shape[0]
    panels = order // ROWS
    sub = lax.broadcasted_iota(jnp.int32, (ROWS, order), 0)
    lane = lax.broadcasted_iota(jnp.int32, (ROWS, order), 1)
    left = [gram[ROWS * i : ROWS * (i + 1)] for i in range(panels)]
    right = [jnp.where(lane == sub + ROWS * i, 1.0, 0.0) for i in range(panels)]
    for k in range(panels):
        columns = {
            i: [
                jnp.broadcast_to(left[i][:, ROWS * k + j : ROWS * k + j + 1], (ROWS, order))
                for j in range(ROWS)
            ]
            for i in range(k, panels)
        }
        row, tail = left[k], right[k]
        scale = jnp.zeros((ROWS, order), jnp.float32)
        rows, tails = [], []
        for j in range(ROWS):
            head = columns[k][j]
            pivot = jnp.broadcast_to(head[j : j + 1], (ROWS, order))
            inverse = pl.reciprocal(pivot, approx=True)
            inverse = inverse * (2.0 - pivot * inverse)
            scale = jnp.where(sub == j, pivot, scale)
            rows.append(jnp.broadcast_to(row[j : j + 1], (ROWS, order)))
            tails.append(jnp.broadcast_to(tail[j : j + 1], (ROWS, order)))
            below = jnp.where(sub > j, head, 0.0) * inverse
            row = row - below * rows[j]
            tail = tail - below * tails[j]
            facts = {k: below}
            for i in range(k + 1, panels):
                facts[i] = columns[i][j] * inverse
            for c in range(j + 1, ROWS):
                crossing = jnp.broadcast_to(head[c : c + 1], (ROWS, order))
                for i in range(k, panels):
                    columns[i][c] = columns[i][c] - facts[i] * crossing
            for i in range(k + 1, panels):
                left[i] = left[i] - facts[i] * rows[j]
                right[i] = right[i] - facts[i] * tails[j]
        right[k] = tail * lax.rsqrt(scale)
    return jnp.concatenate(right, axis=0)


def finish_kernel(total_users, places, me_ref, y_ref, *rest):
    piece_refs, (basis_ref, core_out_ref, pack_ref, full_ref) = rest[: len(PIECES)], rest[len(PIECES) :]
    me = me_ref[0]
    chunk = piece_refs[0].shape[1]
    for piece, ref in zip(PIECES, piece_refs):
        for i, position in enumerate(places[piece]):
            start = pl.multiple_of(jnp.bitwise_xor(me, position) * chunk, ROWS)
            pack_ref[pl.ds(start, chunk)] = ref[i]
    groups = full_ref.shape[0] // LANES
    place = 0
    for i in range(groups):
        for j in range(i, groups):
            block = pack_ref[place * LANES : (place + 1) * LANES]
            full_ref[i * LANES : (i + 1) * LANES, j * LANES : (j + 1) * LANES] = block
            if i != j:
                full_ref[j * LANES : (j + 1) * LANES, i * LANES : (i + 1) * LANES] = block.T
            place += 1
    projection = pack_ref[place * LANES : (place + groups) * LANES]
    crossed = dot_f32(full_ref[...], projection, (1, 0))
    gram = dot_f32(projection, crossed, (0, 0))
    projected = dot_f32(y_ref[...].reshape(full_ref.shape[0], -1), projection, (0, 0))
    inverse = inverse_factor(gram)
    root = total_users ** 0.5
    basis_ref[...] = dot_f32(projected, inverse, (1, 1)) * root
    core_out_ref[...] = dot_f32(inverse, crossed, (1, 1)) * (1.0 / root)


def finish(me, ytrans, pieces, devices):
    rank_c, rank_i, users = ytrans.shape
    ranks = rank_c * rank_i
    chunk = pack_rows(ranks, devices)
    vmem = pl.BlockSpec(memory_space=pltpu.VMEM)
    return pl.pallas_call(
        functools.partial(finish_kernel, users * devices, piece_places(devices)),
        out_shape=(
            jax.ShapeDtypeStruct((users, LANES), jnp.float32),
            jax.ShapeDtypeStruct((LANES, ranks), jnp.float32),
        ),
        in_specs=[pl.BlockSpec(memory_space=pltpu.SMEM)] + [vmem] * (1 + len(PIECES)),
        out_specs=(vmem, vmem),
        scratch_shapes=[
            pltpu.VMEM((devices * chunk, LANES), jnp.float32),
            pltpu.VMEM((ranks, ranks), jnp.float32),
        ],
        compiler_params=pltpu.CompilerParams(vmem_limit_bytes=28 * 2**20),
        name="finish",
    )(me, ytrans, *[pieces[piece] for piece in PIECES])


def swap(value, bit, devices):
    return lax.ppermute(value, "users", [(i, i ^ (1 << bit)) for i in range(devices)])


def reduce_pieces(pieces, devices):
    top_bit = devices.bit_length() - 2
    got = {}
    for second in (1, 0):
        for top in (0, 1):
            got[top, second] = swap(pieces[1, top, second], 0, devices)
    half = devices // 16
    sums = []
    for top in (0, 1):
        away = swap(pieces[0, top, 1] + got[top, 1], 1 + top, devices)
        sums.append((pieces[0, top, 0], got[top, 0], away))
    lone = []
    for top in (0, 1):
        kept, near, away = sums[top]
        further = swap(kept[half:] + near[half:] + away[half:], 2 - top, devices)
        lone.append(kept[:half] + near[:half] + away[:half] + further)
    for bit in range(top_bit - 1, 2, -1):
        half = lone[0].shape[0] // 2
        lone = [value[:half] + swap(value[half:], bit, devices) for value in lone]
    return lone[0] + swap(lone[1], top_bit, devices)


def spread_pieces(total, devices):
    top_bit = devices.bit_length() - 2
    lone = [total, swap(total, top_bit, devices)]
    for bit in range(3, top_bit):
        lone = [jnp.concatenate([value, swap(value, bit, devices)], axis=0) for value in lone]
    pieces = {}
    for top in (0, 1):
        near = jnp.concatenate([lone[top], swap(lone[top], 2 - top, devices)], axis=0)
        pieces[0, top, 0] = near
        pieces[0, top, 1] = swap(near, 1 + top, devices)
    for second in (0, 1):
        for top in (0, 1):
            pieces[1, top, second] = swap(pieces[0, top, second], 0, devices)
    return pieces


def body(
    tile_owner, tile_slot, tile_cblock, tile_context, tile_weights,
    item_factors, context_factors, user_basis, user_counts,
):
    devices = lax.axis_size("users")
    half = devices // 2
    rank_c = context_factors.shape[0]
    me = lax.axis_index("users").astype(jnp.int32).reshape(1)

    mirror = swap(item_factors, devices.bit_length() - 2, devices)
    requests, where = route(me, tile_owner[:, 0], tile_slot, half)
    sides = [list(range(half)), list(range(half, devices))]
    asked = lax.all_to_all(requests, "users", 0, 0, axis_index_groups=sides, tiled=True)
    found = collect(asked, item_factors, mirror)
    blocks = lax.all_to_all(found, "users", 0, 0, axis_index_groups=sides, tiled=True)

    table = context_factors.astype(jnp.float32).reshape(rank_c, -1, CB).transpose(1, 0, 2)
    contexts = context_values(tile_cblock, table, tile_context)
    ytrans, pieces = tile_sums(
        where, user_counts, me, blocks, tile_weights, contexts, user_basis, devices
    )
    pieces = spread_pieces(reduce_pieces(pieces, devices), devices)
    return finish(me, ytrans, pieces, devices)


def solution(mesh):
    return jax.shard_map(
        body,
        mesh=mesh,
        in_specs=(
            P("users", None), P("users"), P("users"), P("users", None), P("users", None, None),
            P("users", None, None), P(), P("users", None), P("users"),
        ),
        out_specs=(P("users", None), P()),
        check_vma=False,
    )
```

```python
import functools

import jax
import jax.numpy as jnp
from jax import lax
from jax.experimental import pallas as pl
from jax.experimental.pallas import tpu as pltpu
from jax.sharding import PartitionSpec as P

CB = 8
SLOTS = 2
PLACES = 2 * SLOTS
HIGH = lax.Precision.HIGHEST
LANES = 128
ROWS = 8
MASKS = 4
BATCH = 8
MIB = 2**20

SMEM = pl.BlockSpec(memory_space=pltpu.SMEM)
VMEM = pl.BlockSpec(memory_space=pltpu.VMEM)


def limit(mib):
    return pltpu.CompilerParams(vmem_limit_bytes=mib * MIB)


def dot(lhs, rhs):
    return jnp.dot(lhs, rhs, preferred_element_type=jnp.float32)


def dot_nt(lhs, rhs):
    return lax.dot_general(lhs, rhs, (((1,), (1,)), ((), ())), preferred_element_type=jnp.float32)


def split(value):
    high = value.astype(jnp.bfloat16)
    return high, (value - high.astype(jnp.float32)).astype(jnp.bfloat16)


def route_kernel(half, me_ref, owner_ref, slot_ref, request_ref, tile_ref, used_ref):
    side = me_ref[0] // half
    low_me = lax.rem(me_ref[0], half)
    lane = lax.broadcasted_iota(jnp.int32, (1, LANES), 1)

    def clear(place, _):
        used_ref[place] = 0
        tile_ref[SLOTS * place] = -1
        tile_ref[SLOTS * place + 1] = -1
        return 0

    lax.fori_loop(0, 2 * half, clear, 0)
    request_ref[...] = jnp.zeros_like(request_ref)

    def assign(tile, _):
        owner = owner_ref[tile]
        taken = used_ref[owner]
        used_ref[owner] = taken + 1
        low = lax.rem(owner, half)
        place = jnp.where(owner // half == side, 0, SLOTS) + taken
        request_ref[low] = jnp.where(lane == place, slot_ref[tile], request_ref[low])
        tile_ref[jnp.bitwise_xor(low, low_me) * PLACES + place] = tile
        return 0

    lax.fori_loop(0, owner_ref.shape[0], assign, 0)


def route(me, owners, slots, half):
    return pl.pallas_call(
        functools.partial(route_kernel, half),
        out_shape=(
            jax.ShapeDtypeStruct((half, 1, LANES), jnp.int32),
            jax.ShapeDtypeStruct((half * PLACES,), jnp.int32),
        ),
        in_specs=[SMEM, SMEM, SMEM],
        out_specs=(VMEM, SMEM),
        scratch_shapes=[pltpu.SMEM((2 * half,), jnp.int32)],
        compiler_params=limit(2),
        name="route",
    )(me, owners, slots)


def collect_kernel(me_ref, asked_ref, own_ref, mirror_ref, *out_refs):
    low_me = lax.rem(me_ref[0], len(out_refs))
    for mask, out_ref in enumerate(out_refs):
        peer = jnp.bitwise_xor(low_me, mask)
        for place in range(PLACES):
            source = own_ref if place < SLOTS else mirror_ref
            out_ref[place] = source[asked_ref[peer, 0, place]]


def collect(me, asked, own, mirror):
    half = asked.shape[0]
    return pl.pallas_call(
        collect_kernel,
        out_shape=(jax.ShapeDtypeStruct((PLACES,) + own.shape[1:], own.dtype),) * half,
        in_specs=[SMEM, SMEM, VMEM, VMEM],
        out_specs=(VMEM,) * half,
        compiler_params=limit(8),
        name="collect",
    )(me, asked, own, mirror)


def piece_places(devices):
    return {
        (core, plane): [core + 2 * plane + 8 * rest for rest in range(devices // 8)]
        for core in range(2)
        for plane in range(4)
    }


PIECES = [(core, plane) for core in (1, 0) for plane in (3, 1, 2, 0)]


def pack_rows(ranks, devices):
    groups = ranks // LANES
    rows = (groups * (groups + 1) // 2 + groups) * LANES
    return -(-rows // (devices * ROWS)) * ROWS


def tiles_kernel(group, last, places, *refs):
    tile_ref, cblock_ref, count_ref, me_ref = refs[:4]
    block_refs = refs[4 : 4 + MASKS]
    weights_ref, marks_ref, factors_ref = refs[4 + MASKS : 7 + MASKS]
    refs = refs[7 + MASKS :]
    before_ref = basis_ref = None
    if group:
        before_ref, refs = refs[0], refs[1:]
    if last:
        basis_ref, refs = refs[0], refs[1:]
        piece_refs, refs = refs[: len(PIECES)], refs[len(PIECES) :]
        high_ref, low_ref, refs = refs[0], refs[1], refs[2:]
        y_ref, pack_ref, refs = refs[0], refs[1], refs[2:]
    else:
        y_ref, refs = refs[0], refs[1:]
    held_ref, sem_ref, product_ref, context_ref = refs
    rank_c, rank_i, users = y_ref.shape
    slots = MASKS * PLACES

    tiles = [tile_ref[group * slots + slot] for slot in range(slots)]
    copies = []
    for slot in range(slots):
        copy = pltpu.make_async_copy(
            weights_ref.at[jnp.maximum(tiles[slot], 0)], held_ref.at[slot], sem_ref.at[slot]
        )
        copy.start()
        copies.append(copy)

    for first in range(0, slots, BATCH):
        for place in range(BATCH):
            tile = jnp.maximum(tiles[first + place], 0)
            used = tiles[first + place] >= 0
            cblock = cblock_ref[tile]
            per = LANES // CB
            start = pl.multiple_of(cblock // per * LANES, LANES)
            table = factors_ref[:, pl.ds(start, LANES)].astype(jnp.float32)
            table = jnp.where(used, table, 0.0)
            marks = marks_ref[pl.ds(tile, 1), :] + lax.rem(cblock, per) * CB
            for lane in range(users // LANES):
                index = jnp.broadcast_to(marks[:, lane * LANES : (lane + 1) * LANES], (rank_c, LANES))
                context_ref[place, :, lane * LANES : (lane + 1) * LANES] = jnp.take_along_axis(
                    table, index, axis=1, mode="promise_in_bounds"
                )
        for place in range(BATCH):
            slot = first + place
            copies[slot].wait()
            product = dot(block_refs[slot // PLACES][slot % PLACES], held_ref[slot])
            product_ref[place] = product.astype(jnp.bfloat16).astype(jnp.float32)
        half = rank_i // 2
        for lane in range(users // LANES):
            lanes = slice(lane * LANES, (lane + 1) * LANES)
            for part in range(2):
                rows = slice(part * half, (part + 1) * half)
                if first:
                    total = y_ref[:, rows, lanes]
                elif group:
                    total = before_ref[:, rows, lanes]
                else:
                    total = jnp.zeros((rank_c, half, LANES), jnp.float32)
                for place in range(BATCH):
                    values = context_ref[place, :, lanes]
                    total = total + values[:, None, :] * product_ref[place, rows, lanes][None]
                y_ref[:, rows, lanes] = total

    if not last:
        return
    living = lax.broadcasted_iota(jnp.int32, (rank_i, users), 1) < count_ref[0]
    for r in range(rank_c):
        high, low = split(jnp.where(living, y_ref[r], 0.0))
        high_ref[r * rank_i : (r + 1) * rank_i] = high
        low_ref[r * rank_i : (r + 1) * rank_i] = low
    ranks = rank_c * rank_i
    groups = ranks // LANES
    place = 0
    for i in range(groups):
        rows = slice(i * LANES, (i + 1) * LANES)
        strip = dot_nt(high_ref[rows], high_ref[i * LANES :])
        strip = strip + dot_nt(high_ref[rows], low_ref[i * LANES :])
        strip = strip + dot_nt(low_ref[rows], high_ref[i * LANES :])
        for j in range(groups - i):
            pack_ref[place * LANES : (place + 1) * LANES] = strip[:, j * LANES : (j + 1) * LANES]
            place += 1
    basis_high, basis_low = split(basis_ref[...])
    projection = dot(high_ref[...], basis_high) + dot(high_ref[...], basis_low) + dot(low_ref[...], basis_high)
    pack_ref[place * LANES : (place + groups) * LANES] = projection
    place += groups
    if place * LANES < pack_ref.shape[0]:
        pack_ref[place * LANES :] = jnp.zeros((pack_ref.shape[0] - place * LANES, LANES), jnp.float32)
    me = me_ref[0]
    chunk = piece_refs[0].shape[1]
    for piece, ref in zip(PIECES, piece_refs):
        for i, position in enumerate(places[piece]):
            start = pl.multiple_of(jnp.bitwise_xor(me, position) * chunk, ROWS)
            ref[i] = pack_ref[pl.ds(start, chunk)]


def tile_sums(tile_of, cblock, count, me, blocks, weights, marks, factors, user_basis, devices):
    block_len, users = weights.shape[1:]
    rank_i = blocks[0].shape[1]
    rank_c = factors.shape[0]
    ranks = rank_c * rank_i
    slots = MASKS * PLACES
    chunk = pack_rows(ranks, devices)
    calls = len(blocks) // MASKS
    y_shape = (rank_c, rank_i, users)
    y_type = jax.ShapeDtypeStruct(y_shape, jnp.float32)
    y = None
    for group in range(calls):
        last = group == calls - 1
        operands = [tile_of, cblock, count, me, *blocks[group * MASKS : (group + 1) * MASKS], weights, marks, factors]
        in_specs = [SMEM] * 4 + [VMEM] * MASKS + [pl.BlockSpec(memory_space=pltpu.HBM), VMEM, VMEM]
        aliases = {}
        if group:
            if not last:
                aliases = {len(operands): 0}
            operands.append(y)
            in_specs.append(VMEM)
        scratch = [
            pltpu.VMEM((slots, block_len, users), jnp.bfloat16),
            pltpu.SemaphoreType.DMA((slots,)),
            pltpu.VMEM((BATCH, rank_i, users), jnp.float32),
            pltpu.VMEM((BATCH, rank_c, users), jnp.float32),
        ]
        if last:
            operands.append(user_basis)
            in_specs.append(VMEM)
            out_shape = (jax.ShapeDtypeStruct((devices // 8, chunk, LANES), jnp.float32),) * len(PIECES)
            out_shape += (jax.ShapeDtypeStruct((ranks, users), jnp.bfloat16),) * 2
            out_specs = (VMEM,) * len(out_shape)
            scratch = [pltpu.VMEM(y_shape, jnp.float32), pltpu.VMEM((devices * chunk, LANES), jnp.float32)] + scratch
        else:
            out_shape, out_specs = y_type, VMEM
        y = pl.pallas_call(
            functools.partial(tiles_kernel, group, last, piece_places(devices)),
            out_shape=out_shape,
            in_specs=in_specs,
            out_specs=out_specs,
            input_output_aliases=aliases,
            scratch_shapes=scratch,
            compiler_params=limit(16),
            cost_estimate=pl.CostEstimate(flops=5 * 10**8, bytes_accessed=4 * 10**6, transcendentals=0),
            name="tile_sums",
        )(*operands)
    return dict(zip(PIECES, y[:-2])), y[-2], y[-1]


def inverse_factor(gram):
    order = gram.shape[0]
    panels = order // ROWS
    sub = lax.broadcasted_iota(jnp.int32, (ROWS, order), 0)
    lane = lax.broadcasted_iota(jnp.int32, (ROWS, order), 1)
    left = [gram[ROWS * i : ROWS * (i + 1)] for i in range(panels)]
    right = [jnp.where(lane == sub + ROWS * i, 1.0, 0.0) for i in range(panels)]
    for k in range(panels):
        columns = {
            i: [
                jnp.broadcast_to(left[i][:, ROWS * k + j : ROWS * k + j + 1], (ROWS, order))
                for j in range(ROWS)
            ]
            for i in range(k, panels)
        }
        row, tail = left[k], right[k]
        scale = jnp.zeros((ROWS, order), jnp.float32)
        rows, tails = [], []
        for j in range(ROWS):
            head = columns[k][j]
            pivot = jnp.broadcast_to(head[j : j + 1], (ROWS, order))
            inverse = pl.reciprocal(pivot, approx=True)
            inverse = inverse * (2.0 - pivot * inverse)
            scale = jnp.where(sub == j, pivot, scale)
            rows.append(jnp.broadcast_to(row[j : j + 1], (ROWS, order)))
            tails.append(jnp.broadcast_to(tail[j : j + 1], (ROWS, order)))
            below = jnp.where(sub > j, head, 0.0) * inverse
            row = row - below * rows[j]
            tail = tail - below * tails[j]
            facts = {k: below}
            for i in range(k + 1, panels):
                facts[i] = columns[i][j] * inverse
            for c in range(j + 1, ROWS):
                crossing = jnp.broadcast_to(head[c : c + 1], (ROWS, order))
                for i in range(k, panels):
                    columns[i][c] = columns[i][c] - facts[i] * crossing
            for i in range(k + 1, panels):
                left[i] = left[i] - facts[i] * rows[j]
                right[i] = right[i] - facts[i] * tails[j]
        right[k] = tail * lax.rsqrt(scale)
    return jnp.concatenate(right, axis=0)


def finish_kernel(total_users, places, me_ref, high_ref, low_ref, *rest):
    piece_refs, (basis_ref, core_out_ref, pack_ref, full_ref) = rest[: len(PIECES)], rest[len(PIECES) :]
    me = me_ref[0]
    chunk = piece_refs[0].shape[1]
    for piece, ref in zip(PIECES, piece_refs):
        for i, position in enumerate(places[piece]):
            start = pl.multiple_of(jnp.bitwise_xor(me, position) * chunk, ROWS)
            pack_ref[pl.ds(start, chunk)] = ref[i]
    groups = full_ref.shape[0] // LANES
    place = 0
    for i in range(groups):
        for j in range(i, groups):
            block = pack_ref[place * LANES : (place + 1) * LANES]
            full_ref[i * LANES : (i + 1) * LANES, j * LANES : (j + 1) * LANES] = block
            if i != j:
                full_ref[j * LANES : (j + 1) * LANES, i * LANES : (i + 1) * LANES] = block.T
            place += 1
    projection = pack_ref[place * LANES : (place + groups) * LANES]
    turned = jnp.concatenate(
        [projection[i * LANES : (i + 1) * LANES].T for i in range(groups)], axis=1
    )
    turned_high, turned_low = split(turned)
    full_high, full_low = split(full_ref[...])
    crossed = dot(turned_high, full_high) + dot(turned_high, full_low) + dot(turned_low, full_high)
    gram = jnp.dot(crossed, projection, precision=HIGH, preferred_element_type=jnp.float32)
    projected = (
        dot(turned_high, high_ref[...]) + dot(turned_high, low_ref[...]) + dot(turned_low, high_ref[...])
    )
    inverse = inverse_factor(gram)
    root = total_users ** 0.5
    scaled = jnp.dot(inverse * root, projected, precision=HIGH, preferred_element_type=jnp.float32)
    for i in range(scaled.shape[1] // LANES):
        basis_ref[i * LANES : (i + 1) * LANES] = scaled[:, i * LANES : (i + 1) * LANES].T
    core_out_ref[...] = jnp.dot(
        inverse * (1.0 / root), crossed, precision=HIGH, preferred_element_type=jnp.float32
    )


def finish(me, high, low, pieces, devices):
    ranks, users = high.shape
    chunk = pack_rows(ranks, devices)
    return pl.pallas_call(
        functools.partial(finish_kernel, users * devices, piece_places(devices)),
        out_shape=(
            jax.ShapeDtypeStruct((users, LANES), jnp.float32),
            jax.ShapeDtypeStruct((LANES, ranks), jnp.float32),
        ),
        in_specs=[SMEM] + [VMEM] * (2 + len(PIECES)),
        out_specs=(VMEM, VMEM),
        scratch_shapes=[
            pltpu.VMEM((devices * chunk, LANES), jnp.float32),
            pltpu.VMEM((ranks, ranks), jnp.float32),
        ],
        compiler_params=limit(16),
        name="finish",
    )(me, high, low, *[pieces[piece] for piece in PIECES])


def swap(value, mask, devices):
    return lax.ppermute(value, "users", [(i, i ^ mask) for i in range(devices)])


def reduce_pieces(pieces, devices):
    got = {plane: swap(pieces[1, plane], 1, devices) for plane in (3, 1, 2, 0)}
    away = [swap(pieces[0, plane] + got[plane], 2 * plane, devices) for plane in (3, 1, 2)]
    rest = devices // 8
    total = None
    far = []
    for position in list(range(rest - 1, -1, -1)):
        rows = slice(position, position + 1)
        value = pieces[0, 0][rows] + got[0][rows] + away[0][rows] + away[1][rows] + away[2][rows]
        if position:
            far.append(swap(value, 8 * position, devices))
        else:
            total = value
    for value in far:
        total = total + value
    return total


def spread_pieces(total, devices):
    near = [total] + [swap(total, 8 * position, devices) for position in range(1, devices // 8)]
    near = jnp.concatenate(near, axis=0)
    pieces = {(0, 0): near}
    for plane in (3, 1, 2):
        pieces[0, plane] = swap(near, 2 * plane, devices)
    for plane in (0, 3, 1, 2):
        pieces[1, plane] = swap(pieces[0, plane], 1, devices)
    return pieces


def body(
    tile_owner, tile_slot, tile_cblock, tile_context, tile_weights,
    item_factors, context_factors, user_basis, user_counts,
):
    devices = lax.axis_size("users")
    half = devices // 2
    me = lax.axis_index("users").astype(jnp.int32).reshape(1)

    mirror = swap(item_factors, half, devices)
    requests, tile_of = route(me, tile_owner[:, 0], tile_slot, half)
    sides = [list(range(half)), list(range(half, devices))]
    asked = lax.all_to_all(requests, "users", 0, 0, axis_index_groups=sides, tiled=True)
    found = collect(me, asked, item_factors, mirror)
    blocks = [found[0]] + [swap(found[mask], mask, devices) for mask in range(1, half)]
    pieces, high, low = tile_sums(
        tile_of, tile_cblock, user_counts, me, blocks, tile_weights, tile_context,
        context_factors, user_basis, devices,
    )
    pieces = spread_pieces(reduce_pieces(pieces, devices), devices)
    return finish(me, high, low, pieces, devices)


def solution(mesh):
    return jax.shard_map(
        body,
        mesh=mesh,
        in_specs=(
            P("users", None), P("users"), P("users"), P("users", None), P("users", None, None),
            P("users", None, None), P(), P("users", None), P("users"),
        ),
        out_specs=(P("users", None), P()),
        check_vma=False,
    )
```

```python
import functools

import jax
import jax.numpy as jnp
from jax import lax
from jax.experimental import pallas as pl
from jax.experimental.pallas import tpu as pltpu
from jax.sharding import PartitionSpec as P

CB = 8
SLOTS = 2
PLACES = 2 * SLOTS
HIGH = lax.Precision.HIGHEST
LANES = 128
ROWS = 8
BATCH = 8
MIB = 2**20

SMEM = pl.BlockSpec(memory_space=pltpu.SMEM)
VMEM = pl.BlockSpec(memory_space=pltpu.VMEM)
ANY = pl.BlockSpec(memory_space=pl.ANY)


def in_hbm(value):
    return pltpu.with_memory_space_constraint(value, pltpu.HBM)


def limit(mib):
    return pltpu.CompilerParams(vmem_limit_bytes=mib * MIB)


def dot(lhs, rhs):
    return jnp.dot(lhs, rhs, preferred_element_type=jnp.float32)


def dot_nt(lhs, rhs):
    return lax.dot_general(lhs, rhs, (((1,), (1,)), ((), ())), preferred_element_type=jnp.float32)


def split(value):
    high = value.astype(jnp.bfloat16)
    return high, (value - high.astype(jnp.float32)).astype(jnp.bfloat16)


def route_kernel(half, me_ref, owner_ref, slot_ref, own_ref, request_ref, where_ref, held_ref, used_ref, sem_ref):
    copy = pltpu.make_async_copy(own_ref, held_ref, sem_ref)
    copy.start()
    side = me_ref[0] // half
    lane = lax.broadcasted_iota(jnp.int32, (1, LANES), 1)

    def clear(place, _):
        used_ref[place] = 0
        return 0

    lax.fori_loop(0, 2 * half, clear, 0, unroll=8)
    request_ref[...] = jnp.zeros_like(request_ref)

    def assign(tile, _):
        owner = owner_ref[tile]
        taken = used_ref[owner]
        used_ref[owner] = taken + 1
        low = lax.rem(owner, half)
        place = jnp.where(owner // half == side, 0, SLOTS) + taken
        request_ref[low] = jnp.where(lane == place, slot_ref[tile], request_ref[low])
        where_ref[tile] = low * PLACES + place
        return 0

    lax.fori_loop(0, owner_ref.shape[0], assign, 0, unroll=4)
    copy.wait()


def route(me, owners, slots, own, half):
    return pl.pallas_call(
        functools.partial(route_kernel, half),
        out_shape=(
            jax.ShapeDtypeStruct((half, 1, LANES), jnp.int32),
            jax.ShapeDtypeStruct(owners.shape, jnp.int32),
            jax.ShapeDtypeStruct(own.shape, own.dtype),
        ),
        in_specs=[SMEM, SMEM, SMEM, ANY],
        out_specs=(VMEM, SMEM, VMEM),
        scratch_shapes=[pltpu.SMEM((2 * half,), jnp.int32), pltpu.SemaphoreType.DMA],
        compiler_params=limit(4),
        name="route",
    )(me, in_hbm(owners), in_hbm(slots), in_hbm(own))


def collect_kernel(asked_ref, own_ref, mirror_ref, out_ref):
    def one(peer, _):
        for place in range(PLACES):
            source = own_ref if place < SLOTS else mirror_ref
            out_ref[peer * PLACES + place] = source[asked_ref[peer, 0, place]]
        return 0

    lax.fori_loop(0, asked_ref.shape[0], one, 0, unroll=4)


def collect(asked, own, mirror):
    return pl.pallas_call(
        collect_kernel,
        out_shape=jax.ShapeDtypeStruct((asked.shape[0] * PLACES,) + own.shape[1:], own.dtype),
        in_specs=[SMEM, VMEM, VMEM],
        out_specs=VMEM,
        compiler_params=limit(4),
        name="collect",
    )(asked, own, mirror)


def stage_kernel(cblock_ref, table_ref, marks_ref, weights_ref, context_ref, held_ref, sem_ref):
    copy = pltpu.make_async_copy(weights_ref, held_ref, sem_ref)
    copy.start()
    tiles, users = marks_ref.shape

    def one(tile, _):
        table = table_ref[cblock_ref[tile]]
        marks = jnp.broadcast_to(marks_ref[pl.ds(tile, 1), :], (ROWS, users))
        total = jnp.zeros((ROWS, users), jnp.float32)
        for k in range(CB):
            column = jnp.broadcast_to(table[:, k : k + 1], (ROWS, users))
            total = jnp.where(marks == k, column, total)
        context_ref[tile] = total
        return 0

    lax.fori_loop(0, tiles, one, 0, unroll=2)
    copy.wait()


def stage(cblock, table, marks, weights):
    tiles, users = marks.shape
    return pl.pallas_call(
        stage_kernel,
        out_shape=(
            jax.ShapeDtypeStruct((tiles, ROWS, users), jnp.float32),
            jax.ShapeDtypeStruct(weights.shape, weights.dtype),
        ),
        in_specs=[SMEM, VMEM, VMEM, ANY],
        out_specs=(VMEM, VMEM),
        scratch_shapes=[pltpu.SemaphoreType.DMA],
        compiler_params=limit(4),
        cost_estimate=pl.CostEstimate(flops=10**7, bytes_accessed=2 * 10**7, transcendentals=0),
        name="stage",
    )(in_hbm(cblock), table, marks, in_hbm(weights))


def piece_places(devices):
    return {
        (core, plane): [core + 2 * plane + 8 * rest for rest in range(devices // 8)]
        for core in range(2)
        for plane in range(4)
    }


PIECES = [(core, plane) for core in (1, 0) for plane in (3, 1, 2, 0)]


def pack_rows(ranks, devices):
    groups = ranks // LANES
    rows = (groups * (groups + 1) // 2 + groups) * LANES
    return -(-rows // (devices * ROWS)) * ROWS


def tiles_kernel(places, where_ref, count_ref, me_ref, blocks_ref, weights_ref, context_ref, basis_ref, *refs):
    piece_refs, refs = refs[: len(PIECES)], refs[len(PIECES) :]
    high_ref, low_ref, y_ref, pack_ref, product_ref = refs
    rank_c, rank_i, users = y_ref.shape
    tiles = weights_ref.shape[0]
    batches = tiles // BATCH
    half = rank_i * users // LANES // BATCH

    def multiply(tile, bank, place):
        product = dot(blocks_ref[where_ref[tile]], weights_ref[tile])
        product_ref[bank, place] = product.astype(jnp.bfloat16).astype(jnp.float32)

    def first(place, _):
        multiply(place, 0, place)
        return 0

    lax.fori_loop(0, BATCH, first, 0)
    y_ref[...] = jnp.zeros_like(y_ref)

    def step(index, _):
        batch, part = index // BATCH, lax.rem(index, BATCH)
        bank = lax.rem(batch, 2)
        multiply(jnp.minimum(index + BATCH, tiles - 1), 1 - bank, part)
        lanes = pl.ds(pl.multiple_of(part // (rank_i // half) * LANES, LANES), LANES)
        rows = pl.ds(pl.multiple_of(lax.rem(part, rank_i // half) * half, ROWS), half)
        total = y_ref[:, rows, lanes]
        for place in range(BATCH):
            values = context_ref[batch * BATCH + place, :, lanes]
            total = total + values[:, None, :] * product_ref[bank, place, rows, lanes][None]
        y_ref[:, rows, lanes] = total
        return 0

    lax.fori_loop(0, batches * BATCH, step, 0)

    living = lax.broadcasted_iota(jnp.int32, (rank_i, users), 1) < count_ref[0]
    for r in range(rank_c):
        high, low = split(jnp.where(living, y_ref[r], 0.0))
        high_ref[r * rank_i : (r + 1) * rank_i] = high
        low_ref[r * rank_i : (r + 1) * rank_i] = low
    ranks = rank_c * rank_i
    groups = ranks // LANES
    place = 0
    for i in range(groups):
        rows = slice(i * LANES, (i + 1) * LANES)
        strip = dot_nt(high_ref[rows], high_ref[i * LANES :])
        strip = strip + dot_nt(high_ref[rows], low_ref[i * LANES :])
        strip = strip + dot_nt(low_ref[rows], high_ref[i * LANES :])
        for j in range(groups - i):
            pack_ref[place * LANES : (place + 1) * LANES] = strip[:, j * LANES : (j + 1) * LANES]
            place += 1
    basis_high, basis_low = split(basis_ref[...])
    projection = dot(high_ref[...], basis_high) + dot(high_ref[...], basis_low) + dot(low_ref[...], basis_high)
    pack_ref[place * LANES : (place + groups) * LANES] = projection
    place += groups
    if place * LANES < pack_ref.shape[0]:
        pack_ref[place * LANES :] = jnp.zeros((pack_ref.shape[0] - place * LANES, LANES), jnp.float32)
    me = me_ref[0]
    chunk = piece_refs[0].shape[1]
    for piece, ref in zip(PIECES, piece_refs):
        for i, position in enumerate(places[piece]):
            start = pl.multiple_of(jnp.bitwise_xor(me, position) * chunk, ROWS)
            ref[i] = pack_ref[pl.ds(start, chunk)]


def tile_sums(where, count, me, blocks, weights, contexts, user_basis, devices):
    users = weights.shape[2]
    rank_i = blocks.shape[1]
    rank_c = contexts.shape[1]
    ranks = rank_c * rank_i
    chunk = pack_rows(ranks, devices)
    out_shape = (jax.ShapeDtypeStruct((devices // 8, chunk, LANES), jnp.float32),) * len(PIECES)
    out_shape += (jax.ShapeDtypeStruct((ranks, users), jnp.bfloat16),) * 2
    out = pl.pallas_call(
        functools.partial(tiles_kernel, piece_places(devices)),
        out_shape=out_shape,
        in_specs=[SMEM] * 3 + [VMEM] * 4,
        out_specs=(VMEM,) * len(out_shape),
        scratch_shapes=[
            pltpu.VMEM((rank_c, rank_i, users), jnp.float32),
            pltpu.VMEM((devices * chunk, LANES), jnp.float32),
            pltpu.VMEM((2, BATCH, rank_i, users), jnp.float32),
        ],
        compiler_params=limit(12),
        cost_estimate=pl.CostEstimate(flops=2 * 10**9, bytes_accessed=12 * 10**6, transcendentals=0),
        name="tile_sums",
    )(where, count, me, blocks, weights, contexts, user_basis)
    return dict(zip(PIECES, out[:-2])), out[-2], out[-1]


def inverse_factor(gram):
    order = gram.shape[0]
    panels = order // ROWS
    sub = lax.broadcasted_iota(jnp.int32, (ROWS, order), 0)
    lane = lax.broadcasted_iota(jnp.int32, (ROWS, order), 1)
    left = [gram[ROWS * i : ROWS * (i + 1)] for i in range(panels)]
    right = [jnp.where(lane == sub + ROWS * i, 1.0, 0.0) for i in range(panels)]
    for k in range(panels):
        columns = {
            i: [
                jnp.broadcast_to(left[i][:, ROWS * k + j : ROWS * k + j + 1], (ROWS, order))
                for j in range(ROWS)
            ]
            for i in range(k, panels)
        }
        row, tail = left[k], right[k]
        scale = jnp.zeros((ROWS, order), jnp.float32)
        rows, tails = [], []
        for j in range(ROWS):
            head = columns[k][j]
            pivot = jnp.broadcast_to(head[j : j + 1], (ROWS, order))
            inverse = pl.reciprocal(pivot, approx=True)
            inverse = inverse * (2.0 - pivot * inverse)
            scale = jnp.where(sub == j, pivot, scale)
            rows.append(jnp.broadcast_to(row[j : j + 1], (ROWS, order)))
            tails.append(jnp.broadcast_to(tail[j : j + 1], (ROWS, order)))
            below = jnp.where(sub > j, head, 0.0) * inverse
            row = row - below * rows[j]
            tail = tail - below * tails[j]
            facts = {k: below}
            for i in range(k + 1, panels):
                facts[i] = columns[i][j] * inverse
            for c in range(j + 1, ROWS):
                crossing = jnp.broadcast_to(head[c : c + 1], (ROWS, order))
                for i in range(k, panels):
                    columns[i][c] = columns[i][c] - facts[i] * crossing
            for i in range(k + 1, panels):
                left[i] = left[i] - facts[i] * rows[j]
                right[i] = right[i] - facts[i] * tails[j]
        right[k] = tail * lax.rsqrt(scale)
    return jnp.concatenate(right, axis=0)


def finish_kernel(total_users, places, me_ref, high_ref, low_ref, *rest):
    piece_refs, (basis_ref, core_out_ref, pack_ref, full_ref) = rest[: len(PIECES)], rest[len(PIECES) :]
    me = me_ref[0]
    chunk = piece_refs[0].shape[1]
    for piece, ref in zip(PIECES, piece_refs):
        for i, position in enumerate(places[piece]):
            start = pl.multiple_of(jnp.bitwise_xor(me, position) * chunk, ROWS)
            pack_ref[pl.ds(start, chunk)] = ref[i]
    groups = full_ref.shape[0] // LANES
    place = 0
    for i in range(groups):
        for j in range(i, groups):
            block = pack_ref[place * LANES : (place + 1) * LANES]
            full_ref[i * LANES : (i + 1) * LANES, j * LANES : (j + 1) * LANES] = block
            if i != j:
                full_ref[j * LANES : (j + 1) * LANES, i * LANES : (i + 1) * LANES] = block.T
            place += 1
    projection = pack_ref[place * LANES : (place + groups) * LANES]
    turned = jnp.concatenate(
        [projection[i * LANES : (i + 1) * LANES].T for i in range(groups)], axis=1
    )
    turned_high, turned_low = split(turned)
    full_high, full_low = split(full_ref[...])
    crossed = dot(turned_high, full_high) + dot(turned_high, full_low) + dot(turned_low, full_high)
    gram = jnp.dot(crossed, projection, precision=HIGH, preferred_element_type=jnp.float32)
    projected = (
        dot(turned_high, high_ref[...]) + dot(turned_high, low_ref[...]) + dot(turned_low, high_ref[...])
    )
    inverse = inverse_factor(gram)
    root = total_users ** 0.5
    scaled = jnp.dot(inverse * root, projected, precision=HIGH, preferred_element_type=jnp.float32)
    for i in range(scaled.shape[1] // LANES):
        basis_ref[i * LANES : (i + 1) * LANES] = scaled[:, i * LANES : (i + 1) * LANES].T
    core_out_ref[...] = jnp.dot(
        inverse * (1.0 / root), crossed, precision=HIGH, preferred_element_type=jnp.float32
    )


def finish(me, high, low, pieces, devices):
    ranks, users = high.shape
    chunk = pack_rows(ranks, devices)
    return pl.pallas_call(
        functools.partial(finish_kernel, users * devices, piece_places(devices)),
        out_shape=(
            jax.ShapeDtypeStruct((users, LANES), jnp.float32),
            jax.ShapeDtypeStruct((LANES, ranks), jnp.float32),
        ),
        in_specs=[SMEM] + [VMEM] * (2 + len(PIECES)),
        out_specs=(VMEM, VMEM),
        scratch_shapes=[
            pltpu.VMEM((devices * chunk, LANES), jnp.float32),
            pltpu.VMEM((ranks, ranks), jnp.float32),
        ],
        compiler_params=limit(16),
        name="finish",
    )(me, high, low, *[pieces[piece] for piece in PIECES])


def swap(value, mask, devices):
    return lax.ppermute(value, "users", [(i, i ^ mask) for i in range(devices)])


def reduce_pieces(pieces, devices):
    got = {plane: swap(pieces[1, plane], 1, devices) for plane in (3, 1, 2, 0)}
    away = [swap(pieces[0, plane] + got[plane], 2 * plane, devices) for plane in (3, 1, 2)]
    rest = devices // 8
    total = None
    far = []
    for position in list(range(rest - 1, -1, -1)):
        rows = slice(position, position + 1)
        value = pieces[0, 0][rows] + got[0][rows] + away[0][rows] + away[1][rows] + away[2][rows]
        if position:
            far.append(swap(value, 8 * position, devices))
        else:
            total = value
    for value in far:
        total = total + value
    return total


def spread_pieces(total, devices):
    near = [total] + [swap(total, 8 * position, devices) for position in range(1, devices // 8)]
    near = jnp.concatenate(near, axis=0)
    pieces = {(0, 0): near}
    for plane in (3, 1, 2):
        pieces[0, plane] = swap(near, 2 * plane, devices)
    for plane in (0, 3, 1, 2):
        pieces[1, plane] = swap(pieces[0, plane], 1, devices)
    return pieces


def body(
    tile_owner, tile_slot, tile_cblock, tile_context, tile_weights,
    item_factors, context_factors, user_basis, user_counts,
):
    devices = lax.axis_size("users")
    half = devices // 2
    rank_c = context_factors.shape[0]
    me = lax.axis_index("users").astype(jnp.int32).reshape(1)

    mirror = swap(item_factors, half, devices)
    requests, where, own = route(me, tile_owner[:, 0], tile_slot, item_factors, half)
    sides = [list(range(half)), list(range(half, devices))]
    asked = lax.all_to_all(requests, "users", 0, 0, axis_index_groups=sides, tiled=True)
    found = collect(asked, own, mirror)
    found, cblock, factors = lax.optimization_barrier((found, tile_cblock, context_factors))
    blocks = lax.all_to_all(found, "users", 0, 0, axis_index_groups=sides, tiled=True)

    table = factors.astype(jnp.float32).reshape(rank_c, -1, CB).transpose(1, 0, 2)
    contexts, weights = stage(cblock, table, tile_context, tile_weights)
    pieces, high, low = tile_sums(
        where, user_counts, me, blocks, weights, contexts, user_basis, devices
    )
    pieces = spread_pieces(reduce_pieces(pieces, devices), devices)
    return finish(me, high, low, pieces, devices)


def solution(mesh):
    return jax.shard_map(
        body,
        mesh=mesh,
        in_specs=(
            P("users", None), P("users"), P("users"), P("users", None), P("users", None, None),
            P("users", None, None), P(), P("users", None), P("users"),
        ),
        out_specs=(P("users", None), P()),
        check_vma=False,
    )
```

```python
import functools

import jax
import jax.numpy as jnp
from jax import lax
from jax.experimental import pallas as pl
from jax.experimental.pallas import tpu as pltpu
from jax.sharding import PartitionSpec as P

CB = 8
SLOTS = 2
PLACES = 2 * SLOTS
HIGH = lax.Precision.HIGHEST
LANES = 128
ROWS = 8
BATCH = 8
CHUNKS = 8
MIB = 2**20

SMEM = pl.BlockSpec(memory_space=pltpu.SMEM)
VMEM = pl.BlockSpec(memory_space=pltpu.VMEM)
ANY = pl.BlockSpec(memory_space=pl.ANY)


def in_hbm(value):
    return pltpu.with_memory_space_constraint(value, pltpu.HBM)


def limit(mib):
    return pltpu.CompilerParams(vmem_limit_bytes=mib * MIB)


def dot(lhs, rhs):
    return jnp.dot(lhs, rhs, preferred_element_type=jnp.float32)


def dot_nt(lhs, rhs):
    return lax.dot_general(lhs, rhs, (((1,), (1,)), ((), ())), preferred_element_type=jnp.float32)


def split(value):
    high = value.astype(jnp.bfloat16)
    return high, (value - high.astype(jnp.float32)).astype(jnp.bfloat16)


def route_kernel(half, me_ref, owner_ref, slot_ref, own_ref, request_ref, where_ref, held_ref, used_ref, sem_ref):
    copy = pltpu.make_async_copy(own_ref, held_ref, sem_ref)
    copy.start()
    side = me_ref[0] // half
    lane = lax.broadcasted_iota(jnp.int32, (1, LANES), 1)

    def clear(place, _):
        used_ref[place] = 0
        return 0

    lax.fori_loop(0, 2 * half, clear, 0, unroll=8)
    request_ref[...] = jnp.zeros_like(request_ref)

    def assign(tile, _):
        owner = owner_ref[tile]
        taken = used_ref[owner]
        used_ref[owner] = taken + 1
        low = lax.rem(owner, half)
        place = jnp.where(owner // half == side, 0, SLOTS) + taken
        request_ref[low] = jnp.where(lane == place, slot_ref[tile], request_ref[low])
        where_ref[tile] = low * PLACES + place
        return 0

    lax.fori_loop(0, owner_ref.shape[0], assign, 0, unroll=4)
    copy.wait()


def route(me, owners, slots, own, half):
    return pl.pallas_call(
        functools.partial(route_kernel, half),
        out_shape=(
            jax.ShapeDtypeStruct((half, 1, LANES), jnp.int32),
            jax.ShapeDtypeStruct(owners.shape, jnp.int32),
            jax.ShapeDtypeStruct(own.shape, own.dtype),
        ),
        in_specs=[SMEM, SMEM, SMEM, ANY],
        out_specs=(VMEM, SMEM, VMEM),
        scratch_shapes=[pltpu.SMEM((2 * half,), jnp.int32), pltpu.SemaphoreType.DMA],
        compiler_params=limit(4),
        name="route",
    )(me, in_hbm(owners), in_hbm(slots), in_hbm(own))


def collect_kernel(asked_ref, own_ref, mirror_ref, out_ref):
    for peer in range(asked_ref.shape[0]):
        for place in range(PLACES):
            source = own_ref if place < SLOTS else mirror_ref
            out_ref[peer * PLACES + place] = source[asked_ref[peer, 0, place]]


def collect(asked, own, mirror):
    return pl.pallas_call(
        collect_kernel,
        out_shape=jax.ShapeDtypeStruct((asked.shape[0] * PLACES,) + own.shape[1:], own.dtype),
        in_specs=[SMEM, VMEM, VMEM],
        out_specs=VMEM,
        compiler_params=limit(4),
        name="collect",
    )(asked, own, mirror)


def context_kernel(cblock_ref, table_ref, marks_ref, context_ref):
    tiles, users = marks_ref.shape

    def one(tile, _):
        table = table_ref[cblock_ref[tile]]
        marks = jnp.broadcast_to(marks_ref[pl.ds(tile, 1), :], (ROWS, users))
        total = jnp.zeros((ROWS, users), jnp.float32)
        for k in range(CB):
            column = jnp.broadcast_to(table[:, k : k + 1], (ROWS, users))
            total = jnp.where(marks == k, column, total)
        context_ref[tile] = total
        return 0

    lax.fori_loop(0, tiles, one, 0, unroll=2)


def context_values(cblock, table, marks):
    tiles, users = marks.shape
    return pl.pallas_call(
        context_kernel,
        out_shape=jax.ShapeDtypeStruct((tiles, ROWS, users), jnp.float32),
        in_specs=[SMEM, VMEM, VMEM],
        out_specs=VMEM,
        compiler_params=limit(4),
        cost_estimate=pl.CostEstimate(flops=10**7, bytes_accessed=2 * 10**7, transcendentals=0),
        name="contexts",
    )(in_hbm(cblock), table, marks)


def pack_places(me):
    return {
        (core, plane): jnp.bitwise_xor(lax.rem(me, CHUNKS), core + 2 * plane)
        for core in range(2)
        for plane in range(4)
    }


PIECES = [(core, plane) for core in (1, 0) for plane in (3, 1, 2, 0)]


def pack_rows(ranks):
    groups = ranks // LANES
    return (groups * (groups + 1) // 2 + groups) * LANES


def tiles_kernel(
    where_ref, count_ref, me_ref, blocks_ref, weights_ref, context_ref, basis_ref, *refs
):
    piece_refs, refs = refs[: len(PIECES)], refs[len(PIECES) :]
    high_ref, low_ref, y_ref, pack_ref, even_ref, odd_ref = refs[:6]
    weights_held, context_held, basis_held, weights_sem, context_sem, basis_sem = refs[6:]
    rank_c, rank_i, users = y_ref.shape
    batches = weights_ref.shape[0] // BATCH
    half = rank_c // 2

    def weights_copy(batch):
        rows = pl.ds(batch * BATCH, BATCH)
        return pltpu.make_async_copy(weights_ref.at[rows], weights_held.at[rows], weights_sem.at[batch])

    weights_copy(0).start()
    contexts_copy = pltpu.make_async_copy(context_ref, context_held, context_sem)
    contexts_copy.start()
    for batch in range(1, batches):
        weights_copy(batch).start()
    basis_copy = pltpu.make_async_copy(basis_ref, basis_held, basis_sem)
    basis_copy.start()

    def multiply(batch, place, into_ref):
        tile = batch * BATCH + place
        product = dot(blocks_ref[where_ref[tile]], weights_held[tile])
        into_ref[place] = product.astype(jnp.bfloat16).astype(jnp.float32)

    def add(batch, part, from_ref):
        lanes = slice(part // 2 * LANES, (part // 2 + 1) * LANES)
        ranks = slice(part % 2 * half, (part % 2 + 1) * half)
        total = y_ref[ranks, :, lanes]
        for place in range(BATCH):
            values = context_held[batch * BATCH + place, ranks, lanes]
            total = total + values[:, None, :] * from_ref[place, :, lanes][None]
        y_ref[ranks, :, lanes] = total

    y_ref[...] = jnp.zeros_like(y_ref)
    parts = 2 * users // LANES
    weights_copy(0).wait()
    for place in range(BATCH):
        multiply(0, place, even_ref)
    contexts_copy.wait()

    def turn(batch, from_ref, into_ref):
        weights_copy(batch + 1).wait()
        for part in range(max(parts, BATCH)):
            if part < BATCH:
                multiply(batch + 1, part, into_ref)
            if part < parts:
                add(batch, part, from_ref)

    def pair(index, _):
        turn(2 * index, even_ref, odd_ref)
        turn(2 * index + 1, odd_ref, even_ref)
        return 0

    lax.fori_loop(0, batches // 2 - 1, pair, 0)
    turn(batches - 2, even_ref, odd_ref)
    for part in range(parts):
        add(batches - 1, part, odd_ref)

    living = lax.broadcasted_iota(jnp.int32, (rank_i, users), 1) < count_ref[0]
    for r in range(rank_c):
        high, low = split(jnp.where(living, y_ref[r], 0.0))
        high_ref[r * rank_i : (r + 1) * rank_i] = high
        low_ref[r * rank_i : (r + 1) * rank_i] = low
    ranks = rank_c * rank_i
    groups = ranks // LANES
    place = 0
    for i in range(groups):
        rows = slice(i * LANES, (i + 1) * LANES)
        strip = dot_nt(high_ref[rows], high_ref[i * LANES :])
        strip = strip + dot_nt(high_ref[rows], low_ref[i * LANES :])
        strip = strip + dot_nt(low_ref[rows], high_ref[i * LANES :])
        for j in range(groups - i):
            pack_ref[place * LANES : (place + 1) * LANES] = strip[:, j * LANES : (j + 1) * LANES]
            place += 1
    basis_copy.wait()
    basis_high, basis_low = split(basis_held[...])
    projection = dot(high_ref[...], basis_high) + dot(high_ref[...], basis_low) + dot(low_ref[...], basis_high)
    pack_ref[place * LANES : (place + groups) * LANES] = projection
    chunk = piece_refs[0].shape[0]
    places = pack_places(me_ref[0])
    for piece, ref in zip(PIECES, piece_refs):
        ref[...] = pack_ref[pl.ds(pl.multiple_of(places[piece] * chunk, ROWS), chunk)]


def tile_sums(where, count, me, blocks, weights, contexts, user_basis):
    tiles, _, users = weights.shape
    rank_i = blocks.shape[1]
    rank_c = contexts.shape[1]
    ranks = rank_c * rank_i
    rows = pack_rows(ranks)
    out_shape = (jax.ShapeDtypeStruct((rows // CHUNKS, LANES), jnp.float32),) * len(PIECES)
    out_shape += (jax.ShapeDtypeStruct((ranks, users), jnp.bfloat16),) * 2
    held = 3 * weights.size * 2 // (2 * MIB)
    out = pl.pallas_call(
        tiles_kernel,
        out_shape=out_shape,
        in_specs=[SMEM] * 3 + [VMEM] + [ANY] * 3,
        out_specs=(VMEM,) * len(out_shape),
        scratch_shapes=[
            pltpu.VMEM((rank_c, rank_i, users), jnp.float32),
            pltpu.VMEM((rows, LANES), jnp.float32),
            pltpu.VMEM((BATCH, rank_i, users), jnp.float32),
            pltpu.VMEM((BATCH, rank_i, users), jnp.float32),
            pltpu.VMEM(weights.shape, weights.dtype),
            pltpu.VMEM(contexts.shape, contexts.dtype),
            pltpu.VMEM(user_basis.shape, user_basis.dtype),
            pltpu.SemaphoreType.DMA((tiles // BATCH,)),
            pltpu.SemaphoreType.DMA,
            pltpu.SemaphoreType.DMA,
        ],
        compiler_params=limit(8 + held),
        cost_estimate=pl.CostEstimate(flops=2 * 10**9, bytes_accessed=12 * 10**6, transcendentals=0),
        name="tile_sums",
    )(where, count, me, blocks, in_hbm(weights), in_hbm(contexts), in_hbm(user_basis))
    return dict(zip(PIECES, out[:-2])), out[-2], out[-1]


def inverse_factor(gram):
    order = gram.shape[0]
    panels = order // ROWS
    sub = lax.broadcasted_iota(jnp.int32, (ROWS, order), 0)
    lane = lax.broadcasted_iota(jnp.int32, (ROWS, order), 1)
    left = [gram[ROWS * i : ROWS * (i + 1)] for i in range(panels)]
    right = [jnp.where(lane == sub + ROWS * i, 1.0, 0.0) for i in range(panels)]
    for k in range(panels):
        columns = {
            i: [
                jnp.broadcast_to(left[i][:, ROWS * k + j : ROWS * k + j + 1], (ROWS, order))
                for j in range(ROWS)
            ]
            for i in range(k, panels)
        }
        row, tail = left[k], right[k]
        scale = jnp.zeros((ROWS, order), jnp.float32)
        rows, tails = [], []
        for j in range(ROWS):
            head = columns[k][j]
            pivot = jnp.broadcast_to(head[j : j + 1], (ROWS, order))
            inverse = pl.reciprocal(pivot, approx=True)
            inverse = inverse * (2.0 - pivot * inverse)
            scale = jnp.where(sub == j, pivot, scale)
            rows.append(jnp.broadcast_to(row[j : j + 1], (ROWS, order)))
            tails.append(jnp.broadcast_to(tail[j : j + 1], (ROWS, order)))
            below = jnp.where(sub > j, head, 0.0) * inverse
            row = row - below * rows[j]
            tail = tail - below * tails[j]
            facts = {k: below}
            for i in range(k + 1, panels):
                facts[i] = columns[i][j] * inverse
            for c in range(j + 1, ROWS):
                crossing = jnp.broadcast_to(head[c : c + 1], (ROWS, order))
                for i in range(k, panels):
                    columns[i][c] = columns[i][c] - facts[i] * crossing
            for i in range(k + 1, panels):
                left[i] = left[i] - facts[i] * rows[j]
                right[i] = right[i] - facts[i] * tails[j]
        right[k] = tail * lax.rsqrt(scale)
    return jnp.concatenate(right, axis=0)


def finish_kernel(total_users, me_ref, high_ref, low_ref, *rest):
    piece_refs, (basis_ref, core_out_ref, pack_ref, full_ref) = rest[: len(PIECES)], rest[len(PIECES) :]
    chunk = piece_refs[0].shape[0]
    places = pack_places(me_ref[0])
    for piece, ref in zip(PIECES, piece_refs):
        pack_ref[pl.ds(pl.multiple_of(places[piece] * chunk, ROWS), chunk)] = ref[...]
    groups = full_ref.shape[0] // LANES
    place = 0
    for i in range(groups):
        for j in range(i, groups):
            block = pack_ref[place * LANES : (place + 1) * LANES]
            full_ref[i * LANES : (i + 1) * LANES, j * LANES : (j + 1) * LANES] = block
            if i != j:
                full_ref[j * LANES : (j + 1) * LANES, i * LANES : (i + 1) * LANES] = block.T
            place += 1
    projection = pack_ref[place * LANES : (place + groups) * LANES]
    turned = jnp.concatenate(
        [projection[i * LANES : (i + 1) * LANES].T for i in range(groups)], axis=1
    )
    turned_high, turned_low = split(turned)
    full_high, full_low = split(full_ref[...])
    crossed = dot(turned_high, full_high) + dot(turned_high, full_low) + dot(turned_low, full_high)
    gram = jnp.dot(crossed, projection, precision=HIGH, preferred_element_type=jnp.float32)
    projected = (
        dot(turned_high, high_ref[...]) + dot(turned_high, low_ref[...]) + dot(turned_low, high_ref[...])
    )
    inverse = inverse_factor(gram)
    root = total_users ** 0.5
    scaled = jnp.dot(inverse * root, projected, precision=HIGH, preferred_element_type=jnp.float32)
    for i in range(scaled.shape[1] // LANES):
        basis_ref[i * LANES : (i + 1) * LANES] = scaled[:, i * LANES : (i + 1) * LANES].T
    core_out_ref[...] = jnp.dot(
        inverse * (1.0 / root), crossed, precision=HIGH, preferred_element_type=jnp.float32
    )


def finish(me, high, low, pieces, devices):
    ranks, users = high.shape
    return pl.pallas_call(
        functools.partial(finish_kernel, users * devices),
        out_shape=(
            jax.ShapeDtypeStruct((users, LANES), jnp.float32),
            jax.ShapeDtypeStruct((LANES, ranks), jnp.float32),
        ),
        in_specs=[SMEM] + [VMEM] * (2 + len(PIECES)),
        out_specs=(VMEM, VMEM),
        scratch_shapes=[
            pltpu.VMEM((pack_rows(ranks), LANES), jnp.float32),
            pltpu.VMEM((ranks, ranks), jnp.float32),
        ],
        compiler_params=limit(16),
        name="finish",
    )(me, high, low, *[pieces[piece] for piece in PIECES])


def swap(value, mask, devices):
    return lax.ppermute(value, "users", [(i, i ^ mask) for i in range(devices)])


def reduce_pieces(pieces, devices):
    got = {plane: swap(pieces[1, plane], 1, devices) for plane in (3, 1, 2, 0)}
    total = pieces[0, 0] + got[0]
    for plane in (3, 1, 2):
        total = total + swap(pieces[0, plane] + got[plane], 2 * plane, devices)
    mask = CHUNKS
    while mask < devices:
        total = total + swap(total, mask, devices)
        mask *= 2
    return total


def spread_pieces(total, devices):
    pieces = {(0, 0): total}
    for plane in (3, 1, 2):
        pieces[0, plane] = swap(total, 2 * plane, devices)
    for plane in (0, 3, 1, 2):
        pieces[1, plane] = swap(pieces[0, plane], 1, devices)
    return pieces


def body(
    tile_owner, tile_slot, tile_cblock, tile_context, tile_weights,
    item_factors, context_factors, user_basis, user_counts,
):
    devices = lax.axis_size("users")
    half = devices // 2
    rank_c = context_factors.shape[0]
    me = lax.axis_index("users").astype(jnp.int32).reshape(1)

    mirror = swap(item_factors, half, devices)
    requests, where, own = route(me, tile_owner[:, 0], tile_slot, item_factors, half)
    sides = [list(range(half)), list(range(half, devices))]
    asked = lax.all_to_all(requests, "users", 0, 0, axis_index_groups=sides, tiled=True)
    found = collect(asked, own, mirror)
    found, cblock, factors = lax.optimization_barrier((found, tile_cblock, context_factors))
    blocks = lax.all_to_all(found, "users", 0, 0, axis_index_groups=sides, tiled=True)

    table = factors.astype(jnp.float32).reshape(rank_c, -1, CB).transpose(1, 0, 2)
    contexts = context_values(cblock, table, tile_context)
    pieces, high, low = tile_sums(
        where, user_counts, me, blocks, tile_weights, contexts, user_basis
    )
    pieces = spread_pieces(reduce_pieces(pieces, devices), devices)
    return finish(me, high, low, pieces, devices)


def solution(mesh):
    return jax.shard_map(
        body,
        mesh=mesh,
        in_specs=(
            P("users", None), P("users"), P("users"), P("users", None), P("users", None, None),
            P("users", None, None), P(), P("users", None), P("users"),
        ),
        out_specs=(P("users", None), P()),
        check_vma=False,
    )
```

```python
import functools

import jax
import jax.numpy as jnp
from jax import lax
from jax.experimental import pallas as pl
from jax.experimental.pallas import tpu as pltpu
from jax.sharding import PartitionSpec as P

CB = 8
SLOTS = 2
PLACES = 2 * SLOTS
HIGH = lax.Precision.HIGHEST
LANES = 128
ROWS = 8
BATCH = 8
CHUNKS = 8
MIB = 2**20

SMEM = pl.BlockSpec(memory_space=pltpu.SMEM)
VMEM = pl.BlockSpec(memory_space=pltpu.VMEM)
ANY = pl.BlockSpec(memory_space=pl.ANY)


def in_hbm(value):
    return pltpu.with_memory_space_constraint(value, pltpu.HBM)


def limit(mib):
    return pltpu.CompilerParams(vmem_limit_bytes=mib * MIB)


def dot(lhs, rhs):
    return jnp.dot(lhs, rhs, preferred_element_type=jnp.float32)


def dot_nt(lhs, rhs):
    return lax.dot_general(lhs, rhs, (((1,), (1,)), ((), ())), preferred_element_type=jnp.float32)


def split(value):
    high = value.astype(jnp.bfloat16)
    return high, (value - high.astype(jnp.float32)).astype(jnp.bfloat16)


def route_kernel(half, me_ref, owner_ref, slot_ref, own_ref, request_ref, where_ref, held_ref, used_ref, sem_ref):
    copy = pltpu.make_async_copy(own_ref, held_ref, sem_ref)
    copy.start()
    side = me_ref[0] // half
    lane = lax.broadcasted_iota(jnp.int32, (1, LANES), 1)

    def clear(place, _):
        used_ref[place] = 0
        return 0

    lax.fori_loop(0, 2 * half, clear, 0, unroll=8)
    request_ref[...] = jnp.zeros_like(request_ref)

    def assign(tile, _):
        owner = owner_ref[tile]
        taken = used_ref[owner]
        used_ref[owner] = taken + 1
        low = lax.rem(owner, half)
        place = jnp.where(owner // half == side, 0, SLOTS) + taken
        request_ref[low] = jnp.where(lane == place, slot_ref[tile], request_ref[low])
        where_ref[tile] = low * PLACES + place
        return 0

    lax.fori_loop(0, owner_ref.shape[0], assign, 0, unroll=4)
    copy.wait()


def route(me, owners, slots, own, half):
    return pl.pallas_call(
        functools.partial(route_kernel, half),
        out_shape=(
            jax.ShapeDtypeStruct((half, 1, LANES), jnp.int32),
            jax.ShapeDtypeStruct(owners.shape, jnp.int32),
            jax.ShapeDtypeStruct(own.shape, own.dtype),
        ),
        in_specs=[SMEM, SMEM, SMEM, ANY],
        out_specs=(VMEM, SMEM, VMEM),
        scratch_shapes=[pltpu.SMEM((2 * half,), jnp.int32), pltpu.SemaphoreType.DMA],
        compiler_params=limit(4),
        name="route",
    )(me, in_hbm(owners), in_hbm(slots), in_hbm(own))


def collect_kernel(asked_ref, own_ref, mirror_ref, out_ref):
    for peer in range(asked_ref.shape[0]):
        for place in range(PLACES):
            source = own_ref if place < SLOTS else mirror_ref
            out_ref[peer * PLACES + place] = source[asked_ref[peer, 0, place]]


def collect(asked, own, mirror):
    return pl.pallas_call(
        collect_kernel,
        out_shape=jax.ShapeDtypeStruct((asked.shape[0] * PLACES,) + own.shape[1:], own.dtype),
        in_specs=[SMEM, VMEM, VMEM],
        out_specs=VMEM,
        compiler_params=limit(4),
        name="collect",
    )(asked, own, mirror)


def context_kernel(cblock_ref, table_ref, marks_ref, context_ref):
    tiles, users = marks_ref.shape

    def one(tile, _):
        table = table_ref[cblock_ref[tile]]
        marks = jnp.broadcast_to(marks_ref[pl.ds(tile, 1), :], (ROWS, users))
        total = jnp.zeros((ROWS, users), jnp.float32)
        for k in range(CB):
            column = jnp.broadcast_to(table[:, k : k + 1], (ROWS, users))
            total = jnp.where(marks == k, column, total)
        context_ref[tile] = total
        return 0

    lax.fori_loop(0, tiles, one, 0, unroll=2)


def context_values(cblock, table, marks):
    tiles, users = marks.shape
    return pl.pallas_call(
        context_kernel,
        out_shape=jax.ShapeDtypeStruct((tiles, ROWS, users), jnp.float32),
        in_specs=[SMEM, VMEM, VMEM],
        out_specs=VMEM,
        compiler_params=limit(4),
        cost_estimate=pl.CostEstimate(flops=10**7, bytes_accessed=2 * 10**7, transcendentals=0),
        name="contexts",
    )(in_hbm(cblock), table, marks)


def pack_places(me):
    return {
        (core, plane): jnp.bitwise_xor(lax.rem(me, CHUNKS), core + 2 * plane)
        for core in range(2)
        for plane in range(4)
    }


PIECES = [(core, plane) for core in (1, 0) for plane in (3, 1, 2, 0)]


def pack_rows(ranks):
    groups = ranks // LANES
    return (groups * (groups + 1) // 2 + groups) * LANES


def tiles_kernel(
    where_ref, count_ref, me_ref, blocks_ref, weights_ref, context_ref, basis_ref, *refs
):
    piece_refs, refs = refs[: len(PIECES)], refs[len(PIECES) :]
    high_ref, low_ref, y_ref, pack_ref, even_ref, odd_ref = refs[:6]
    weights_held, context_held, basis_held, weights_sem, context_sem, basis_sem = refs[6:]
    rank_c, rank_i, users = y_ref.shape
    batches = weights_ref.shape[0] // BATCH
    half = rank_c // 2

    def weights_copy(batch):
        rows = pl.ds(batch * BATCH, BATCH)
        return pltpu.make_async_copy(weights_ref.at[rows], weights_held.at[rows], weights_sem.at[batch])

    weights_copy(0).start()
    contexts_copy = pltpu.make_async_copy(context_ref, context_held, context_sem)
    contexts_copy.start()
    for batch in range(1, batches):
        weights_copy(batch).start()
    basis_copy = pltpu.make_async_copy(basis_ref, basis_held, basis_sem)
    basis_copy.start()

    def multiply(batch, place, into_ref):
        tile = batch * BATCH + place
        product = dot(blocks_ref[where_ref[tile]], weights_held[tile])
        into_ref[place] = product.astype(jnp.bfloat16).astype(jnp.float32)

    def add(batch, part, from_ref):
        lanes = slice(part // 2 * LANES, (part // 2 + 1) * LANES)
        ranks = range(part % 2 * half, (part % 2 + 1) * half)
        strips = [slice(i, i + ROWS) for i in range(0, rank_i, ROWS)]
        totals = [[y_ref[r, strip, lanes] for strip in strips] for r in ranks]
        for place in range(BATCH):
            parts_of = [from_ref[place, strip, lanes] for strip in strips]
            for i, r in enumerate(ranks):
                values = context_held[batch * BATCH + place, r : r + 1, lanes]
                values = jnp.broadcast_to(values, (ROWS, LANES))
                for j in range(len(strips)):
                    totals[i][j] = totals[i][j] + values * parts_of[j]
        for i, r in enumerate(ranks):
            for strip, total in zip(strips, totals[i]):
                y_ref[r, strip, lanes] = total

    y_ref[...] = jnp.zeros_like(y_ref)
    parts = 2 * users // LANES
    weights_copy(0).wait()
    for place in range(BATCH):
        multiply(0, place, even_ref)
    contexts_copy.wait()

    def turn(batch, from_ref, into_ref):
        weights_copy(batch + 1).wait()
        for part in range(max(parts, BATCH)):
            if part < BATCH:
                multiply(batch + 1, part, into_ref)
            if part < parts:
                add(batch, part, from_ref)

    def pair(index, _):
        turn(2 * index, even_ref, odd_ref)
        turn(2 * index + 1, odd_ref, even_ref)
        return 0

    lax.fori_loop(0, batches // 2 - 1, pair, 0)
    turn(batches - 2, even_ref, odd_ref)
    for part in range(parts):
        add(batches - 1, part, odd_ref)

    living = lax.broadcasted_iota(jnp.int32, (rank_i, users), 1) < count_ref[0]
    for r in range(rank_c):
        high, low = split(jnp.where(living, y_ref[r], 0.0))
        high_ref[r * rank_i : (r + 1) * rank_i] = high
        low_ref[r * rank_i : (r + 1) * rank_i] = low
    ranks = rank_c * rank_i
    groups = ranks // LANES
    place = 0
    for i in range(groups):
        rows = slice(i * LANES, (i + 1) * LANES)
        strip = dot_nt(high_ref[rows], high_ref[i * LANES :])
        strip = strip + dot_nt(high_ref[rows], low_ref[i * LANES :])
        strip = strip + dot_nt(low_ref[rows], high_ref[i * LANES :])
        for j in range(groups - i):
            pack_ref[place * LANES : (place + 1) * LANES] = strip[:, j * LANES : (j + 1) * LANES]
            place += 1
    basis_copy.wait()
    basis_high, basis_low = split(basis_held[...])
    projection = dot(high_ref[...], basis_high) + dot(high_ref[...], basis_low) + dot(low_ref[...], basis_high)
    pack_ref[place * LANES : (place + groups) * LANES] = projection
    chunk = piece_refs[0].shape[0]
    places = pack_places(me_ref[0])
    for piece, ref in zip(PIECES, piece_refs):
        ref[...] = pack_ref[pl.ds(pl.multiple_of(places[piece] * chunk, ROWS), chunk)]


def tile_sums(where, count, me, blocks, weights, contexts, user_basis):
    tiles, _, users = weights.shape
    rank_i = blocks.shape[1]
    rank_c = contexts.shape[1]
    ranks = rank_c * rank_i
    rows = pack_rows(ranks)
    out_shape = (jax.ShapeDtypeStruct((rows // CHUNKS, LANES), jnp.float32),) * len(PIECES)
    out_shape += (jax.ShapeDtypeStruct((ranks, users), jnp.bfloat16),) * 2
    held = 3 * weights.size * 2 // (2 * MIB)
    out = pl.pallas_call(
        tiles_kernel,
        out_shape=out_shape,
        in_specs=[SMEM] * 3 + [VMEM] + [ANY] * 3,
        out_specs=(VMEM,) * len(out_shape),
        scratch_shapes=[
            pltpu.VMEM((rank_c, rank_i, users), jnp.float32),
            pltpu.VMEM((rows, LANES), jnp.float32),
            pltpu.VMEM((BATCH, rank_i, users), jnp.float32),
            pltpu.VMEM((BATCH, rank_i, users), jnp.float32),
            pltpu.VMEM(weights.shape, weights.dtype),
            pltpu.VMEM(contexts.shape, contexts.dtype),
            pltpu.VMEM(user_basis.shape, user_basis.dtype),
            pltpu.SemaphoreType.DMA((tiles // BATCH,)),
            pltpu.SemaphoreType.DMA,
            pltpu.SemaphoreType.DMA,
        ],
        compiler_params=limit(8 + held),
        cost_estimate=pl.CostEstimate(flops=2 * 10**9, bytes_accessed=12 * 10**6, transcendentals=0),
        name="tile_sums",
    )(where, count, me, blocks, in_hbm(weights), in_hbm(contexts), in_hbm(user_basis))
    return dict(zip(PIECES, out[:-2])), out[-2], out[-1]


def inverse_factor(gram):
    order = gram.shape[0]
    panels = order // ROWS
    sub = lax.broadcasted_iota(jnp.int32, (ROWS, order), 0)
    lane = lax.broadcasted_iota(jnp.int32, (ROWS, order), 1)
    left = [gram[ROWS * i : ROWS * (i + 1)] for i in range(panels)]
    right = [jnp.where(lane == sub + ROWS * i, 1.0, 0.0) for i in range(panels)]
    for k in range(panels):
        columns = {
            i: [
                jnp.broadcast_to(left[i][:, ROWS * k + j : ROWS * k + j + 1], (ROWS, order))
                for j in range(ROWS)
            ]
            for i in range(k, panels)
        }
        row, tail = left[k], right[k]
        scale = jnp.zeros((ROWS, order), jnp.float32)
        rows, tails = [], []
        for j in range(ROWS):
            head = columns[k][j]
            pivot = jnp.broadcast_to(head[j : j + 1], (ROWS, order))
            inverse = pl.reciprocal(pivot, approx=True)
            inverse = inverse * (2.0 - pivot * inverse)
            scale = jnp.where(sub == j, pivot, scale)
            rows.append(jnp.broadcast_to(row[j : j + 1], (ROWS, order)))
            tails.append(jnp.broadcast_to(tail[j : j + 1], (ROWS, order)))
            below = jnp.where(sub > j, head, 0.0) * inverse
            row = row - below * rows[j]
            tail = tail - below * tails[j]
            facts = {k: below}
            for i in range(k + 1, panels):
                facts[i] = columns[i][j] * inverse
            for c in range(j + 1, ROWS):
                crossing = jnp.broadcast_to(head[c : c + 1], (ROWS, order))
                for i in range(k, panels):
                    columns[i][c] = columns[i][c] - facts[i] * crossing
            for i in range(k + 1, panels):
                left[i] = left[i] - facts[i] * rows[j]
                right[i] = right[i] - facts[i] * tails[j]
        right[k] = tail * lax.rsqrt(scale)
    return jnp.concatenate(right, axis=0)


def finish_kernel(total_users, me_ref, high_ref, low_ref, *rest):
    piece_refs, (basis_ref, core_out_ref, pack_ref, full_ref) = rest[: len(PIECES)], rest[len(PIECES) :]
    chunk = piece_refs[0].shape[0]
    places = pack_places(me_ref[0])
    for piece, ref in zip(PIECES, piece_refs):
        pack_ref[pl.ds(pl.multiple_of(places[piece] * chunk, ROWS), chunk)] = ref[...]
    groups = full_ref.shape[0] // LANES
    place = 0
    for i in range(groups):
        for j in range(i, groups):
            block = pack_ref[place * LANES : (place + 1) * LANES]
            full_ref[i * LANES : (i + 1) * LANES, j * LANES : (j + 1) * LANES] = block
            if i != j:
                full_ref[j * LANES : (j + 1) * LANES, i * LANES : (i + 1) * LANES] = block.T
            place += 1
    projection = pack_ref[place * LANES : (place + groups) * LANES]
    turned = jnp.concatenate(
        [projection[i * LANES : (i + 1) * LANES].T for i in range(groups)], axis=1
    )
    turned_high, turned_low = split(turned)
    full_high, full_low = split(full_ref[...])
    crossed = dot(turned_high, full_high) + dot(turned_high, full_low) + dot(turned_low, full_high)
    gram = jnp.dot(crossed, projection, precision=HIGH, preferred_element_type=jnp.float32)
    projected = (
        dot(turned_high, high_ref[...]) + dot(turned_high, low_ref[...]) + dot(turned_low, high_ref[...])
    )
    inverse = inverse_factor(gram)
    root = total_users ** 0.5
    scaled = jnp.dot(inverse * root, projected, precision=HIGH, preferred_element_type=jnp.float32)
    for i in range(scaled.shape[1] // LANES):
        basis_ref[i * LANES : (i + 1) * LANES] = scaled[:, i * LANES : (i + 1) * LANES].T
    core_out_ref[...] = jnp.dot(
        inverse * (1.0 / root), crossed, precision=HIGH, preferred_element_type=jnp.float32
    )


def finish(me, high, low, pieces, devices):
    ranks, users = high.shape
    return pl.pallas_call(
        functools.partial(finish_kernel, users * devices),
        out_shape=(
            jax.ShapeDtypeStruct((users, LANES), jnp.float32),
            jax.ShapeDtypeStruct((LANES, ranks), jnp.float32),
        ),
        in_specs=[SMEM] + [VMEM] * (2 + len(PIECES)),
        out_specs=(VMEM, VMEM),
        scratch_shapes=[
            pltpu.VMEM((pack_rows(ranks), LANES), jnp.float32),
            pltpu.VMEM((ranks, ranks), jnp.float32),
        ],
        compiler_params=limit(16),
        name="finish",
    )(me, high, low, *[pieces[piece] for piece in PIECES])


def swap(value, mask, devices):
    return lax.ppermute(value, "users", [(i, i ^ mask) for i in range(devices)])


def reduce_pieces(pieces, devices):
    got = {plane: swap(pieces[1, plane], 1, devices) for plane in (3, 1, 2, 0)}
    total = pieces[0, 0] + got[0]
    for plane in (3, 1, 2):
        total = total + swap(pieces[0, plane] + got[plane], 2 * plane, devices)
    mask = CHUNKS
    while mask < devices:
        total = total + swap(total, mask, devices)
        mask *= 2
    return total


def spread_pieces(total, devices):
    pieces = {(0, 0): total}
    for plane in (3, 1, 2):
        pieces[0, plane] = swap(total, 2 * plane, devices)
    for plane in (0, 3, 1, 2):
        pieces[1, plane] = swap(pieces[0, plane], 1, devices)
    return pieces


def body(
    tile_owner, tile_slot, tile_cblock, tile_context, tile_weights,
    item_factors, context_factors, user_basis, user_counts,
):
    devices = lax.axis_size("users")
    half = devices // 2
    rank_c = context_factors.shape[0]
    me = lax.axis_index("users").astype(jnp.int32).reshape(1)

    mirror = swap(item_factors, half, devices)
    requests, where, own = route(me, tile_owner[:, 0], tile_slot, item_factors, half)
    sides = [list(range(half)), list(range(half, devices))]
    asked = lax.all_to_all(requests, "users", 0, 0, axis_index_groups=sides, tiled=True)
    found = collect(asked, own, mirror)
    found, cblock, factors = lax.optimization_barrier((found, tile_cblock, context_factors))
    blocks = lax.all_to_all(found, "users", 0, 0, axis_index_groups=sides, tiled=True)

    table = factors.astype(jnp.float32).reshape(rank_c, -1, CB).transpose(1, 0, 2)
    contexts = context_values(cblock, table, tile_context)
    pieces, high, low = tile_sums(
        where, user_counts, me, blocks, tile_weights, contexts, user_basis
    )
    pieces = spread_pieces(reduce_pieces(pieces, devices), devices)
    return finish(me, high, low, pieces, devices)


def solution(mesh):
    return jax.shard_map(
        body,
        mesh=mesh,
        in_specs=(
            P("users", None), P("users"), P("users"), P("users", None), P("users", None, None),
            P("users", None, None), P(), P("users", None), P("users"),
        ),
        out_specs=(P("users", None), P()),
        check_vma=False,
    )
```

```python
import functools

import jax
import jax.numpy as jnp
from jax import lax
from jax.experimental import pallas as pl
from jax.experimental.pallas import tpu as pltpu
from jax.sharding import PartitionSpec as P

CB = 8
SLOTS = 2
PLACES = 2 * SLOTS
LANES = 128
ROWS = 8
BATCH = 8
CHUNKS = 8
MIB = 2**20

SMEM = pl.BlockSpec(memory_space=pltpu.SMEM)
VMEM = pl.BlockSpec(memory_space=pltpu.VMEM)
ANY = pl.BlockSpec(memory_space=pl.ANY)


def in_hbm(value):
    return pltpu.with_memory_space_constraint(value, pltpu.HBM)


def limit(mib):
    return pltpu.CompilerParams(vmem_limit_bytes=mib * MIB)


def dot(lhs, rhs):
    return jnp.dot(lhs, rhs, preferred_element_type=jnp.float32)


def dot_nt(lhs, rhs):
    return lax.dot_general(lhs, rhs, (((1,), (1,)), ((), ())), preferred_element_type=jnp.float32)


def split(value):
    high = value.astype(jnp.bfloat16)
    return high, (value - high.astype(jnp.float32)).astype(jnp.bfloat16)


def quarters(value):
    rows, lanes = value.shape[0] // 2, value.shape[1] // 2
    return (value[:rows, :lanes] + value[:rows, lanes:]) + (value[rows:, :lanes] + value[rows:, lanes:])


def thrice(stack, high, low, product):
    rows = stack.shape[0] // 2
    first = product(stack, high)
    return first[:rows] + (first[rows:] + product(stack[:rows], low))


def route_kernel(half, me_ref, owner_ref, slot_ref, own_ref, request_ref, where_ref, held_ref, used_ref, sem_ref):
    copy = pltpu.make_async_copy(own_ref, held_ref, sem_ref)
    copy.start()
    side = me_ref[0] // half
    lane = lax.broadcasted_iota(jnp.int32, (1, LANES), 1)

    def clear(place, _):
        used_ref[place] = 0
        return 0

    lax.fori_loop(0, 2 * half, clear, 0, unroll=8)
    request_ref[...] = jnp.zeros_like(request_ref)

    def assign(tile, _):
        owner = owner_ref[tile]
        taken = used_ref[owner]
        used_ref[owner] = taken + 1
        low = lax.rem(owner, half)
        place = jnp.where(owner // half == side, 0, SLOTS) + taken
        request_ref[low] = jnp.where(lane == place, slot_ref[tile], request_ref[low])
        where_ref[tile] = low * PLACES + place
        return 0

    lax.fori_loop(0, owner_ref.shape[0], assign, 0, unroll=4)
    copy.wait()


def route(me, owners, slots, own, half):
    return pl.pallas_call(
        functools.partial(route_kernel, half),
        out_shape=(
            jax.ShapeDtypeStruct((half, 1, LANES), jnp.int32),
            jax.ShapeDtypeStruct(owners.shape, jnp.int32),
            jax.ShapeDtypeStruct(own.shape, own.dtype),
        ),
        in_specs=[SMEM, SMEM, SMEM, ANY],
        out_specs=(VMEM, SMEM, VMEM),
        scratch_shapes=[pltpu.SMEM((2 * half,), jnp.int32), pltpu.SemaphoreType.DMA],
        compiler_params=limit(4),
        name="route",
    )(me, in_hbm(owners), in_hbm(slots), in_hbm(own))


def collect_kernel(asked_ref, own_ref, mirror_ref, out_ref):
    for peer in range(asked_ref.shape[0]):
        for place in range(PLACES):
            source = own_ref if place < SLOTS else mirror_ref
            out_ref[peer * PLACES + place] = source[asked_ref[peer, 0, place]]


def collect(asked, own, mirror):
    return pl.pallas_call(
        collect_kernel,
        out_shape=jax.ShapeDtypeStruct((asked.shape[0] * PLACES,) + own.shape[1:], own.dtype),
        in_specs=[SMEM, VMEM, VMEM],
        out_specs=VMEM,
        compiler_params=limit(4),
        name="collect",
    )(asked, own, mirror)


def context_kernel(cblock_ref, table_ref, marks_ref, context_ref):
    tiles, users = marks_ref.shape

    def one(tile, _):
        table = table_ref[cblock_ref[tile]]
        marks = jnp.broadcast_to(marks_ref[pl.ds(tile, 1), :], (ROWS, users))
        total = jnp.zeros((ROWS, users), jnp.float32)
        for k in range(CB):
            column = jnp.broadcast_to(table[:, k : k + 1], (ROWS, users))
            total = jnp.where(marks == k, column, total)
        context_ref[tile] = total
        return 0

    lax.fori_loop(0, tiles, one, 0, unroll=2)


def context_values(cblock, table, marks):
    tiles, users = marks.shape
    return pl.pallas_call(
        context_kernel,
        out_shape=jax.ShapeDtypeStruct((tiles, ROWS, users), jnp.float32),
        in_specs=[SMEM, VMEM, VMEM],
        out_specs=VMEM,
        compiler_params=limit(4),
        cost_estimate=pl.CostEstimate(flops=10**7, bytes_accessed=2 * 10**7, transcendentals=0),
        name="contexts",
    )(in_hbm(cblock), table, marks)


def pack_places(me):
    return {
        (core, plane): jnp.bitwise_xor(lax.rem(me, CHUNKS), core + 2 * plane)
        for core in range(2)
        for plane in range(4)
    }


PIECES = [(core, plane) for core in (1, 0) for plane in (3, 1, 2, 0)]


def pack_rows(ranks):
    groups = ranks // LANES
    return (groups * (groups + 1) // 2 + groups) * LANES


def tiles_kernel(
    where_ref, count_ref, me_ref, blocks_ref, weights_ref, context_ref, basis_ref, *refs
):
    piece_refs, refs = refs[: len(PIECES)], refs[len(PIECES) :]
    stack_ref, y_ref, square_ref, pack_ref, even_ref, odd_ref = refs[:6]
    weights_held, context_held, basis_held, weights_sem, context_sem, basis_sem = refs[6:]
    rank_c, rank_i, users = y_ref.shape
    batches = weights_ref.shape[0] // BATCH
    half = rank_c // 2

    def weights_copy(batch):
        rows = pl.ds(batch * BATCH, BATCH)
        return pltpu.make_async_copy(weights_ref.at[rows], weights_held.at[rows], weights_sem.at[batch])

    weights_copy(0).start()
    contexts_copy = pltpu.make_async_copy(context_ref, context_held, context_sem)
    contexts_copy.start()
    for batch in range(1, batches):
        weights_copy(batch).start()
    basis_copy = pltpu.make_async_copy(basis_ref, basis_held, basis_sem)
    basis_copy.start()

    def multiply(batch, place, into_ref):
        tile = batch * BATCH + place
        product = dot(blocks_ref[where_ref[tile]], weights_held[tile])
        into_ref[place] = product.astype(jnp.bfloat16).astype(jnp.float32)

    def add(batch, part, from_ref):
        lanes = slice(part // 2 * LANES, (part // 2 + 1) * LANES)
        ranks = range(part % 2 * half, (part % 2 + 1) * half)
        strips = [slice(i, i + ROWS) for i in range(0, rank_i, ROWS)]
        totals = [[y_ref[r, strip, lanes] for strip in strips] for r in ranks]
        for place in range(BATCH):
            parts_of = [from_ref[place, strip, lanes] for strip in strips]
            for i, r in enumerate(ranks):
                values = context_held[batch * BATCH + place, r : r + 1, lanes]
                values = jnp.broadcast_to(values, (ROWS, LANES))
                for j in range(len(strips)):
                    totals[i][j] = totals[i][j] + values * parts_of[j]
        for i, r in enumerate(ranks):
            for strip, total in zip(strips, totals[i]):
                y_ref[r, strip, lanes] = total

    y_ref[...] = jnp.zeros_like(y_ref)
    parts = 2 * users // LANES
    weights_copy(0).wait()
    for place in range(BATCH):
        multiply(0, place, even_ref)
    contexts_copy.wait()

    def turn(batch, from_ref, into_ref):
        weights_copy(batch + 1).wait()
        for part in range(max(parts, BATCH)):
            if part < BATCH:
                multiply(batch + 1, part, into_ref)
            if part < parts:
                add(batch, part, from_ref)

    def pair(index, _):
        turn(2 * index, even_ref, odd_ref)
        turn(2 * index + 1, odd_ref, even_ref)
        return 0

    lax.fori_loop(0, batches // 2 - 1, pair, 0)
    turn(batches - 2, even_ref, odd_ref)
    for part in range(parts):
        add(batches - 1, part, odd_ref)

    living = lax.broadcasted_iota(jnp.int32, (rank_i, users), 1) < count_ref[0]
    ranks = rank_c * rank_i
    for r in range(rank_c):
        high, low = split(jnp.where(living, y_ref[r], 0.0))
        stack_ref[r * rank_i : (r + 1) * rank_i] = high
        stack_ref[ranks + r * rank_i : ranks + (r + 1) * rank_i] = low
    square_ref[...] = dot_nt(stack_ref[...], stack_ref[:ranks])
    basis_copy.wait()
    projection = dot(stack_ref[...], jnp.concatenate(split(basis_held[...]), axis=1))
    groups = ranks // LANES
    place = 0
    for i in range(groups):
        rows = slice(i * LANES, (i + 1) * LANES)
        low_rows = slice(ranks + i * LANES, ranks + (i + 1) * LANES)
        for j in range(i, groups):
            lanes = slice(j * LANES, (j + 1) * LANES)
            low_lanes = slice(ranks + j * LANES, ranks + (j + 1) * LANES)
            block = square_ref[rows, lanes] + square_ref[low_rows, lanes] + square_ref[low_lanes, rows].T
            pack_ref[place * LANES : (place + 1) * LANES] = block
            place += 1
    pack_ref[place * LANES : (place + groups) * LANES] = quarters(projection)
    chunk = piece_refs[0].shape[0]
    places = pack_places(me_ref[0])
    for piece, ref in zip(PIECES, piece_refs):
        ref[...] = pack_ref[pl.ds(pl.multiple_of(places[piece] * chunk, ROWS), chunk)]


def tile_sums(where, count, me, blocks, weights, contexts, user_basis):
    tiles, _, users = weights.shape
    rank_i = blocks.shape[1]
    rank_c = contexts.shape[1]
    ranks = rank_c * rank_i
    rows = pack_rows(ranks)
    out_shape = (jax.ShapeDtypeStruct((rows // CHUNKS, LANES), jnp.float32),) * len(PIECES)
    out_shape += (jax.ShapeDtypeStruct((2 * ranks, users), jnp.bfloat16),)
    held = 3 * weights.size * 2 // (2 * MIB)
    out = pl.pallas_call(
        tiles_kernel,
        out_shape=out_shape,
        in_specs=[SMEM] * 3 + [VMEM] + [ANY] * 3,
        out_specs=(VMEM,) * len(out_shape),
        scratch_shapes=[
            pltpu.VMEM((rank_c, rank_i, users), jnp.float32),
            pltpu.VMEM((2 * ranks, ranks), jnp.float32),
            pltpu.VMEM((rows, LANES), jnp.float32),
            pltpu.VMEM((BATCH, rank_i, users), jnp.float32),
            pltpu.VMEM((BATCH, rank_i, users), jnp.float32),
            pltpu.VMEM(weights.shape, weights.dtype),
            pltpu.VMEM(contexts.shape, contexts.dtype),
            pltpu.VMEM(user_basis.shape, user_basis.dtype),
            pltpu.SemaphoreType.DMA((tiles // BATCH,)),
            pltpu.SemaphoreType.DMA,
            pltpu.SemaphoreType.DMA,
        ],
        compiler_params=limit(12 + held),
        cost_estimate=pl.CostEstimate(flops=2 * 10**9, bytes_accessed=12 * 10**6, transcendentals=0),
        name="tile_sums",
    )(where, count, me, blocks, in_hbm(weights), in_hbm(contexts), in_hbm(user_basis))
    return dict(zip(PIECES, out[:-1])), out[-1]


def inverse_factor(gram):
    order = gram.shape[0]
    panels = order // ROWS
    sub = lax.broadcasted_iota(jnp.int32, (ROWS, order), 0)
    lane = lax.broadcasted_iota(jnp.int32, (ROWS, order), 1)
    left = [gram[ROWS * i : ROWS * (i + 1)] for i in range(panels)]
    right = [jnp.where(lane == sub + ROWS * i, 1.0, 0.0) for i in range(panels)]
    for k in range(panels):
        columns = {
            i: [
                jnp.broadcast_to(left[i][:, ROWS * k + j : ROWS * k + j + 1], (ROWS, order))
                for j in range(ROWS)
            ]
            for i in range(k, panels)
        }
        row, tail = left[k], right[k]
        scale = jnp.zeros((ROWS, order), jnp.float32)
        rows, tails = [], []
        for j in range(ROWS):
            head = columns[k][j]
            pivot = jnp.broadcast_to(head[j : j + 1], (ROWS, order))
            inverse = pl.reciprocal(pivot, approx=True)
            inverse = inverse * (2.0 - pivot * inverse)
            scale = jnp.where(sub == j, pivot, scale)
            rows.append(jnp.broadcast_to(row[j : j + 1], (ROWS, order)))
            tails.append(jnp.broadcast_to(tail[j : j + 1], (ROWS, order)))
            below = jnp.where(sub > j, head, 0.0) * inverse
            row = row - below * rows[j]
            tail = tail - below * tails[j]
            facts = {k: below}
            for i in range(k + 1, panels):
                facts[i] = columns[i][j] * inverse
            for c in range(j + 1, ROWS):
                crossing = jnp.broadcast_to(head[c : c + 1], (ROWS, order))
                for i in range(k, panels):
                    columns[i][c] = columns[i][c] - facts[i] * crossing
            for i in range(k + 1, panels):
                left[i] = left[i] - facts[i] * rows[j]
                right[i] = right[i] - facts[i] * tails[j]
        right[k] = tail * lax.rsqrt(scale)
    return jnp.concatenate(right, axis=0)


def finish_kernel(total_users, me_ref, stack_ref, *rest):
    piece_refs, (basis_ref, core_out_ref, pack_ref, full_ref) = rest[: len(PIECES)], rest[len(PIECES) :]
    chunk = piece_refs[0].shape[0]
    places = pack_places(me_ref[0])
    for piece, ref in zip(PIECES, piece_refs):
        pack_ref[pl.ds(pl.multiple_of(places[piece] * chunk, ROWS), chunk)] = ref[...]
    ranks = full_ref.shape[1]
    groups = ranks // LANES
    place = 0
    for i in range(groups):
        for j in range(i, groups):
            block = pack_ref[place * LANES : (place + 1) * LANES]
            for row, lane, part in ((i, j, block), (j, i, block.T))[: 1 if i == j else 2]:
                lanes = slice(lane * LANES, (lane + 1) * LANES)
                high, low = split(part)
                full_ref[row * LANES : (row + 1) * LANES, lanes] = high
                full_ref[ranks + row * LANES : ranks + (row + 1) * LANES, lanes] = low
            place += 1
    projection = pack_ref[place * LANES : (place + groups) * LANES]
    crossed = quarters(dot(full_ref[...], jnp.concatenate(split(projection), axis=1)))
    crossed_high, crossed_low = split(crossed)
    turned = jnp.concatenate(
        [projection[i * LANES : (i + 1) * LANES].T for i in range(groups)], axis=1
    )
    turned_stack = jnp.concatenate(split(turned), axis=0)
    gram = quarters(dot(turned_stack, jnp.concatenate([crossed_high, crossed_low], axis=1)))
    projected_high, projected_low = split(thrice(turned_stack, stack_ref[:ranks], stack_ref[ranks:], dot))
    inverse_stack = jnp.concatenate(split(inverse_factor(gram)), axis=0)
    root = total_users ** 0.5
    scaled = thrice(inverse_stack, projected_high, projected_low, dot) * root
    for i in range(scaled.shape[1] // LANES):
        basis_ref[i * LANES : (i + 1) * LANES] = scaled[:, i * LANES : (i + 1) * LANES].T
    core_out_ref[...] = thrice(inverse_stack, crossed_high, crossed_low, dot_nt) * (1.0 / root)


def finish(me, stack, pieces, devices):
    ranks, users = stack.shape[0] // 2, stack.shape[1]
    return pl.pallas_call(
        functools.partial(finish_kernel, users * devices),
        out_shape=(
            jax.ShapeDtypeStruct((users, LANES), jnp.float32),
            jax.ShapeDtypeStruct((LANES, ranks), jnp.float32),
        ),
        in_specs=[SMEM] + [VMEM] * (1 + len(PIECES)),
        out_specs=(VMEM, VMEM),
        scratch_shapes=[
            pltpu.VMEM((pack_rows(ranks), LANES), jnp.float32),
            pltpu.VMEM((2 * ranks, ranks), jnp.bfloat16),
        ],
        compiler_params=limit(16),
        name="finish",
    )(me, stack, *[pieces[piece] for piece in PIECES])


def swap(value, mask, devices):
    return lax.ppermute(value, "users", [(i, i ^ mask) for i in range(devices)])


def reduce_pieces(pieces, devices):
    got = {plane: swap(pieces[1, plane], 1, devices) for plane in (3, 1, 2, 0)}
    total = pieces[0, 0] + got[0]
    for plane in (3, 1, 2):
        total = total + swap(pieces[0, plane] + got[plane], 2 * plane, devices)
    mask = CHUNKS
    while mask < devices:
        total = total + swap(total, mask, devices)
        mask *= 2
    return total


def spread_pieces(total, devices):
    pieces = {(0, 0): total}
    for plane in (3, 1, 2):
        pieces[0, plane] = swap(total, 2 * plane, devices)
    for plane in (0, 3, 1, 2):
        pieces[1, plane] = swap(pieces[0, plane], 1, devices)
    return pieces


def body(
    tile_owner, tile_slot, tile_cblock, tile_context, tile_weights,
    item_factors, context_factors, user_basis, user_counts,
):
    devices = lax.axis_size("users")
    half = devices // 2
    rank_c = context_factors.shape[0]
    me = lax.axis_index("users").astype(jnp.int32).reshape(1)

    mirror = swap(item_factors, half, devices)
    requests, where, own = route(me, tile_owner[:, 0], tile_slot, item_factors, half)
    sides = [list(range(half)), list(range(half, devices))]
    asked = lax.all_to_all(requests, "users", 0, 0, axis_index_groups=sides, tiled=True)
    found = collect(asked, own, mirror)
    found, cblock, factors = lax.optimization_barrier((found, tile_cblock, context_factors))
    blocks = lax.all_to_all(found, "users", 0, 0, axis_index_groups=sides, tiled=True)

    table = factors.astype(jnp.float32).reshape(rank_c, -1, CB).transpose(1, 0, 2)
    contexts = context_values(cblock, table, tile_context)
    pieces, stack = tile_sums(
        where, user_counts, me, blocks, tile_weights, contexts, user_basis
    )
    pieces = spread_pieces(reduce_pieces(pieces, devices), devices)
    return finish(me, stack, pieces, devices)


def solution(mesh):
    return jax.shard_map(
        body,
        mesh=mesh,
        in_specs=(
            P("users", None), P("users"), P("users"), P("users", None), P("users", None, None),
            P("users", None, None), P(), P("users", None), P("users"),
        ),
        out_specs=(P("users", None), P()),
        check_vma=False,
    )
```

```python
import functools

import jax
import jax.numpy as jnp
from jax import lax
from jax.experimental import pallas as pl
from jax.experimental.pallas import tpu as pltpu
from jax.sharding import PartitionSpec as P

CB = 8
SLOTS = 2
PLACES = 2 * SLOTS
LANES = 128
ROWS = 8
BATCH = 8
CHUNKS = 8
MIB = 2**20

SMEM = pl.BlockSpec(memory_space=pltpu.SMEM)
VMEM = pl.BlockSpec(memory_space=pltpu.VMEM)
ANY = pl.BlockSpec(memory_space=pl.ANY)


def in_hbm(value):
    return pltpu.with_memory_space_constraint(value, pltpu.HBM)


def limit(mib):
    return pltpu.CompilerParams(vmem_limit_bytes=mib * MIB)


def dot(lhs, rhs):
    return jnp.dot(lhs, rhs, preferred_element_type=jnp.float32)


def dot_nt(lhs, rhs):
    return lax.dot_general(lhs, rhs, (((1,), (1,)), ((), ())), preferred_element_type=jnp.float32)


def split(value):
    high = value.astype(jnp.bfloat16)
    return high, (value - high.astype(jnp.float32)).astype(jnp.bfloat16)


def quarters(value):
    rows, lanes = value.shape[0] // 2, value.shape[1] // 2
    return (value[:rows, :lanes] + value[:rows, lanes:]) + (value[rows:, :lanes] + value[rows:, lanes:])


def thrice(stack, high, low, product):
    rows = stack.shape[0] // 2
    first = product(stack, high)
    return first[:rows] + (first[rows:] + product(stack[:rows], low))


def route_kernel(half, me_ref, owner_ref, slot_ref, own_ref, request_ref, where_ref, held_ref, used_ref, sem_ref):
    copy = pltpu.make_async_copy(own_ref, held_ref, sem_ref)
    copy.start()
    side = me_ref[0] // half
    lane = lax.broadcasted_iota(jnp.int32, (1, LANES), 1)

    def clear(place, _):
        used_ref[place] = 0
        return 0

    lax.fori_loop(0, 2 * half, clear, 0, unroll=8)
    request_ref[...] = jnp.zeros_like(request_ref)

    def assign(tile, _):
        owner = owner_ref[tile]
        taken = used_ref[owner]
        used_ref[owner] = taken + 1
        low = lax.rem(owner, half)
        place = jnp.where(owner // half == side, 0, SLOTS) + taken
        request_ref[low] = jnp.where(lane == place, slot_ref[tile], request_ref[low])
        where_ref[tile] = low * PLACES + place
        return 0

    lax.fori_loop(0, owner_ref.shape[0], assign, 0, unroll=4)
    copy.wait()


def route(me, owners, slots, own, half):
    return pl.pallas_call(
        functools.partial(route_kernel, half),
        out_shape=(
            jax.ShapeDtypeStruct((half, 1, LANES), jnp.int32),
            jax.ShapeDtypeStruct(owners.shape, jnp.int32),
            jax.ShapeDtypeStruct(own.shape, own.dtype),
        ),
        in_specs=[SMEM, SMEM, SMEM, ANY],
        out_specs=(VMEM, SMEM, VMEM),
        scratch_shapes=[pltpu.SMEM((2 * half,), jnp.int32), pltpu.SemaphoreType.DMA],
        compiler_params=limit(4),
        name="route",
    )(me, in_hbm(owners), in_hbm(slots), in_hbm(own))


def collect_kernel(asked_ref, own_ref, mirror_ref, out_ref):
    for peer in range(asked_ref.shape[0]):
        for place in range(PLACES):
            source = own_ref if place < SLOTS else mirror_ref
            out_ref[peer * PLACES + place] = source[asked_ref[peer, 0, place]]


def collect(asked, own, mirror):
    return pl.pallas_call(
        collect_kernel,
        out_shape=jax.ShapeDtypeStruct((asked.shape[0] * PLACES,) + own.shape[1:], own.dtype),
        in_specs=[SMEM, VMEM, VMEM],
        out_specs=VMEM,
        compiler_params=limit(4),
        name="collect",
    )(asked, own, mirror)


def context_kernel(cblock_ref, table_ref, marks_ref, context_ref):
    tiles, users = marks_ref.shape

    def one(tile, _):
        table = table_ref[cblock_ref[tile]]
        marks = jnp.broadcast_to(marks_ref[pl.ds(tile, 1), :], (ROWS, users))
        total = jnp.zeros((ROWS, users), jnp.float32)
        for k in range(CB):
            column = jnp.broadcast_to(table[:, k : k + 1], (ROWS, users))
            total = jnp.where(marks == k, column, total)
        context_ref[tile] = total
        return 0

    lax.fori_loop(0, tiles, one, 0, unroll=2)


def context_values(cblock, table, marks):
    tiles, users = marks.shape
    return pl.pallas_call(
        context_kernel,
        out_shape=jax.ShapeDtypeStruct((tiles, ROWS, users), jnp.float32),
        in_specs=[SMEM, VMEM, VMEM],
        out_specs=VMEM,
        compiler_params=limit(4),
        cost_estimate=pl.CostEstimate(flops=10**7, bytes_accessed=2 * 10**7, transcendentals=0),
        name="contexts",
    )(in_hbm(cblock), table, marks)


def pack_places(me):
    return {
        (core, plane): jnp.bitwise_xor(lax.rem(me, CHUNKS), core + 2 * plane)
        for core in range(2)
        for plane in range(4)
    }


PIECES = [(core, plane) for core in (1, 0) for plane in (3, 1, 2, 0)]


def pack_rows(ranks):
    groups = ranks // LANES
    return (groups * (groups + 1) // 2 + groups) * LANES


def tiles_kernel(
    where_ref, count_ref, me_ref, blocks_ref, weights_ref, context_ref, basis_ref, *refs
):
    piece_refs, refs = refs[: len(PIECES)], refs[len(PIECES) :]
    stack_ref, y_ref, square_ref, pack_ref, product_ref = refs[:5]
    weights_held, context_held, basis_held, weights_sem, context_sem, basis_sem = refs[5:]
    rank_c, rank_i, users = y_ref.shape
    batches = weights_ref.shape[0] // BATCH
    half = rank_c // 2

    def weights_copy(batch):
        rows = pl.ds(batch * BATCH, BATCH)
        return pltpu.make_async_copy(weights_ref.at[rows], weights_held.at[rows], weights_sem.at[batch])

    weights_copy(0).start()
    contexts_copy = pltpu.make_async_copy(context_ref, context_held, context_sem)
    contexts_copy.start()
    for batch in range(1, batches):
        weights_copy(batch).start()
    basis_copy = pltpu.make_async_copy(basis_ref, basis_held, basis_sem)
    basis_copy.start()

    def multiply(tile):
        product = dot(blocks_ref[where_ref[tile]], weights_held[tile])
        return product.astype(jnp.bfloat16).astype(jnp.float32)

    def add(batch, bank, lanes, ranks):
        strips = [slice(i, i + ROWS) for i in range(0, rank_i, ROWS)]
        totals = [[y_ref[r, strip, lanes] for strip in strips] for r in ranks]
        for place in range(BATCH):
            parts_of = [product_ref[bank, place, strip, lanes] for strip in strips]
            for i, r in enumerate(ranks):
                values = context_held[batch * BATCH + place, r : r + 1, lanes]
                values = jnp.broadcast_to(values, (ROWS, LANES))
                for j in range(len(strips)):
                    totals[i][j] = totals[i][j] + values * parts_of[j]
        for i, r in enumerate(ranks):
            for strip, total in zip(strips, totals[i]):
                y_ref[r, strip, lanes] = total

    y_ref[...] = jnp.zeros_like(y_ref)
    weights_copy(0).wait()

    def first(place, _):
        product_ref[0, place] = multiply(place)
        return 0

    lax.fori_loop(0, BATCH, first, 0, unroll=2)
    contexts_copy.wait()
    turns = users // LANES
    share = BATCH // turns

    def turn(index, _):
        batch, lane = index // turns, lax.rem(index, turns)
        bank = lax.rem(batch, 2)

        @pl.when(jnp.logical_and(lane == 0, batch + 1 < batches))
        def _():
            weights_copy(batch + 1).wait()

        start = jnp.minimum(batch + 1, batches - 1) * BATCH + lane * share
        products = [multiply(start + i) for i in range(share)]
        lanes = pl.ds(pl.multiple_of(lane * LANES, LANES), LANES)
        add(batch, bank, lanes, range(half))
        add(batch, bank, lanes, range(half, rank_c))
        for i in range(share):
            product_ref[1 - bank, lane * share + i] = products[i]
        return 0

    lax.fori_loop(0, batches * turns, turn, 0)

    living = lax.broadcasted_iota(jnp.int32, (rank_i, users), 1) < count_ref[0]
    ranks = rank_c * rank_i
    for r in range(rank_c):
        high, low = split(jnp.where(living, y_ref[r], 0.0))
        stack_ref[r * rank_i : (r + 1) * rank_i] = high
        stack_ref[ranks + r * rank_i : ranks + (r + 1) * rank_i] = low
    square_ref[...] = dot_nt(stack_ref[...], stack_ref[:ranks])
    basis_copy.wait()
    projection = dot(stack_ref[...], jnp.concatenate(split(basis_held[...]), axis=1))
    groups = ranks // LANES
    place = 0
    for i in range(groups):
        rows = slice(i * LANES, (i + 1) * LANES)
        low_rows = slice(ranks + i * LANES, ranks + (i + 1) * LANES)
        for j in range(i, groups):
            lanes = slice(j * LANES, (j + 1) * LANES)
            low_lanes = slice(ranks + j * LANES, ranks + (j + 1) * LANES)
            block = square_ref[rows, lanes] + square_ref[low_rows, lanes] + square_ref[low_lanes, rows].T
            pack_ref[place * LANES : (place + 1) * LANES] = block
            place += 1
    pack_ref[place * LANES : (place + groups) * LANES] = quarters(projection)
    chunk = piece_refs[0].shape[0]
    places = pack_places(me_ref[0])
    for piece, ref in zip(PIECES, piece_refs):
        ref[...] = pack_ref[pl.ds(pl.multiple_of(places[piece] * chunk, ROWS), chunk)]


def tile_sums(where, count, me, blocks, weights, contexts, user_basis):
    tiles, _, users = weights.shape
    rank_i = blocks.shape[1]
    rank_c = contexts.shape[1]
    ranks = rank_c * rank_i
    rows = pack_rows(ranks)
    out_shape = (jax.ShapeDtypeStruct((rows // CHUNKS, LANES), jnp.float32),) * len(PIECES)
    out_shape += (jax.ShapeDtypeStruct((2 * ranks, users), jnp.bfloat16),)
    held = 3 * weights.size * 2 // (2 * MIB)
    out = pl.pallas_call(
        tiles_kernel,
        out_shape=out_shape,
        in_specs=[SMEM] * 3 + [VMEM] + [ANY] * 3,
        out_specs=(VMEM,) * len(out_shape),
        scratch_shapes=[
            pltpu.VMEM((rank_c, rank_i, users), jnp.float32),
            pltpu.VMEM((2 * ranks, ranks), jnp.float32),
            pltpu.VMEM((rows, LANES), jnp.float32),
            pltpu.VMEM((2, BATCH, rank_i, users), jnp.float32),
            pltpu.VMEM(weights.shape, weights.dtype),
            pltpu.VMEM(contexts.shape, contexts.dtype),
            pltpu.VMEM(user_basis.shape, user_basis.dtype),
            pltpu.SemaphoreType.DMA((tiles // BATCH,)),
            pltpu.SemaphoreType.DMA,
            pltpu.SemaphoreType.DMA,
        ],
        compiler_params=limit(12 + held),
        cost_estimate=pl.CostEstimate(flops=2 * 10**9, bytes_accessed=12 * 10**6, transcendentals=0),
        name="tile_sums",
    )(where, count, me, blocks, in_hbm(weights), in_hbm(contexts), in_hbm(user_basis))
    return dict(zip(PIECES, out[:-1])), out[-1]


def inverse_factor(left_ref, right_ref, out_ref):
    order = left_ref.shape[0]
    panels = order // ROWS
    sub = lax.broadcasted_iota(jnp.int32, (ROWS, order), 0)
    lane = lax.broadcasted_iota(jnp.int32, (ROWS, order), 1)
    for i in range(panels):
        right_ref[ROWS * i : ROWS * (i + 1)] = jnp.where(lane == sub + ROWS * i, 1.0, 0.0)
    spread = lambda value, j: jnp.broadcast_to(value[j : j + 1], (ROWS, order))

    def panel(stage, live, step, _):
        blocks = [slice(ROWS * i, ROWS * (i + 1)) for i in range(live)]
        row, tail = left_ref[blocks[0]], right_ref[blocks[0]]
        columns = []
        for block in blocks:
            value = left_ref[block]
            columns.append([jnp.broadcast_to(value[:, j : j + 1], (ROWS, order)) for j in range(ROWS)])
        scale = jnp.ones((ROWS, order), jnp.float32)
        rows, tails, facts = [], [], [[] for _ in range(live)]
        for j in range(ROWS):
            head = columns[0][j]
            pivot = spread(head, j)
            inverse = pl.reciprocal(pivot, approx=True)
            inverse = inverse * (2.0 - pivot * inverse)
            scale = jnp.where(sub == j, pivot, scale)
            rows.append(spread(row, j))
            tails.append(spread(tail, j))
            below = jnp.where(sub > j, head, 0.0) * inverse
            row = row - below * rows[j]
            tail = tail - below * tails[j]
            crossings = {c: spread(head, c) for c in range(j + 1, ROWS)}
            for i in range(live):
                facts[i].append(columns[i][j] * inverse if i else below)
                for c in range(j + 1, ROWS):
                    columns[i][c] = columns[i][c] - facts[i][j] * crossings[c]
        out_ref[pl.ds(pl.multiple_of((stage + step) * ROWS, ROWS), ROWS)] = tail * lax.rsqrt(scale)
        for i in range(1, live):
            left, right = left_ref[blocks[i]], right_ref[blocks[i]]
            for j in range(ROWS):
                left = left - facts[i][j] * rows[j]
                right = right - facts[i][j] * tails[j]
            left_ref[blocks[i - 1]] = pltpu.roll(left, order - ROWS, 1)
            right_ref[blocks[i - 1]] = right
        left_ref[blocks[-1]] = jnp.zeros((ROWS, order), jnp.float32)
        right_ref[blocks[-1]] = jnp.zeros((ROWS, order), jnp.float32)
        return 0

    steps = 4
    for stage in range(0, panels, steps):
        lax.fori_loop(0, steps, functools.partial(panel, stage, panels - stage), 0)


def finish_kernel(total_users, me_ref, stack_ref, *rest):
    piece_refs, rest = rest[: len(PIECES)], rest[len(PIECES) :]
    basis_ref, core_out_ref, pack_ref, full_ref, left_ref, right_ref, inverse_ref = rest
    chunk = piece_refs[0].shape[0]
    places = pack_places(me_ref[0])
    for piece, ref in zip(PIECES, piece_refs):
        pack_ref[pl.ds(pl.multiple_of(places[piece] * chunk, ROWS), chunk)] = ref[...]
    ranks = full_ref.shape[1]
    groups = ranks // LANES
    place = 0
    for i in range(groups):
        for j in range(i, groups):
            block = pack_ref[place * LANES : (place + 1) * LANES]
            for row, lane, part in ((i, j, block), (j, i, block.T))[: 1 if i == j else 2]:
                lanes = slice(lane * LANES, (lane + 1) * LANES)
                high, low = split(part)
                full_ref[row * LANES : (row + 1) * LANES, lanes] = high
                full_ref[ranks + row * LANES : ranks + (row + 1) * LANES, lanes] = low
            place += 1
    projection = pack_ref[place * LANES : (place + groups) * LANES]
    crossed = quarters(dot(full_ref[...], jnp.concatenate(split(projection), axis=1)))
    crossed_high, crossed_low = split(crossed)
    turned = jnp.concatenate(
        [projection[i * LANES : (i + 1) * LANES].T for i in range(groups)], axis=1
    )
    turned_stack = jnp.concatenate(split(turned), axis=0)
    left_ref[...] = quarters(dot(turned_stack, jnp.concatenate([crossed_high, crossed_low], axis=1)))
    projected_high, projected_low = split(thrice(turned_stack, stack_ref[:ranks], stack_ref[ranks:], dot))
    inverse_factor(left_ref, right_ref, inverse_ref)
    inverse_stack = jnp.concatenate(split(inverse_ref[...]), axis=0)
    root = total_users ** 0.5
    scaled = thrice(inverse_stack, projected_high, projected_low, dot) * root
    for i in range(scaled.shape[1] // LANES):
        basis_ref[i * LANES : (i + 1) * LANES] = scaled[:, i * LANES : (i + 1) * LANES].T
    core_out_ref[...] = thrice(inverse_stack, crossed_high, crossed_low, dot_nt) * (1.0 / root)


def finish(me, stack, pieces, devices):
    ranks, users = stack.shape[0] // 2, stack.shape[1]
    return pl.pallas_call(
        functools.partial(finish_kernel, users * devices),
        out_shape=(
            jax.ShapeDtypeStruct((users, LANES), jnp.float32),
            jax.ShapeDtypeStruct((LANES, ranks), jnp.float32),
        ),
        in_specs=[SMEM] + [VMEM] * (1 + len(PIECES)),
        out_specs=(VMEM, VMEM),
        scratch_shapes=[
            pltpu.VMEM((pack_rows(ranks), LANES), jnp.float32),
            pltpu.VMEM((2 * ranks, ranks), jnp.bfloat16),
        ]
        + [pltpu.VMEM((LANES, LANES), jnp.float32)] * 3,
        compiler_params=limit(16),
        name="finish",
    )(me, stack, *[pieces[piece] for piece in PIECES])


def swap(value, mask, devices):
    return lax.ppermute(value, "users", [(i, i ^ mask) for i in range(devices)])


def reduce_pieces(pieces, devices):
    got = {plane: swap(pieces[1, plane], 1, devices) for plane in (3, 1, 2, 0)}
    total = pieces[0, 0] + got[0]
    for plane in (3, 1, 2):
        total = total + swap(pieces[0, plane] + got[plane], 2 * plane, devices)
    mask = CHUNKS
    while mask < devices:
        total = total + swap(total, mask, devices)
        mask *= 2
    return total


def spread_pieces(total, devices):
    pieces = {(0, 0): total}
    for plane in (3, 1, 2):
        pieces[0, plane] = swap(total, 2 * plane, devices)
    for plane in (0, 3, 1, 2):
        pieces[1, plane] = swap(pieces[0, plane], 1, devices)
    return pieces


def body(
    tile_owner, tile_slot, tile_cblock, tile_context, tile_weights,
    item_factors, context_factors, user_basis, user_counts,
):
    devices = lax.axis_size("users")
    half = devices // 2
    rank_c = context_factors.shape[0]
    me = lax.axis_index("users").astype(jnp.int32).reshape(1)

    mirror = swap(item_factors, half, devices)
    requests, where, own = route(me, tile_owner[:, 0], tile_slot, item_factors, half)
    sides = [list(range(half)), list(range(half, devices))]
    asked = lax.all_to_all(requests, "users", 0, 0, axis_index_groups=sides, tiled=True)
    found = collect(asked, own, mirror)
    found, cblock, factors = lax.optimization_barrier((found, tile_cblock, context_factors))
    blocks = lax.all_to_all(found, "users", 0, 0, axis_index_groups=sides, tiled=True)

    table = factors.astype(jnp.float32).reshape(rank_c, -1, CB).transpose(1, 0, 2)
    contexts = context_values(cblock, table, tile_context)
    pieces, stack = tile_sums(
        where, user_counts, me, blocks, tile_weights, contexts, user_basis
    )
    pieces = spread_pieces(reduce_pieces(pieces, devices), devices)
    return finish(me, stack, pieces, devices)


def solution(mesh):
    return jax.shard_map(
        body,
        mesh=mesh,
        in_specs=(
            P("users", None), P("users"), P("users"), P("users", None), P("users", None, None),
            P("users", None, None), P(), P("users", None), P("users"),
        ),
        out_specs=(P("users", None), P()),
        check_vma=False,
    )
```

```python
import functools

import jax
import jax.numpy as jnp
from jax import lax
from jax.experimental import pallas as pl
from jax.experimental.pallas import tpu as pltpu
from jax.sharding import PartitionSpec as P

CB = 8
SLOTS = 2
LANES = 128
ROWS = 8
BATCH = 8
CHUNKS = 8
MIB = 2**20

SMEM = pl.BlockSpec(memory_space=pltpu.SMEM)
VMEM = pl.BlockSpec(memory_space=pltpu.VMEM)
ANY = pl.BlockSpec(memory_space=pl.ANY)


def in_hbm(value):
    return pltpu.with_memory_space_constraint(value, pltpu.HBM)


def limit(mib):
    return pltpu.CompilerParams(vmem_limit_bytes=mib * MIB)


def dot(lhs, rhs):
    return jnp.dot(lhs, rhs, preferred_element_type=jnp.float32)


def dot_nt(lhs, rhs):
    return lax.dot_general(lhs, rhs, (((1,), (1,)), ((), ())), preferred_element_type=jnp.float32)


def split(value):
    high = value.astype(jnp.bfloat16)
    return high, (value - high.astype(jnp.float32)).astype(jnp.bfloat16)


def quarters(value):
    rows, lanes = value.shape[0] // 2, value.shape[1] // 2
    return (value[:rows, :lanes] + value[:rows, lanes:]) + (value[rows:, :lanes] + value[rows:, lanes:])


def thrice(stack, high, low, product):
    rows = stack.shape[0] // 2
    first = product(stack, high)
    return first[:rows] + (first[rows:] + product(stack[:rows], low))


def route_kernel(half, me_ref, owner_ref, slot_ref, own_ref, request_ref, tile_ref, held_ref, used_ref, sem_ref):
    copy = pltpu.make_async_copy(own_ref, held_ref, sem_ref)
    copy.start()
    side = me_ref[0] // half
    lane = lax.broadcasted_iota(jnp.int32, (1, LANES), 1)

    def clear(place, _):
        used_ref[place] = 0
        for slot in range(SLOTS):
            tile_ref[place * SLOTS + slot] = -1
        return 0

    lax.fori_loop(0, 2 * half, clear, 0, unroll=8)
    request_ref[...] = jnp.zeros_like(request_ref)

    def assign(tile, _):
        owner = owner_ref[tile]
        taken = used_ref[owner]
        used_ref[owner] = taken + 1
        low = lax.rem(owner, half)
        mirrored = jnp.where(owner // half == side, 0, 1)
        request_ref[low] = jnp.where(lane == mirrored * SLOTS + taken, slot_ref[tile], request_ref[low])
        tile_ref[(mirrored * half + low) * SLOTS + taken] = tile
        return 0

    lax.fori_loop(0, owner_ref.shape[0], assign, 0, unroll=4)
    copy.wait()


def route(me, owners, slots, own, half):
    return pl.pallas_call(
        functools.partial(route_kernel, half),
        out_shape=(
            jax.ShapeDtypeStruct((half, 1, LANES), jnp.int32),
            jax.ShapeDtypeStruct((2 * half * SLOTS,), jnp.int32),
            jax.ShapeDtypeStruct(own.shape, own.dtype),
        ),
        in_specs=[SMEM, SMEM, SMEM, ANY],
        out_specs=(VMEM, SMEM, VMEM),
        scratch_shapes=[pltpu.SMEM((2 * half,), jnp.int32), pltpu.SemaphoreType.DMA],
        compiler_params=limit(4),
        name="route",
    )(me, in_hbm(owners), in_hbm(slots), in_hbm(own))


def collect_kernel(lane, asked_ref, source_ref, out_ref):
    for peer in range(asked_ref.shape[0]):
        for slot in range(SLOTS):
            out_ref[peer * SLOTS + slot] = source_ref[asked_ref[peer, 0, lane + slot]]


def collect(lane, asked, source):
    return pl.pallas_call(
        functools.partial(collect_kernel, lane),
        out_shape=jax.ShapeDtypeStruct((asked.shape[0] * SLOTS,) + source.shape[1:], source.dtype),
        in_specs=[SMEM, VMEM],
        out_specs=VMEM,
        compiler_params=limit(4),
        name="collect",
    )(asked, source)


def context_kernel(tile_ref, cblock_ref, table_ref, marks_ref, context_ref):
    users = marks_ref.shape[1]

    def one(slot, _):
        tile = jnp.maximum(tile_ref[slot], 0)
        table = jnp.where(tile_ref[slot] >= 0, table_ref[cblock_ref[tile]], 0.0)
        marks = jnp.broadcast_to(marks_ref[pl.ds(tile, 1), :], (ROWS, users))
        total = jnp.zeros((ROWS, users), jnp.float32)
        for k in range(CB):
            column = jnp.broadcast_to(table[:, k : k + 1], (ROWS, users))
            total = jnp.where(marks == k, column, total)
        context_ref[slot] = total
        return 0

    lax.fori_loop(0, tile_ref.shape[0], one, 0, unroll=2)


def context_values(tile_of, cblock, table, marks):
    return pl.pallas_call(
        context_kernel,
        out_shape=jax.ShapeDtypeStruct((tile_of.shape[0], ROWS, marks.shape[1]), jnp.float32),
        in_specs=[SMEM, SMEM, VMEM, VMEM],
        out_specs=VMEM,
        compiler_params=limit(8),
        cost_estimate=pl.CostEstimate(flops=10**7, bytes_accessed=2 * 10**7, transcendentals=0),
        name="contexts",
    )(tile_of, in_hbm(cblock), table, marks)


def pack_places(me):
    return {
        (core, plane): jnp.bitwise_xor(lax.rem(me, CHUNKS), core + 2 * plane)
        for core in range(2)
        for plane in range(4)
    }


PIECES = [(core, plane) for core in (1, 0) for plane in (3, 1, 2, 0)]


def pack_rows(ranks):
    groups = ranks // LANES
    return (groups * (groups + 1) // 2 + groups) * LANES


def tiles_kernel(side, tile_ref, count_ref, me_ref, blocks_ref, weights_ref, context_ref, basis_ref, *refs):
    if side:
        before_ref, refs = refs[0], refs[1:]
        piece_refs, refs = refs[: len(PIECES)], refs[len(PIECES) :]
        stack_ref, square_ref, pack_ref, basis_held, basis_sem, *refs = refs
    y_ref, even_ref, odd_ref, weights_held, context_held, weights_sem, context_sem = refs
    rank_c, rank_i, users = y_ref.shape
    places = blocks_ref.shape[0]
    batches = places // BATCH
    half = rank_c // 2

    def weights_copy(place):
        tile = jnp.maximum(tile_ref[side * places + place], 0)
        return pltpu.make_async_copy(weights_ref.at[tile], weights_held.at[place], weights_sem.at[place])

    def start(place, _):
        weights_copy(place).start()
        return 0

    lax.fori_loop(0, BATCH, start, 0)
    contexts_copy = pltpu.make_async_copy(
        context_ref.at[pl.ds(side * places, places)], context_held, context_sem
    )
    contexts_copy.start()
    lax.fori_loop(BATCH, places, start, 0)
    if side:
        basis_copy = pltpu.make_async_copy(basis_ref, basis_held, basis_sem)
        basis_copy.start()

    def multiply(batch, place, into_ref):
        tile = batch * BATCH + place
        product = dot(blocks_ref[tile], weights_held[tile])
        into_ref[place] = product.astype(jnp.bfloat16).astype(jnp.float32)

    def add(batch, part, from_ref):
        lanes = slice(part // 2 * LANES, (part // 2 + 1) * LANES)
        ranks = range(part % 2 * half, (part % 2 + 1) * half)
        strips = [slice(i, i + ROWS) for i in range(0, rank_i, ROWS)]
        totals = [[y_ref[r, strip, lanes] for strip in strips] for r in ranks]
        for place in range(BATCH):
            parts_of = [from_ref[place, strip, lanes] for strip in strips]
            for i, r in enumerate(ranks):
                values = context_held[batch * BATCH + place, r : r + 1, lanes]
                values = jnp.broadcast_to(values, (ROWS, LANES))
                for j in range(len(strips)):
                    totals[i][j] = totals[i][j] + values * parts_of[j]
        for i, r in enumerate(ranks):
            for strip, total in zip(strips, totals[i]):
                y_ref[r, strip, lanes] = total

    y_ref[...] = before_ref[...] if side else jnp.zeros_like(y_ref)
    parts = 2 * users // LANES
    for place in range(BATCH):
        weights_copy(place).wait()
    for place in range(BATCH):
        multiply(0, place, even_ref)
    contexts_copy.wait()

    def turn(batch, from_ref, into_ref):
        for place in range(BATCH):
            weights_copy((batch + 1) * BATCH + place).wait()
        for part in range(max(parts, BATCH)):
            if part < BATCH:
                multiply(batch + 1, part, into_ref)
            if part < parts:
                add(batch, part, from_ref)

    def pair(index, _):
        turn(2 * index, even_ref, odd_ref)
        turn(2 * index + 1, odd_ref, even_ref)
        return 0

    lax.fori_loop(0, batches // 2 - 1, pair, 0)
    turn(batches - 2, even_ref, odd_ref)
    for part in range(parts):
        add(batches - 1, part, odd_ref)
    if not side:
        return

    living = lax.broadcasted_iota(jnp.int32, (rank_i, users), 1) < count_ref[0]
    ranks = rank_c * rank_i
    for r in range(rank_c):
        high, low = split(jnp.where(living, y_ref[r], 0.0))
        stack_ref[r * rank_i : (r + 1) * rank_i] = high
        stack_ref[ranks + r * rank_i : ranks + (r + 1) * rank_i] = low
    square_ref[...] = dot_nt(stack_ref[...], stack_ref[:ranks])
    basis_copy.wait()
    projection = dot(stack_ref[...], jnp.concatenate(split(basis_held[...]), axis=1))
    groups = ranks // LANES
    place = 0
    for i in range(groups):
        rows = slice(i * LANES, (i + 1) * LANES)
        low_rows = slice(ranks + i * LANES, ranks + (i + 1) * LANES)
        for j in range(i, groups):
            lanes = slice(j * LANES, (j + 1) * LANES)
            low_lanes = slice(ranks + j * LANES, ranks + (j + 1) * LANES)
            block = square_ref[rows, lanes] + square_ref[low_rows, lanes] + square_ref[low_lanes, rows].T
            pack_ref[place * LANES : (place + 1) * LANES] = block
            place += 1
    pack_ref[place * LANES : (place + groups) * LANES] = quarters(projection)
    chunk = piece_refs[0].shape[0]
    places = pack_places(me_ref[0])
    for piece, ref in zip(PIECES, piece_refs):
        ref[...] = pack_ref[pl.ds(pl.multiple_of(places[piece] * chunk, ROWS), chunk)]


def tile_sums(side, tile_of, count, me, blocks, weights, contexts, user_basis, before=None):
    _, block_len, users = weights.shape
    places, rank_i = blocks.shape[:2]
    rank_c = contexts.shape[1]
    ranks = rank_c * rank_i
    rows = pack_rows(ranks)
    y = jax.ShapeDtypeStruct((rank_c, rank_i, users), jnp.float32)
    scratch = [
        pltpu.VMEM((BATCH, rank_i, users), jnp.float32),
        pltpu.VMEM((BATCH, rank_i, users), jnp.float32),
        pltpu.VMEM((places, block_len, users), weights.dtype),
        pltpu.VMEM((places,) + contexts.shape[1:], contexts.dtype),
        pltpu.SemaphoreType.DMA((places,)),
        pltpu.SemaphoreType.DMA,
    ]
    out_shape = (y,)
    operands = [tile_of, count, me, blocks, in_hbm(weights), in_hbm(contexts), in_hbm(user_basis)]
    in_specs = [SMEM] * 3 + [VMEM] + [ANY] * 3
    if side:
        operands.append(before)
        in_specs.append(VMEM)
        out_shape = (jax.ShapeDtypeStruct((rows // CHUNKS, LANES), jnp.float32),) * len(PIECES)
        out_shape += (jax.ShapeDtypeStruct((2 * ranks, users), jnp.bfloat16),)
        scratch = [
            pltpu.VMEM((2 * ranks, ranks), jnp.float32),
            pltpu.VMEM((rows, LANES), jnp.float32),
            pltpu.VMEM(user_basis.shape, user_basis.dtype),
            pltpu.SemaphoreType.DMA,
            pltpu.VMEM(y.shape, y.dtype),
        ] + scratch
    held = 3 * places * block_len * users // MIB
    out = pl.pallas_call(
        functools.partial(tiles_kernel, side),
        out_shape=out_shape,
        in_specs=in_specs,
        out_specs=(VMEM,) * len(out_shape),
        scratch_shapes=scratch,
        compiler_params=limit(12 + held),
        cost_estimate=pl.CostEstimate(flops=10**9, bytes_accessed=6 * 10**6, transcendentals=0),
        name="tile_sums",
    )(*operands)
    return (dict(zip(PIECES, out[:-1])), out[-1]) if side else out[0]


def inverse_factor(gram):
    order = gram.shape[0]
    panels = order // ROWS
    sub = lax.broadcasted_iota(jnp.int32, (ROWS, order), 0)
    lane = lax.broadcasted_iota(jnp.int32, (ROWS, order), 1)
    left = [gram[ROWS * i : ROWS * (i + 1)] for i in range(panels)]
    right = [jnp.where(lane == sub + ROWS * i, 1.0, 0.0) for i in range(panels)]
    for k in range(panels):
        columns = {
            i: [
                jnp.broadcast_to(left[i][:, ROWS * k + j : ROWS * k + j + 1], (ROWS, order))
                for j in range(ROWS)
            ]
            for i in range(k, panels)
        }
        row, tail = left[k], right[k]
        scale = jnp.zeros((ROWS, order), jnp.float32)
        rows, tails = [], []
        for j in range(ROWS):
            head = columns[k][j]
            pivot = jnp.broadcast_to(head[j : j + 1], (ROWS, order))
            inverse = pl.reciprocal(pivot, approx=True)
            inverse = inverse * (2.0 - pivot * inverse)
            scale = jnp.where(sub == j, pivot, scale)
            rows.append(jnp.broadcast_to(row[j : j + 1], (ROWS, order)))
            tails.append(jnp.broadcast_to(tail[j : j + 1], (ROWS, order)))
            below = jnp.where(sub > j, head, 0.0) * inverse
            row = row - below * rows[j]
            tail = tail - below * tails[j]
            facts = {k: below}
            for i in range(k + 1, panels):
                facts[i] = columns[i][j] * inverse
            for c in range(j + 1, ROWS):
                crossing = jnp.broadcast_to(head[c : c + 1], (ROWS, order))
                for i in range(k, panels):
                    columns[i][c] = columns[i][c] - facts[i] * crossing
            for i in range(k + 1, panels):
                left[i] = left[i] - facts[i] * rows[j]
                right[i] = right[i] - facts[i] * tails[j]
        right[k] = tail * lax.rsqrt(scale)
    return jnp.concatenate(right, axis=0)


def finish_kernel(total_users, me_ref, stack_ref, *rest):
    piece_refs, (basis_ref, core_out_ref, pack_ref, full_ref) = rest[: len(PIECES)], rest[len(PIECES) :]
    chunk = piece_refs[0].shape[0]
    places = pack_places(me_ref[0])
    for piece, ref in zip(PIECES, piece_refs):
        pack_ref[pl.ds(pl.multiple_of(places[piece] * chunk, ROWS), chunk)] = ref[...]
    ranks = full_ref.shape[1]
    groups = ranks // LANES
    place = 0
    for i in range(groups):
        for j in range(i, groups):
            block = pack_ref[place * LANES : (place + 1) * LANES]
            for row, lane, part in ((i, j, block), (j, i, block.T))[: 1 if i == j else 2]:
                lanes = slice(lane * LANES, (lane + 1) * LANES)
                high, low = split(part)
                full_ref[row * LANES : (row + 1) * LANES, lanes] = high
                full_ref[ranks + row * LANES : ranks + (row + 1) * LANES, lanes] = low
            place += 1
    projection = pack_ref[place * LANES : (place + groups) * LANES]
    crossed = quarters(dot(full_ref[...], jnp.concatenate(split(projection), axis=1)))
    crossed_high, crossed_low = split(crossed)
    turned = jnp.concatenate(
        [projection[i * LANES : (i + 1) * LANES].T for i in range(groups)], axis=1
    )
    turned_stack = jnp.concatenate(split(turned), axis=0)
    gram = quarters(dot(turned_stack, jnp.concatenate([crossed_high, crossed_low], axis=1)))
    projected_high, projected_low = split(thrice(turned_stack, stack_ref[:ranks], stack_ref[ranks:], dot))
    inverse_stack = jnp.concatenate(split(inverse_factor(gram)), axis=0)
    root = total_users ** 0.5
    scaled = thrice(inverse_stack, projected_high, projected_low, dot) * root
    for i in range(scaled.shape[1] // LANES):
        basis_ref[i * LANES : (i + 1) * LANES] = scaled[:, i * LANES : (i + 1) * LANES].T
    core_out_ref[...] = thrice(inverse_stack, crossed_high, crossed_low, dot_nt) * (1.0 / root)


def finish(me, stack, pieces, devices):
    ranks, users = stack.shape[0] // 2, stack.shape[1]
    return pl.pallas_call(
        functools.partial(finish_kernel, users * devices),
        out_shape=(
            jax.ShapeDtypeStruct((users, LANES), jnp.float32),
            jax.ShapeDtypeStruct((LANES, ranks), jnp.float32),
        ),
        in_specs=[SMEM] + [VMEM] * (1 + len(PIECES)),
        out_specs=(VMEM, VMEM),
        scratch_shapes=[
            pltpu.VMEM((pack_rows(ranks), LANES), jnp.float32),
            pltpu.VMEM((2 * ranks, ranks), jnp.bfloat16),
        ],
        compiler_params=limit(16),
        name="finish",
    )(me, stack, *[pieces[piece] for piece in PIECES])


def swap(value, mask, devices):
    return lax.ppermute(value, "users", [(i, i ^ mask) for i in range(devices)])


def reduce_pieces(pieces, devices):
    got = {plane: swap(pieces[1, plane], 1, devices) for plane in (3, 1, 2, 0)}
    total = pieces[0, 0] + got[0]
    for plane in (3, 1, 2):
        total = total + swap(pieces[0, plane] + got[plane], 2 * plane, devices)
    mask = CHUNKS
    while mask < devices:
        total = total + swap(total, mask, devices)
        mask *= 2
    return total


def spread_pieces(total, devices):
    pieces = {(0, 0): total}
    for plane in (3, 1, 2):
        pieces[0, plane] = swap(total, 2 * plane, devices)
    for plane in (0, 3, 1, 2):
        pieces[1, plane] = swap(pieces[0, plane], 1, devices)
    return pieces


def body(
    tile_owner, tile_slot, tile_cblock, tile_context, tile_weights,
    item_factors, context_factors, user_basis, user_counts,
):
    devices = lax.axis_size("users")
    half = devices // 2
    rank_c = context_factors.shape[0]
    me = lax.axis_index("users").astype(jnp.int32).reshape(1)

    mirror = swap(item_factors, half, devices)
    requests, tile_of, own = route(me, tile_owner[:, 0], tile_slot, item_factors, half)
    sides = [list(range(half)), list(range(half, devices))]

    def exchange(value):
        return lax.all_to_all(value, "users", 0, 0, axis_index_groups=sides, tiled=True)

    asked = exchange(requests)
    found = collect(0, asked, own)
    found, cblock, factors = lax.optimization_barrier((found, tile_cblock, context_factors))
    near = exchange(found)
    far = exchange(collect(SLOTS, asked, mirror))

    table = factors.astype(jnp.float32).reshape(rank_c, -1, CB).transpose(1, 0, 2)
    contexts = context_values(tile_of, cblock, table, tile_context)
    shared = (tile_of, user_counts, me)
    before = tile_sums(0, *shared, near, tile_weights, contexts, user_basis)
    pieces, stack = tile_sums(1, *shared, far, tile_weights, contexts, user_basis, before)
    pieces = spread_pieces(reduce_pieces(pieces, devices), devices)
    return finish(me, stack, pieces, devices)


def solution(mesh):
    return jax.shard_map(
        body,
        mesh=mesh,
        in_specs=(
            P("users", None), P("users"), P("users"), P("users", None), P("users", None, None),
            P("users", None, None), P(), P("users", None), P("users"),
        ),
        out_specs=(P("users", None), P()),
        check_vma=False,
    )
```

```python
import functools

import jax
import jax.numpy as jnp
from jax import lax
from jax.experimental import pallas as pl
from jax.experimental.pallas import tpu as pltpu
from jax.sharding import PartitionSpec as P

CB = 8
SLOTS = 2
LANES = 128
ROWS = 8
BATCH = 8
CHUNKS = 8
MIB = 2**20

SMEM = pl.BlockSpec(memory_space=pltpu.SMEM)
VMEM = pl.BlockSpec(memory_space=pltpu.VMEM)
ANY = pl.BlockSpec(memory_space=pl.ANY)


def in_hbm(value):
    return pltpu.with_memory_space_constraint(value, pltpu.HBM)


def limit(mib):
    return pltpu.CompilerParams(vmem_limit_bytes=mib * MIB)


def dot(lhs, rhs):
    return jnp.dot(lhs, rhs, preferred_element_type=jnp.float32)


def dot_nt(lhs, rhs):
    return lax.dot_general(lhs, rhs, (((1,), (1,)), ((), ())), preferred_element_type=jnp.float32)


def split(value):
    high = value.astype(jnp.bfloat16)
    return high, (value - high.astype(jnp.float32)).astype(jnp.bfloat16)


def quarters(value):
    rows, lanes = value.shape[0] // 2, value.shape[1] // 2
    return (value[:rows, :lanes] + value[:rows, lanes:]) + (value[rows:, :lanes] + value[rows:, lanes:])


def thrice(stack, high, low, product):
    rows = stack.shape[0] // 2
    first = product(stack, high)
    return first[:rows] + (first[rows:] + product(stack[:rows], low))


def route_kernel(half, me_ref, owner_ref, slot_ref, own_ref, request_ref, tile_ref, held_ref, used_ref, sem_ref):
    copy = pltpu.make_async_copy(own_ref, held_ref, sem_ref)
    copy.start()
    side = me_ref[0] // half
    lane = lax.broadcasted_iota(jnp.int32, (1, LANES), 1)

    def clear(place, _):
        used_ref[place] = 0
        for slot in range(SLOTS):
            tile_ref[place * SLOTS + slot] = -1
        return 0

    lax.fori_loop(0, 2 * half, clear, 0, unroll=8)
    request_ref[...] = jnp.zeros_like(request_ref)

    def assign(tile, _):
        owner = owner_ref[tile]
        taken = used_ref[owner]
        used_ref[owner] = taken + 1
        low = lax.rem(owner, half)
        mirrored = jnp.where(owner // half == side, 0, 1)
        request_ref[low] = jnp.where(lane == mirrored * SLOTS + taken, slot_ref[tile], request_ref[low])
        tile_ref[(mirrored * half + low) * SLOTS + taken] = tile
        return 0

    lax.fori_loop(0, owner_ref.shape[0], assign, 0, unroll=4)
    copy.wait()


def route(me, owners, slots, own, half):
    return pl.pallas_call(
        functools.partial(route_kernel, half),
        out_shape=(
            jax.ShapeDtypeStruct((half, 1, LANES), jnp.int32),
            jax.ShapeDtypeStruct((2 * half * SLOTS,), jnp.int32),
            jax.ShapeDtypeStruct(own.shape, own.dtype),
        ),
        in_specs=[SMEM, SMEM, SMEM, ANY],
        out_specs=(VMEM, SMEM, VMEM),
        scratch_shapes=[pltpu.SMEM((2 * half,), jnp.int32), pltpu.SemaphoreType.DMA],
        compiler_params=limit(4),
        name="route",
    )(me, in_hbm(owners), in_hbm(slots), in_hbm(own))


def collect_kernel(asked_ref, own_ref, mirror_ref, near_ref, far_ref):
    for peer in range(asked_ref.shape[0]):
        for slot in range(SLOTS):
            near_ref[peer * SLOTS + slot] = own_ref[asked_ref[peer, 0, slot]]
            far_ref[peer * SLOTS + slot] = mirror_ref[asked_ref[peer, 0, SLOTS + slot]]


def collect(asked, own, mirror):
    return pl.pallas_call(
        collect_kernel,
        out_shape=(jax.ShapeDtypeStruct((asked.shape[0] * SLOTS,) + own.shape[1:], own.dtype),) * 2,
        in_specs=[SMEM, VMEM, VMEM],
        out_specs=(VMEM, VMEM),
        compiler_params=limit(4),
        name="collect",
    )(asked, own, mirror)


def context_kernel(tile_ref, cblock_ref, factors_ref, marks_ref, context_ref, wide_ref, held_ref, sem_ref):
    copy = pltpu.make_async_copy(marks_ref, held_ref, sem_ref)
    copy.start()
    users = held_ref.shape[1]
    per = LANES // CB
    wide_ref[...] = factors_ref[...].astype(jnp.float32)
    lane = lax.broadcasted_iota(jnp.int32, (ROWS, LANES), 1)
    sub = lax.broadcasted_iota(jnp.int32, (CB, users), 0)
    copy.wait()

    def some(first, _):
        factors, hits = [], []
        for i in range(per):
            named = tile_ref[first * per + i]
            tile = jnp.maximum(named, 0)
            cblock = cblock_ref[tile]
            start = pl.multiple_of(cblock // per * LANES, LANES)
            shift = lax.rem(LANES + (i - lax.rem(cblock, per)) * CB, LANES)
            turned = pltpu.roll(wide_ref[:, pl.ds(start, LANES)], shift, 1)
            here = jnp.logical_and(lane // CB == i, named >= 0)
            factors.append(jnp.where(here, turned, 0.0))
            marks = jnp.broadcast_to(held_ref[pl.ds(tile, 1), :], (CB, users))
            hits.append(jnp.where(marks == sub, 1.0, 0.0))
        factors = jnp.concatenate(factors, axis=0).astype(jnp.bfloat16)
        hits = jnp.concatenate(hits, axis=0).astype(jnp.bfloat16)
        rows = pl.ds(pl.multiple_of(first * per, per), per)
        context_ref[rows] = dot(factors, hits).reshape(per, ROWS, users)
        return 0

    lax.fori_loop(0, tile_ref.shape[0] // per, some, 0)


def context_values(tile_of, cblock, factors, marks):
    places, users = tile_of.shape[0], marks.shape[1]
    return pl.pallas_call(
        context_kernel,
        out_shape=jax.ShapeDtypeStruct((places, ROWS, users), jnp.float32),
        in_specs=[SMEM, SMEM, VMEM, ANY],
        out_specs=VMEM,
        scratch_shapes=[
            pltpu.VMEM(factors.shape, jnp.float32),
            pltpu.VMEM(marks.shape, marks.dtype),
            pltpu.SemaphoreType.DMA,
        ],
        compiler_params=limit(8),
        cost_estimate=pl.CostEstimate(flops=10**7, bytes_accessed=2 * 10**7, transcendentals=0),
        name="contexts",
    )(tile_of, in_hbm(cblock), factors, in_hbm(marks))


def pack_places(me):
    return {
        (core, plane): jnp.bitwise_xor(lax.rem(me, CHUNKS), core + 2 * plane)
        for core in range(2)
        for plane in range(4)
    }


PIECES = [(core, plane) for core in (1, 0) for plane in (3, 1, 2, 0)]


def pack_rows(ranks):
    groups = ranks // LANES
    return (groups * (groups + 1) // 2 + groups) * LANES


def tiles_kernel(side, tile_ref, count_ref, me_ref, blocks_ref, weights_ref, context_ref, basis_ref, *refs):
    if side:
        before_ref, refs = refs[0], refs[1:]
        piece_refs, refs = refs[: len(PIECES)], refs[len(PIECES) :]
        stack_ref, square_ref, pack_ref, basis_held, basis_sem, *refs = refs
    y_ref, even_ref, odd_ref, weights_held, context_held, weights_sem, context_sem = refs
    rank_c, rank_i, users = y_ref.shape
    places = blocks_ref.shape[0]
    batches = places // BATCH
    half = rank_c // 2

    def weights_copy(place):
        tile = jnp.maximum(tile_ref[side * places + place], 0)
        return pltpu.make_async_copy(weights_ref.at[tile], weights_held.at[place], weights_sem.at[place])

    def start(place, _):
        weights_copy(place).start()
        return 0

    lax.fori_loop(0, BATCH, start, 0)
    contexts_copy = pltpu.make_async_copy(
        context_ref.at[pl.ds(side * places, places)], context_held, context_sem
    )
    contexts_copy.start()
    lax.fori_loop(BATCH, places, start, 0)
    if side:
        basis_copy = pltpu.make_async_copy(basis_ref, basis_held, basis_sem)
        basis_copy.start()

    def multiply(batch, place, into_ref):
        tile = batch * BATCH + place
        product = dot(blocks_ref[tile], weights_held[tile])
        into_ref[place] = product.astype(jnp.bfloat16).astype(jnp.float32)

    def add(batch, part, from_ref):
        lanes = slice(part // 2 * LANES, (part // 2 + 1) * LANES)
        ranks = range(part % 2 * half, (part % 2 + 1) * half)
        strips = [slice(i, i + ROWS) for i in range(0, rank_i, ROWS)]
        totals = [[y_ref[r, strip, lanes] for strip in strips] for r in ranks]
        for place in range(BATCH):
            parts_of = [from_ref[place, strip, lanes] for strip in strips]
            for i, r in enumerate(ranks):
                values = context_held[batch * BATCH + place, r : r + 1, lanes]
                values = jnp.broadcast_to(values, (ROWS, LANES))
                for j in range(len(strips)):
                    totals[i][j] = totals[i][j] + values * parts_of[j]
        for i, r in enumerate(ranks):
            for strip, total in zip(strips, totals[i]):
                y_ref[r, strip, lanes] = total

    y_ref[...] = before_ref[...] if side else jnp.zeros_like(y_ref)
    parts = 2 * users // LANES
    for place in range(BATCH):
        weights_copy(place).wait()
    for place in range(BATCH):
        multiply(0, place, even_ref)
    contexts_copy.wait()

    def turn(batch, from_ref, into_ref):
        for place in range(BATCH):
            weights_copy((batch + 1) * BATCH + place).wait()
        for part in range(max(parts, BATCH)):
            if part < BATCH:
                multiply(batch + 1, part, into_ref)
            if part < parts:
                add(batch, part, from_ref)

    def pair(index, _):
        turn(2 * index, even_ref, odd_ref)
        turn(2 * index + 1, odd_ref, even_ref)
        return 0

    lax.fori_loop(0, batches // 2 - 1, pair, 0)
    turn(batches - 2, even_ref, odd_ref)
    for part in range(parts):
        add(batches - 1, part, odd_ref)
    if not side:
        return

    living = lax.broadcasted_iota(jnp.int32, (rank_i, users), 1) < count_ref[0]
    ranks = rank_c * rank_i
    for r in range(rank_c):
        high, low = split(jnp.where(living, y_ref[r], 0.0))
        stack_ref[r * rank_i : (r + 1) * rank_i] = high
        stack_ref[ranks + r * rank_i : ranks + (r + 1) * rank_i] = low
    square_ref[...] = dot_nt(stack_ref[...], stack_ref[:ranks])
    basis_copy.wait()
    projection = dot(stack_ref[...], jnp.concatenate(split(basis_held[...]), axis=1))
    groups = ranks // LANES
    place = 0
    for i in range(groups):
        rows = slice(i * LANES, (i + 1) * LANES)
        low_rows = slice(ranks + i * LANES, ranks + (i + 1) * LANES)
        for j in range(i, groups):
            lanes = slice(j * LANES, (j + 1) * LANES)
            low_lanes = slice(ranks + j * LANES, ranks + (j + 1) * LANES)
            block = square_ref[rows, lanes] + square_ref[low_rows, lanes] + square_ref[low_lanes, rows].T
            pack_ref[place * LANES : (place + 1) * LANES] = block
            place += 1
    pack_ref[place * LANES : (place + groups) * LANES] = quarters(projection)
    chunk = piece_refs[0].shape[0]
    places = pack_places(me_ref[0])
    for piece, ref in zip(PIECES, piece_refs):
        ref[...] = pack_ref[pl.ds(pl.multiple_of(places[piece] * chunk, ROWS), chunk)]


def tile_sums(side, tile_of, count, me, blocks, weights, contexts, user_basis, before=None):
    _, block_len, users = weights.shape
    places, rank_i = blocks.shape[:2]
    rank_c = contexts.shape[1]
    ranks = rank_c * rank_i
    rows = pack_rows(ranks)
    y = jax.ShapeDtypeStruct((rank_c, rank_i, users), jnp.float32)
    scratch = [
        pltpu.VMEM((BATCH, rank_i, users), jnp.float32),
        pltpu.VMEM((BATCH, rank_i, users), jnp.float32),
        pltpu.VMEM((places, block_len, users), weights.dtype),
        pltpu.VMEM((places,) + contexts.shape[1:], contexts.dtype),
        pltpu.SemaphoreType.DMA((places,)),
        pltpu.SemaphoreType.DMA,
    ]
    out_shape = (y,)
    operands = [tile_of, count, me, blocks, in_hbm(weights), contexts, in_hbm(user_basis)]
    in_specs = [SMEM] * 3 + [VMEM] + [ANY] * 3
    if side:
        operands.append(before)
        in_specs.append(VMEM)
        out_shape = (jax.ShapeDtypeStruct((rows // CHUNKS, LANES), jnp.float32),) * len(PIECES)
        out_shape += (jax.ShapeDtypeStruct((2 * ranks, users), jnp.bfloat16),)
        scratch = [
            pltpu.VMEM((2 * ranks, ranks), jnp.float32),
            pltpu.VMEM((rows, LANES), jnp.float32),
            pltpu.VMEM(user_basis.shape, user_basis.dtype),
            pltpu.SemaphoreType.DMA,
            pltpu.VMEM(y.shape, y.dtype),
        ] + scratch
    held = 3 * places * block_len * users // MIB
    out = pl.pallas_call(
        functools.partial(tiles_kernel, side),
        out_shape=out_shape,
        in_specs=in_specs,
        out_specs=(VMEM,) * len(out_shape),
        scratch_shapes=scratch,
        compiler_params=limit(12 + held),
        cost_estimate=pl.CostEstimate(flops=10**9, bytes_accessed=6 * 10**6, transcendentals=0),
        name="tile_sums",
    )(*operands)
    return (dict(zip(PIECES, out[:-1])), out[-1]) if side else out[0]


def inverse_factor(gram):
    order = gram.shape[0]
    panels = order // ROWS
    sub = lax.broadcasted_iota(jnp.int32, (ROWS, order), 0)
    lane = lax.broadcasted_iota(jnp.int32, (ROWS, order), 1)
    left = [gram[ROWS * i : ROWS * (i + 1)] for i in range(panels)]
    right = [jnp.where(lane == sub + ROWS * i, 1.0, 0.0) for i in range(panels)]
    for k in range(panels):
        columns = {
            i: [
                jnp.broadcast_to(left[i][:, ROWS * k + j : ROWS * k + j + 1], (ROWS, order))
                for j in range(ROWS)
            ]
            for i in range(k, panels)
        }
        row, tail = left[k], right[k]
        scale = jnp.zeros((ROWS, order), jnp.float32)
        rows, tails = [], []
        for j in range(ROWS):
            head = columns[k][j]
            pivot = jnp.broadcast_to(head[j : j + 1], (ROWS, order))
            inverse = pl.reciprocal(pivot, approx=True)
            inverse = inverse * (2.0 - pivot * inverse)
            scale = jnp.where(sub == j, pivot, scale)
            rows.append(jnp.broadcast_to(row[j : j + 1], (ROWS, order)))
            tails.append(jnp.broadcast_to(tail[j : j + 1], (ROWS, order)))
            below = jnp.where(sub > j, head, 0.0) * inverse
            row = row - below * rows[j]
            tail = tail - below * tails[j]
            facts = {k: below}
            for i in range(k + 1, panels):
                facts[i] = columns[i][j] * inverse
            for c in range(j + 1, ROWS):
                crossing = jnp.broadcast_to(head[c : c + 1], (ROWS, order))
                for i in range(k, panels):
                    columns[i][c] = columns[i][c] - facts[i] * crossing
            for i in range(k + 1, panels):
                left[i] = left[i] - facts[i] * rows[j]
                right[i] = right[i] - facts[i] * tails[j]
        right[k] = tail * lax.rsqrt(scale)
    return jnp.concatenate(right, axis=0)


def finish_kernel(total_users, me_ref, stack_ref, *rest):
    piece_refs, (basis_ref, core_out_ref, pack_ref, full_ref) = rest[: len(PIECES)], rest[len(PIECES) :]
    chunk = piece_refs[0].shape[0]
    places = pack_places(me_ref[0])
    for piece, ref in zip(PIECES, piece_refs):
        pack_ref[pl.ds(pl.multiple_of(places[piece] * chunk, ROWS), chunk)] = ref[...]
    ranks = full_ref.shape[1]
    groups = ranks // LANES
    place = 0
    for i in range(groups):
        for j in range(i, groups):
            block = pack_ref[place * LANES : (place + 1) * LANES]
            for row, lane, part in ((i, j, block), (j, i, block.T))[: 1 if i == j else 2]:
                lanes = slice(lane * LANES, (lane + 1) * LANES)
                high, low = split(part)
                full_ref[row * LANES : (row + 1) * LANES, lanes] = high
                full_ref[ranks + row * LANES : ranks + (row + 1) * LANES, lanes] = low
            place += 1
    projection = pack_ref[place * LANES : (place + groups) * LANES]
    crossed = quarters(dot(full_ref[...], jnp.concatenate(split(projection), axis=1)))
    crossed_high, crossed_low = split(crossed)
    turned = jnp.concatenate(
        [projection[i * LANES : (i + 1) * LANES].T for i in range(groups)], axis=1
    )
    turned_stack = jnp.concatenate(split(turned), axis=0)
    gram = quarters(dot(turned_stack, jnp.concatenate([crossed_high, crossed_low], axis=1)))
    projected_high, projected_low = split(thrice(turned_stack, stack_ref[:ranks], stack_ref[ranks:], dot))
    inverse_stack = jnp.concatenate(split(inverse_factor(gram)), axis=0)
    root = total_users ** 0.5
    scaled = thrice(inverse_stack, projected_high, projected_low, dot) * root
    for i in range(scaled.shape[1] // LANES):
        basis_ref[i * LANES : (i + 1) * LANES] = scaled[:, i * LANES : (i + 1) * LANES].T
    core_out_ref[...] = thrice(inverse_stack, crossed_high, crossed_low, dot_nt) * (1.0 / root)


def finish(me, stack, pieces, devices):
    ranks, users = stack.shape[0] // 2, stack.shape[1]
    return pl.pallas_call(
        functools.partial(finish_kernel, users * devices),
        out_shape=(
            jax.ShapeDtypeStruct((users, LANES), jnp.float32),
            jax.ShapeDtypeStruct((LANES, ranks), jnp.float32),
        ),
        in_specs=[SMEM] + [VMEM] * (1 + len(PIECES)),
        out_specs=(VMEM, VMEM),
        scratch_shapes=[
            pltpu.VMEM((pack_rows(ranks), LANES), jnp.float32),
            pltpu.VMEM((2 * ranks, ranks), jnp.bfloat16),
        ],
        compiler_params=limit(16),
        name="finish",
    )(me, stack, *[pieces[piece] for piece in PIECES])


def swap(value, mask, devices):
    return lax.ppermute(value, "users", [(i, i ^ mask) for i in range(devices)])


def reduce_pieces(pieces, devices):
    got = {plane: swap(pieces[1, plane], 1, devices) for plane in (3, 1, 2, 0)}
    total = pieces[0, 0] + got[0]
    for plane in (3, 1, 2):
        total = total + swap(pieces[0, plane] + got[plane], 2 * plane, devices)
    mask = CHUNKS
    while mask < devices:
        total = total + swap(total, mask, devices)
        mask *= 2
    return total


def spread_pieces(total, devices):
    pieces = {(0, 0): total}
    for plane in (3, 1, 2):
        pieces[0, plane] = swap(total, 2 * plane, devices)
    for plane in (0, 3, 1, 2):
        pieces[1, plane] = swap(pieces[0, plane], 1, devices)
    return pieces


def body(
    tile_owner, tile_slot, tile_cblock, tile_context, tile_weights,
    item_factors, context_factors, user_basis, user_counts,
):
    devices = lax.axis_size("users")
    half = devices // 2
    me = lax.axis_index("users").astype(jnp.int32).reshape(1)

    mirror = swap(item_factors, half, devices)
    requests, tile_of, own = route(me, tile_owner[:, 0], tile_slot, item_factors, half)
    sides = [list(range(half)), list(range(half, devices))]

    def exchange(value):
        return lax.all_to_all(value, "users", 0, 0, axis_index_groups=sides, tiled=True)

    asked, mirror = lax.optimization_barrier((exchange(requests), mirror))
    near, far = collect(asked, own, mirror)
    near, far, cblock = lax.optimization_barrier((near, far, tile_cblock))
    near, far = exchange(near), exchange(far)
    contexts = context_values(tile_of, cblock, context_factors, tile_context)
    shared = (tile_of, user_counts, me)
    before = tile_sums(0, *shared, near, tile_weights, contexts, user_basis)
    pieces, stack = tile_sums(1, *shared, far, tile_weights, contexts, user_basis, before)
    pieces = spread_pieces(reduce_pieces(pieces, devices), devices)
    return finish(me, stack, pieces, devices)


def solution(mesh):
    return jax.shard_map(
        body,
        mesh=mesh,
        in_specs=(
            P("users", None), P("users"), P("users"), P("users", None), P("users", None, None),
            P("users", None, None), P(), P("users", None), P("users"),
        ),
        out_specs=(P("users", None), P()),
        check_vma=False,
    )
```

```python
import functools

import jax
import jax.numpy as jnp
from jax import lax
from jax.experimental import pallas as pl
from jax.experimental.pallas import tpu as pltpu
from jax.sharding import PartitionSpec as P

CB = 8
SLOTS = 2
PLACES = 2 * SLOTS
LANES = 128
ROWS = 8
BATCH = 8
CHUNKS = 8
GROUP = 32
MIB = 2**20

SMEM = pl.BlockSpec(memory_space=pltpu.SMEM)
VMEM = pl.BlockSpec(memory_space=pltpu.VMEM)
ANY = pl.BlockSpec(memory_space=pl.ANY)


def in_hbm(value):
    return pltpu.with_memory_space_constraint(value, pltpu.HBM)


def limit(mib):
    return pltpu.CompilerParams(vmem_limit_bytes=mib * MIB)


def dot(lhs, rhs):
    return jnp.dot(lhs, rhs, preferred_element_type=jnp.float32)


def dot_nt(lhs, rhs):
    return lax.dot_general(lhs, rhs, (((1,), (1,)), ((), ())), preferred_element_type=jnp.float32)


def split(value):
    high = value.astype(jnp.bfloat16)
    return high, (value - high.astype(jnp.float32)).astype(jnp.bfloat16)


def quarters(value):
    rows, lanes = value.shape[0] // 2, value.shape[1] // 2
    return (value[:rows, :lanes] + value[:rows, lanes:]) + (value[rows:, :lanes] + value[rows:, lanes:])


def thrice(stack, high, low, product):
    rows = stack.shape[0] // 2
    first = product(stack, high)
    return first[:rows] + (first[rows:] + product(stack[:rows], low))


def route_kernel(half, me_ref, owner_ref, slot_ref, own_ref, request_ref, where_ref, held_ref, used_ref, sem_ref):
    copy = pltpu.make_async_copy(own_ref, held_ref, sem_ref)
    copy.start()
    side = me_ref[0] // half
    lane = lax.broadcasted_iota(jnp.int32, (1, LANES), 1)

    def clear(place, _):
        used_ref[place] = 0
        return 0

    lax.fori_loop(0, 2 * half, clear, 0, unroll=8)
    request_ref[...] = jnp.zeros_like(request_ref)

    def assign(tile, _):
        owner = owner_ref[tile]
        taken = used_ref[owner]
        used_ref[owner] = taken + 1
        low = lax.rem(owner, half)
        place = jnp.where(owner // half == side, 0, SLOTS) + taken
        request_ref[low] = jnp.where(lane == place, slot_ref[tile], request_ref[low])
        where_ref[tile] = low * PLACES + place
        return 0

    lax.fori_loop(0, owner_ref.shape[0], assign, 0, unroll=4)
    copy.wait()


def route(me, owners, slots, own, half):
    return pl.pallas_call(
        functools.partial(route_kernel, half),
        out_shape=(
            jax.ShapeDtypeStruct((half, 1, LANES), jnp.int32),
            jax.ShapeDtypeStruct(owners.shape, jnp.int32),
            jax.ShapeDtypeStruct(own.shape, own.dtype),
        ),
        in_specs=[SMEM, SMEM, SMEM, ANY],
        out_specs=(VMEM, SMEM, VMEM),
        scratch_shapes=[pltpu.SMEM((2 * half,), jnp.int32), pltpu.SemaphoreType.DMA],
        compiler_params=limit(4),
        name="route",
    )(me, in_hbm(owners), in_hbm(slots), in_hbm(own))


def collect_kernel(asked_ref, own_ref, mirror_ref, out_ref):
    for peer in range(asked_ref.shape[0]):
        for place in range(PLACES):
            source = own_ref if place < SLOTS else mirror_ref
            out_ref[peer * PLACES + place] = source[asked_ref[peer, 0, place]]


def collect(asked, own, mirror):
    return pl.pallas_call(
        collect_kernel,
        out_shape=jax.ShapeDtypeStruct((asked.shape[0] * PLACES,) + own.shape[1:], own.dtype),
        in_specs=[SMEM, VMEM, VMEM],
        out_specs=VMEM,
        compiler_params=limit(4),
        name="collect",
    )(asked, own, mirror)


def context_kernel(cblock_ref, table_ref, marks_ref, context_ref):
    tiles, users = marks_ref.shape

    def one(tile, _):
        table = table_ref[cblock_ref[tile]]
        marks = jnp.broadcast_to(marks_ref[pl.ds(tile, 1), :], (ROWS, users))
        total = jnp.zeros((ROWS, users), jnp.float32)
        for k in range(CB):
            column = jnp.broadcast_to(table[:, k : k + 1], (ROWS, users))
            total = jnp.where(marks == k, column, total)
        context_ref[tile] = total
        return 0

    lax.fori_loop(0, tiles, one, 0, unroll=2)


def context_values(cblock, table, marks):
    tiles, users = marks.shape
    return pl.pallas_call(
        context_kernel,
        out_shape=jax.ShapeDtypeStruct((tiles, ROWS, users), jnp.float32),
        in_specs=[SMEM, VMEM, VMEM],
        out_specs=VMEM,
        compiler_params=limit(4),
        cost_estimate=pl.CostEstimate(flops=10**7, bytes_accessed=2 * 10**7, transcendentals=0),
        name="contexts",
    )(in_hbm(cblock), table, marks)


def pack_places(me):
    return {
        (core, plane): jnp.bitwise_xor(lax.rem(me, CHUNKS), core + 2 * plane)
        for core in range(2)
        for plane in range(4)
    }


PIECES = [(core, plane) for core in (1, 0) for plane in (3, 1, 2, 0)]


def pack_rows(ranks):
    groups = ranks // LANES
    return (groups * (groups + 1) // 2 + groups) * LANES


def tiles_kernel(
    where_ref, count_ref, me_ref, blocks_ref, weights_ref, context_ref, basis_ref, *refs
):
    piece_refs, refs = refs[: len(PIECES)], refs[len(PIECES) :]
    stack_ref, y_ref, square_ref, pack_ref, even_ref, odd_ref = refs[:6]
    weights_held, context_held, basis_held, weights_sem, context_sem, basis_sem = refs[6:]
    rank_c, rank_i, users = y_ref.shape
    batches = weights_ref.shape[0] // BATCH
    half = rank_c // 2

    def weights_copy(batch):
        rows = pl.ds(batch * BATCH, BATCH)
        return pltpu.make_async_copy(weights_ref.at[rows], weights_held.at[rows], weights_sem.at[batch])

    weights_copy(0).start()
    contexts_copy = pltpu.make_async_copy(context_ref, context_held, context_sem)
    contexts_copy.start()
    for batch in range(1, batches):
        weights_copy(batch).start()
    basis_copy = pltpu.make_async_copy(basis_ref, basis_held, basis_sem)
    basis_copy.start()

    def multiply(batch, place, into_ref):
        tile = batch * BATCH + place
        product = dot(blocks_ref[where_ref[tile]], weights_held[tile])
        into_ref[place] = product.astype(jnp.bfloat16).astype(jnp.float32)

    def add(batch, part, from_ref):
        lanes = slice(part // 2 * LANES, (part // 2 + 1) * LANES)
        ranks = range(part % 2 * half, (part % 2 + 1) * half)
        strips = [slice(i, i + ROWS) for i in range(0, rank_i, ROWS)]
        totals = [[y_ref[r, strip, lanes] for strip in strips] for r in ranks]
        for place in range(BATCH):
            parts_of = [from_ref[place, strip, lanes] for strip in strips]
            for i, r in enumerate(ranks):
                values = context_held[batch * BATCH + place, r : r + 1, lanes]
                values = jnp.broadcast_to(values, (ROWS, LANES))
                for j in range(len(strips)):
                    totals[i][j] = totals[i][j] + values * parts_of[j]
        for i, r in enumerate(ranks):
            for strip, total in zip(strips, totals[i]):
                y_ref[r, strip, lanes] = total

    y_ref[...] = jnp.zeros_like(y_ref)
    parts = 2 * users // LANES
    weights_copy(0).wait()
    for place in range(BATCH):
        multiply(0, place, even_ref)
    contexts_copy.wait()

    def turn(batch, from_ref, into_ref):
        weights_copy(batch + 1).wait()
        for part in range(max(parts, BATCH)):
            if part < BATCH:
                multiply(batch + 1, part, into_ref)
            if part < parts:
                add(batch, part, from_ref)

    def pair(index, _):
        turn(2 * index, even_ref, odd_ref)
        turn(2 * index + 1, odd_ref, even_ref)
        return 0

    lax.fori_loop(0, batches // 2 - 1, pair, 0)
    turn(batches - 2, even_ref, odd_ref)
    for part in range(parts):
        add(batches - 1, part, odd_ref)

    living = lax.broadcasted_iota(jnp.int32, (rank_i, users), 1) < count_ref[0]
    ranks = rank_c * rank_i
    for r in range(rank_c):
        high, low = split(jnp.where(living, y_ref[r], 0.0))
        stack_ref[r * rank_i : (r + 1) * rank_i] = high
        stack_ref[ranks + r * rank_i : ranks + (r + 1) * rank_i] = low
    square_ref[...] = dot_nt(stack_ref[...], stack_ref[:ranks])
    basis_copy.wait()
    projection = dot(stack_ref[...], jnp.concatenate(split(basis_held[...]), axis=1))
    groups = ranks // LANES
    place = 0
    for i in range(groups):
        rows = slice(i * LANES, (i + 1) * LANES)
        low_rows = slice(ranks + i * LANES, ranks + (i + 1) * LANES)
        for j in range(i, groups):
            lanes = slice(j * LANES, (j + 1) * LANES)
            low_lanes = slice(ranks + j * LANES, ranks + (j + 1) * LANES)
            block = square_ref[rows, lanes] + square_ref[low_rows, lanes] + square_ref[low_lanes, rows].T
            pack_ref[place * LANES : (place + 1) * LANES] = block
            place += 1
    pack_ref[place * LANES : (place + groups) * LANES] = quarters(projection)
    chunk = piece_refs[0].shape[0]
    places = pack_places(me_ref[0])
    for piece, ref in zip(PIECES, piece_refs):
        ref[...] = pack_ref[pl.ds(pl.multiple_of(places[piece] * chunk, ROWS), chunk)]


def tile_sums(where, count, me, blocks, weights, contexts, user_basis):
    tiles, _, users = weights.shape
    rank_i = blocks.shape[1]
    rank_c = contexts.shape[1]
    ranks = rank_c * rank_i
    rows = pack_rows(ranks)
    out_shape = (jax.ShapeDtypeStruct((rows // CHUNKS, LANES), jnp.float32),) * len(PIECES)
    out_shape += (jax.ShapeDtypeStruct((2 * ranks, users), jnp.bfloat16),)
    held = 3 * weights.size * 2 // (2 * MIB)
    out = pl.pallas_call(
        tiles_kernel,
        out_shape=out_shape,
        in_specs=[SMEM] * 3 + [VMEM] + [ANY] * 3,
        out_specs=(VMEM,) * len(out_shape),
        scratch_shapes=[
            pltpu.VMEM((rank_c, rank_i, users), jnp.float32),
            pltpu.VMEM((2 * ranks, ranks), jnp.float32),
            pltpu.VMEM((rows, LANES), jnp.float32),
            pltpu.VMEM((BATCH, rank_i, users), jnp.float32),
            pltpu.VMEM((BATCH, rank_i, users), jnp.float32),
            pltpu.VMEM(weights.shape, weights.dtype),
            pltpu.VMEM(contexts.shape, contexts.dtype),
            pltpu.VMEM(user_basis.shape, user_basis.dtype),
            pltpu.SemaphoreType.DMA((tiles // BATCH,)),
            pltpu.SemaphoreType.DMA,
            pltpu.SemaphoreType.DMA,
        ],
        compiler_params=limit(12 + held),
        cost_estimate=pl.CostEstimate(flops=2 * 10**9, bytes_accessed=12 * 10**6, transcendentals=0),
        name="tile_sums",
    )(where, count, me, blocks, in_hbm(weights), in_hbm(contexts), in_hbm(user_basis))
    return dict(zip(PIECES, out[:-1])), out[-1]


def inverse_factor(gram):
    order = gram.shape[0]
    panels = order // ROWS
    sub = lax.broadcasted_iota(jnp.int32, (ROWS, order), 0)
    lane = lax.broadcasted_iota(jnp.int32, (ROWS, order), 1)
    left = [gram[ROWS * i : ROWS * (i + 1)] for i in range(panels)]
    right = [jnp.where(lane == sub + ROWS * i, 1.0, 0.0) for i in range(panels)]
    for k in range(panels):
        columns = {
            i: [
                jnp.broadcast_to(left[i][:, ROWS * k + j : ROWS * k + j + 1], (ROWS, order))
                for j in range(ROWS)
            ]
            for i in range(k, panels)
        }
        row, tail = left[k], right[k]
        scale = jnp.zeros((ROWS, order), jnp.float32)
        rows, tails = [], []
        for j in range(ROWS):
            head = columns[k][j]
            pivot = jnp.broadcast_to(head[j : j + 1], (ROWS, order))
            inverse = pl.reciprocal(pivot, approx=True)
            inverse = inverse * (2.0 - pivot * inverse)
            scale = jnp.where(sub == j, pivot, scale)
            rows.append(jnp.broadcast_to(row[j : j + 1], (ROWS, order)))
            tails.append(jnp.broadcast_to(tail[j : j + 1], (ROWS, order)))
            below = jnp.where(sub > j, head, 0.0) * inverse
            row = row - below * rows[j]
            tail = tail - below * tails[j]
            facts = {k: below}
            for i in range(k + 1, panels):
                facts[i] = columns[i][j] * inverse
            for c in range(j + 1, ROWS):
                crossing = jnp.broadcast_to(head[c : c + 1], (ROWS, order))
                for i in range(k, panels):
                    columns[i][c] = columns[i][c] - facts[i] * crossing
            for i in range(k + 1, panels):
                left[i] = left[i] - facts[i] * rows[j]
                right[i] = right[i] - facts[i] * tails[j]
        right[k] = tail * lax.rsqrt(scale)
    return jnp.concatenate(right, axis=0)


def finish_kernel(total_users, me_ref, stack_ref, *rest):
    piece_refs, (basis_ref, core_out_ref, pack_ref, full_ref) = rest[: len(PIECES)], rest[len(PIECES) :]
    chunk = piece_refs[0].shape[0]
    places = pack_places(me_ref[0])
    for piece, ref in zip(PIECES, piece_refs):
        pack_ref[pl.ds(pl.multiple_of(places[piece] * chunk, ROWS), chunk)] = ref[...]
    ranks = full_ref.shape[1]
    groups = ranks // LANES
    place = 0
    for i in range(groups):
        for j in range(i, groups):
            block = pack_ref[place * LANES : (place + 1) * LANES]
            for row, lane, part in ((i, j, block), (j, i, block.T))[: 1 if i == j else 2]:
                lanes = slice(lane * LANES, (lane + 1) * LANES)
                high, low = split(part)
                full_ref[row * LANES : (row + 1) * LANES, lanes] = high
                full_ref[ranks + row * LANES : ranks + (row + 1) * LANES, lanes] = low
            place += 1
    projection = pack_ref[place * LANES : (place + groups) * LANES]
    crossed = quarters(dot(full_ref[...], jnp.concatenate(split(projection), axis=1)))
    crossed_high, crossed_low = split(crossed)
    turned = jnp.concatenate(
        [projection[i * LANES : (i + 1) * LANES].T for i in range(groups)], axis=1
    )
    turned_stack = jnp.concatenate(split(turned), axis=0)
    gram = quarters(dot(turned_stack, jnp.concatenate([crossed_high, crossed_low], axis=1)))
    projected_high, projected_low = split(thrice(turned_stack, stack_ref[:ranks], stack_ref[ranks:], dot))
    inverse_stack = jnp.concatenate(split(inverse_factor(gram)), axis=0)
    root = total_users ** 0.5
    scaled = thrice(inverse_stack, projected_high, projected_low, dot) * root
    for i in range(scaled.shape[1] // LANES):
        basis_ref[i * LANES : (i + 1) * LANES] = scaled[:, i * LANES : (i + 1) * LANES].T
    core_out_ref[...] = thrice(inverse_stack, crossed_high, crossed_low, dot_nt) * (1.0 / root)


def finish(me, stack, pieces, devices):
    ranks, users = stack.shape[0] // 2, stack.shape[1]
    return pl.pallas_call(
        functools.partial(finish_kernel, users * devices),
        out_shape=(
            jax.ShapeDtypeStruct((users, LANES), jnp.float32),
            jax.ShapeDtypeStruct((LANES, ranks), jnp.float32),
        ),
        in_specs=[SMEM] + [VMEM] * (1 + len(PIECES)),
        out_specs=(VMEM, VMEM),
        scratch_shapes=[
            pltpu.VMEM((pack_rows(ranks), LANES), jnp.float32),
            pltpu.VMEM((2 * ranks, ranks), jnp.bfloat16),
        ],
        compiler_params=limit(16),
        name="finish",
    )(me, stack, *[pieces[piece] for piece in PIECES])


def swap(value, mask, devices):
    return lax.ppermute(value, "users", [(i, i ^ mask) for i in range(devices)])


def encode(value):
    rows, lanes = value.shape
    groups = rows // GROUP
    parts = value.reshape(groups, GROUP, lanes)
    most = jnp.max(jnp.abs(parts), axis=1, keepdims=True)
    exponent = jnp.clip(jnp.floor(jnp.log2(most)) + 1.0, -110.0, 128.0)
    coded = jnp.clip(jnp.round(parts * jnp.exp2(14.0 - exponent)), -32767.0, 32767.0)
    extra = jnp.pad(exponent.reshape(groups, lanes), ((0, -groups % 16), (0, 0)))
    return jnp.concatenate([coded.reshape(rows, lanes), extra], axis=0).astype(jnp.int16)


def decode(coded, rows):
    lanes = coded.shape[1]
    groups = rows // GROUP
    scale = jnp.exp2(coded[rows : rows + groups].astype(jnp.float32) - 14.0)
    parts = coded[:rows].astype(jnp.float32).reshape(groups, GROUP, lanes)
    return (parts * scale.reshape(groups, 1, lanes)).reshape(rows, lanes)


def reduce_pieces(pieces, devices):
    rows = pieces[0, 0].shape[0]
    got = {plane: swap(pieces[1, plane], 1, devices) for plane in (3, 1, 2, 0)}
    total = pieces[0, 0] + got[0]
    for plane in (3, 1, 2):
        coded = encode(pieces[0, plane] + got[plane])
        total = total + decode(swap(coded, 2 * plane, devices), rows)
    mask = CHUNKS
    while mask < devices:
        coded = encode(total)
        total = decode(coded, rows) + decode(swap(coded, mask, devices), rows)
        mask *= 2
    return encode(total)


def spread_pieces(total, devices, rows):
    coded = {(0, 0): total}
    for plane in (3, 1, 2):
        coded[0, plane] = swap(total, 2 * plane, devices)
    for plane in (0, 3, 1, 2):
        coded[1, plane] = swap(coded[0, plane], 1, devices)
    return {piece: decode(value, rows) for piece, value in coded.items()}


def body(
    tile_owner, tile_slot, tile_cblock, tile_context, tile_weights,
    item_factors, context_factors, user_basis, user_counts,
):
    devices = lax.axis_size("users")
    half = devices // 2
    rank_c = context_factors.shape[0]
    me = lax.axis_index("users").astype(jnp.int32).reshape(1)

    mirror = swap(item_factors, half, devices)
    requests, where, own = route(me, tile_owner[:, 0], tile_slot, item_factors, half)
    sides = [list(range(half)), list(range(half, devices))]
    asked = lax.all_to_all(requests, "users", 0, 0, axis_index_groups=sides, tiled=True)
    found = collect(asked, own, mirror)
    found, cblock, factors = lax.optimization_barrier((found, tile_cblock, context_factors))
    blocks = lax.all_to_all(found, "users", 0, 0, axis_index_groups=sides, tiled=True)

    table = factors.astype(jnp.float32).reshape(rank_c, -1, CB).transpose(1, 0, 2)
    contexts = context_values(cblock, table, tile_context)
    pieces, stack = tile_sums(
        where, user_counts, me, blocks, tile_weights, contexts, user_basis
    )
    rows = pieces[0, 0].shape[0]
    pieces = spread_pieces(reduce_pieces(pieces, devices), devices, rows)
    return finish(me, stack, pieces, devices)


def solution(mesh):
    return jax.shard_map(
        body,
        mesh=mesh,
        in_specs=(
            P("users", None), P("users"), P("users"), P("users", None), P("users", None, None),
            P("users", None, None), P(), P("users", None), P("users"),
        ),
        out_specs=(P("users", None), P()),
        check_vma=False,
    )
```

```python
import functools

import jax
import jax.numpy as jnp
from jax import lax
from jax.experimental import pallas as pl
from jax.experimental.pallas import tpu as pltpu
from jax.sharding import PartitionSpec as P

CB = 8
SLOTS = 2
PLACES = 2 * SLOTS
LANES = 128
ROWS = 8
BATCH = 8
CHUNKS = 8
GROUP = 32
MIB = 2**20

SMEM = pl.BlockSpec(memory_space=pltpu.SMEM)
VMEM = pl.BlockSpec(memory_space=pltpu.VMEM)
ANY = pl.BlockSpec(memory_space=pl.ANY)


def in_hbm(value):
    return pltpu.with_memory_space_constraint(value, pltpu.HBM)


def limit(mib):
    return pltpu.CompilerParams(vmem_limit_bytes=mib * MIB)


def dot(lhs, rhs):
    return jnp.dot(lhs, rhs, preferred_element_type=jnp.float32)


def dot_nt(lhs, rhs):
    return lax.dot_general(lhs, rhs, (((1,), (1,)), ((), ())), preferred_element_type=jnp.float32)


def split(value):
    high = value.astype(jnp.bfloat16)
    return high, (value - high.astype(jnp.float32)).astype(jnp.bfloat16)


def quarters(value):
    rows, lanes = value.shape[0] // 2, value.shape[1] // 2
    return (value[:rows, :lanes] + value[:rows, lanes:]) + (value[rows:, :lanes] + value[rows:, lanes:])


def thrice(stack, high, low, product):
    rows = stack.shape[0] // 2
    first = product(stack, high)
    return first[:rows] + (first[rows:] + product(stack[:rows], low))


def route_kernel(half, me_ref, owner_ref, slot_ref, own_ref, request_ref, where_ref, held_ref, used_ref, sem_ref):
    copy = pltpu.make_async_copy(own_ref, held_ref, sem_ref)
    copy.start()
    side = me_ref[0] // half
    lane = lax.broadcasted_iota(jnp.int32, (1, LANES), 1)

    def clear(place, _):
        used_ref[place] = 0
        return 0

    lax.fori_loop(0, 2 * half, clear, 0, unroll=8)
    request_ref[...] = jnp.zeros_like(request_ref)

    def assign(tile, _):
        owner = owner_ref[tile]
        taken = used_ref[owner]
        used_ref[owner] = taken + 1
        low = lax.rem(owner, half)
        place = jnp.where(owner // half == side, 0, SLOTS) + taken
        request_ref[low] = jnp.where(lane == place, slot_ref[tile], request_ref[low])
        where_ref[tile] = low * PLACES + place
        return 0

    lax.fori_loop(0, owner_ref.shape[0], assign, 0, unroll=4)
    copy.wait()


def route(me, owners, slots, own, half):
    return pl.pallas_call(
        functools.partial(route_kernel, half),
        out_shape=(
            jax.ShapeDtypeStruct((half, 1, LANES), jnp.int32),
            jax.ShapeDtypeStruct(owners.shape, jnp.int32),
            jax.ShapeDtypeStruct(own.shape, own.dtype),
        ),
        in_specs=[SMEM, SMEM, SMEM, ANY],
        out_specs=(VMEM, SMEM, VMEM),
        scratch_shapes=[pltpu.SMEM((2 * half,), jnp.int32), pltpu.SemaphoreType.DMA],
        compiler_params=limit(4),
        name="route",
    )(me, in_hbm(owners), in_hbm(slots), in_hbm(own))


def collect_kernel(asked_ref, own_ref, mirror_ref, out_ref):
    for peer in range(asked_ref.shape[0]):
        for place in range(PLACES):
            source = own_ref if place < SLOTS else mirror_ref
            out_ref[peer * PLACES + place] = source[asked_ref[peer, 0, place]]


def collect(asked, own, mirror):
    return pl.pallas_call(
        collect_kernel,
        out_shape=jax.ShapeDtypeStruct((asked.shape[0] * PLACES,) + own.shape[1:], own.dtype),
        in_specs=[SMEM, VMEM, VMEM],
        out_specs=VMEM,
        compiler_params=limit(4),
        name="collect",
    )(asked, own, mirror)


def context_kernel(cblock_ref, table_ref, marks_ref, context_ref):
    tiles, users = marks_ref.shape

    def one(tile, _):
        table = table_ref[cblock_ref[tile]]
        marks = jnp.broadcast_to(marks_ref[pl.ds(tile, 1), :], (ROWS, users))
        total = jnp.zeros((ROWS, users), jnp.float32)
        for k in range(CB):
            column = jnp.broadcast_to(table[:, k : k + 1], (ROWS, users))
            total = jnp.where(marks == k, column, total)
        context_ref[tile] = total
        return 0

    lax.fori_loop(0, tiles, one, 0, unroll=2)


def context_values(cblock, table, marks):
    tiles, users = marks.shape
    return pl.pallas_call(
        context_kernel,
        out_shape=jax.ShapeDtypeStruct((tiles, ROWS, users), jnp.float32),
        in_specs=[SMEM, VMEM, VMEM],
        out_specs=VMEM,
        compiler_params=limit(4),
        cost_estimate=pl.CostEstimate(flops=10**7, bytes_accessed=2 * 10**7, transcendentals=0),
        name="contexts",
    )(in_hbm(cblock), table, marks)


def pack_places(me):
    return {
        (core, plane): jnp.bitwise_xor(lax.rem(me, CHUNKS), core + 2 * plane)
        for core in range(2)
        for plane in range(4)
    }


PIECES = [(core, plane) for core in (1, 0) for plane in (3, 1, 2, 0)]


def pack_rows(ranks):
    groups = ranks // LANES
    return (groups * (groups + 1) // 2 + groups) * LANES


def tiles_kernel(
    where_ref, count_ref, me_ref, blocks_ref, weights_ref, context_ref, basis_ref, *refs
):
    piece_refs, refs = refs[: len(PIECES)], refs[len(PIECES) :]
    stack_ref, y_ref, square_ref, pack_ref, even_ref, odd_ref, paired_ref = refs[:7]
    weights_held, context_held, basis_held, weights_sem, context_sem, basis_sem = refs[7:]
    rank_c, rank_i, users = y_ref.shape
    block_len = weights_ref.shape[1]
    batches = weights_ref.shape[0] // BATCH
    half = rank_c // 2

    def weights_copy(batch):
        rows = pl.ds(batch * BATCH, BATCH)
        return pltpu.make_async_copy(weights_ref.at[rows], weights_held.at[rows], weights_sem.at[batch])

    weights_copy(0).start()
    contexts_copy = pltpu.make_async_copy(context_ref, context_held, context_sem)
    contexts_copy.start()
    for batch in range(1, batches):
        weights_copy(batch).start()
    basis_copy = pltpu.make_async_copy(basis_ref, basis_held, basis_sem)
    basis_copy.start()

    def set_pair(pair, _):
        paired_ref[pair] = jnp.zeros(paired_ref.shape[1:], paired_ref.dtype)
        for i in range(2):
            block = blocks_ref[where_ref[2 * pair + i]]
            paired_ref[pair, i * rank_i : (i + 1) * rank_i, i * block_len : (i + 1) * block_len] = block
        return 0

    lax.fori_loop(0, paired_ref.shape[0], set_pair, 0, unroll=2)

    def multiply(batch, place, into_ref):
        pair = (batch * BATCH + place) // 2
        weights = weights_held[pl.ds(2 * pair, 2)].reshape(2 * block_len, users)
        product = dot(paired_ref[pair], weights).astype(jnp.bfloat16).astype(jnp.float32)
        into_ref[place : place + 2] = product.reshape(2, rank_i, users)

    def add(batch, part, from_ref):
        lanes = slice(part // 2 * LANES, (part // 2 + 1) * LANES)
        ranks = range(part % 2 * half, (part % 2 + 1) * half)
        strips = [slice(i, i + ROWS) for i in range(0, rank_i, ROWS)]
        totals = [[y_ref[r, strip, lanes] for strip in strips] for r in ranks]
        for place in range(BATCH):
            parts_of = [from_ref[place, strip, lanes] for strip in strips]
            for i, r in enumerate(ranks):
                values = context_held[batch * BATCH + place, r : r + 1, lanes]
                values = jnp.broadcast_to(values, (ROWS, LANES))
                for j in range(len(strips)):
                    totals[i][j] = totals[i][j] + values * parts_of[j]
        for i, r in enumerate(ranks):
            for strip, total in zip(strips, totals[i]):
                y_ref[r, strip, lanes] = total

    y_ref[...] = jnp.zeros_like(y_ref)
    parts = 2 * users // LANES
    weights_copy(0).wait()
    for place in range(0, BATCH, 2):
        multiply(0, place, even_ref)
    contexts_copy.wait()

    def turn(batch, from_ref, into_ref):
        weights_copy(batch + 1).wait()
        for part in range(max(parts, BATCH)):
            if part < BATCH and part % 2 == 0:
                multiply(batch + 1, part, into_ref)
            if part < parts:
                add(batch, part, from_ref)

    def pair(index, _):
        turn(2 * index, even_ref, odd_ref)
        turn(2 * index + 1, odd_ref, even_ref)
        return 0

    lax.fori_loop(0, batches // 2 - 1, pair, 0)
    turn(batches - 2, even_ref, odd_ref)
    for part in range(parts):
        add(batches - 1, part, odd_ref)

    living = lax.broadcasted_iota(jnp.int32, (rank_i, users), 1) < count_ref[0]
    ranks = rank_c * rank_i
    for r in range(rank_c):
        high, low = split(jnp.where(living, y_ref[r], 0.0))
        stack_ref[r * rank_i : (r + 1) * rank_i] = high
        stack_ref[ranks + r * rank_i : ranks + (r + 1) * rank_i] = low
    square_ref[...] = dot_nt(stack_ref[...], stack_ref[:ranks])
    basis_copy.wait()
    projection = dot(stack_ref[...], jnp.concatenate(split(basis_held[...]), axis=1))
    groups = ranks // LANES
    place = 0
    for i in range(groups):
        rows = slice(i * LANES, (i + 1) * LANES)
        low_rows = slice(ranks + i * LANES, ranks + (i + 1) * LANES)
        for j in range(i, groups):
            lanes = slice(j * LANES, (j + 1) * LANES)
            low_lanes = slice(ranks + j * LANES, ranks + (j + 1) * LANES)
            block = square_ref[rows, lanes] + square_ref[low_rows, lanes] + square_ref[low_lanes, rows].T
            pack_ref[place * LANES : (place + 1) * LANES] = block
            place += 1
    pack_ref[place * LANES : (place + groups) * LANES] = quarters(projection)
    chunk = piece_refs[0].shape[0]
    places = pack_places(me_ref[0])
    for piece, ref in zip(PIECES, piece_refs):
        ref[...] = pack_ref[pl.ds(pl.multiple_of(places[piece] * chunk, ROWS), chunk)]


def tile_sums(where, count, me, blocks, weights, contexts, user_basis):
    tiles, block_len, users = weights.shape
    rank_i = blocks.shape[1]
    rank_c = contexts.shape[1]
    ranks = rank_c * rank_i
    rows = pack_rows(ranks)
    out_shape = (jax.ShapeDtypeStruct((rows // CHUNKS, LANES), jnp.float32),) * len(PIECES)
    out_shape += (jax.ShapeDtypeStruct((2 * ranks, users), jnp.bfloat16),)
    held = 3 * weights.size * 2 // (2 * MIB)
    out = pl.pallas_call(
        tiles_kernel,
        out_shape=out_shape,
        in_specs=[SMEM] * 3 + [VMEM] + [ANY] * 3,
        out_specs=(VMEM,) * len(out_shape),
        scratch_shapes=[
            pltpu.VMEM((rank_c, rank_i, users), jnp.float32),
            pltpu.VMEM((2 * ranks, ranks), jnp.float32),
            pltpu.VMEM((rows, LANES), jnp.float32),
            pltpu.VMEM((BATCH, rank_i, users), jnp.float32),
            pltpu.VMEM((BATCH, rank_i, users), jnp.float32),
            pltpu.VMEM((tiles // 2, 2 * rank_i, 2 * block_len), blocks.dtype),
            pltpu.VMEM(weights.shape, weights.dtype),
            pltpu.VMEM(contexts.shape, contexts.dtype),
            pltpu.VMEM(user_basis.shape, user_basis.dtype),
            pltpu.SemaphoreType.DMA((tiles // BATCH,)),
            pltpu.SemaphoreType.DMA,
            pltpu.SemaphoreType.DMA,
        ],
        compiler_params=limit(14 + held),
        cost_estimate=pl.CostEstimate(flops=2 * 10**9, bytes_accessed=12 * 10**6, transcendentals=0),
        name="tile_sums",
    )(where, count, me, blocks, in_hbm(weights), in_hbm(contexts), in_hbm(user_basis))
    return dict(zip(PIECES, out[:-1])), out[-1]


def inverse_factor(gram):
    order = gram.shape[0]
    panels = order // ROWS
    sub = lax.broadcasted_iota(jnp.int32, (ROWS, order), 0)
    lane = lax.broadcasted_iota(jnp.int32, (ROWS, order), 1)
    left = [gram[ROWS * i : ROWS * (i + 1)] for i in range(panels)]
    right = [jnp.where(lane == sub + ROWS * i, 1.0, 0.0) for i in range(panels)]
    spread = lambda value, j: jnp.broadcast_to(value[j : j + 1], (ROWS, order))

    def invert(value):
        guess = pl.reciprocal(value, approx=True)
        return guess * (2.0 - value * guess)

    for k in range(panels):
        columns = {
            i: [
                jnp.broadcast_to(left[i][:, ROWS * k + j : ROWS * k + j + 1], (ROWS, order))
                for j in range(ROWS)
            ]
            for i in range(k, panels)
        }
        row, tail = left[k], right[k]
        scale = jnp.ones((ROWS, order), jnp.float32)
        for j in range(0, ROWS, 2):
            first, second = columns[k][j], columns[k][j + 1]
            a, b, d = spread(first, j), spread(first, j + 1), spread(second, j + 1)
            minor = a * d - b * b
            inverse = invert(minor)
            along_a, along_b, along_d = a * inverse, b * inverse, d * inverse
            rows = spread(row, j), spread(row, j + 1)
            tails = spread(tail, j), spread(tail, j + 1)
            lower = invert(a)
            scale = jnp.where(sub == j, a, jnp.where(sub == j + 1, minor * lower, scale))
            facts = {}
            for i in range(k, panels):
                x, y = columns[i][j], columns[i][j + 1]
                facts[i] = x * along_d - y * along_b, y * along_a - x * along_b
            facts[k] = tuple(jnp.where(sub > j + 1, fact, 0.0) for fact in facts[k])
            for c in range(j + 2, ROWS):
                crossings = spread(first, c), spread(second, c)
                for i in range(k, panels):
                    columns[i][c] = columns[i][c] - (facts[i][0] * crossings[0] + facts[i][1] * crossings[1])
            row = row - (facts[k][0] * rows[0] + facts[k][1] * rows[1])
            tail = tail - (facts[k][0] * tails[0] + facts[k][1] * tails[1])
            tail = tail - jnp.where(sub == j + 1, b * lower, 0.0) * tails[0]
            for i in range(k + 1, panels):
                left[i] = left[i] - (facts[i][0] * rows[0] + facts[i][1] * rows[1])
                right[i] = right[i] - (facts[i][0] * tails[0] + facts[i][1] * tails[1])
        right[k] = tail * lax.rsqrt(scale)
    return jnp.concatenate(right, axis=0)


def finish_kernel(total_users, me_ref, stack_ref, *rest):
    piece_refs, (basis_ref, core_out_ref, pack_ref, full_ref) = rest[: len(PIECES)], rest[len(PIECES) :]
    chunk = piece_refs[0].shape[0]
    places = pack_places(me_ref[0])
    for piece, ref in zip(PIECES, piece_refs):
        pack_ref[pl.ds(pl.multiple_of(places[piece] * chunk, ROWS), chunk)] = ref[...]
    ranks = full_ref.shape[1]
    groups = ranks // LANES
    place = 0
    for i in range(groups):
        for j in range(i, groups):
            block = pack_ref[place * LANES : (place + 1) * LANES]
            for row, lane, part in ((i, j, block), (j, i, block.T))[: 1 if i == j else 2]:
                lanes = slice(lane * LANES, (lane + 1) * LANES)
                high, low = split(part)
                full_ref[row * LANES : (row + 1) * LANES, lanes] = high
                full_ref[ranks + row * LANES : ranks + (row + 1) * LANES, lanes] = low
            place += 1
    projection = pack_ref[place * LANES : (place + groups) * LANES]
    crossed = quarters(dot(full_ref[...], jnp.concatenate(split(projection), axis=1)))
    crossed_high, crossed_low = split(crossed)
    turned = jnp.concatenate(
        [projection[i * LANES : (i + 1) * LANES].T for i in range(groups)], axis=1
    )
    turned_stack = jnp.concatenate(split(turned), axis=0)
    gram = quarters(dot(turned_stack, jnp.concatenate([crossed_high, crossed_low], axis=1)))
    projected_high, projected_low = split(thrice(turned_stack, stack_ref[:ranks], stack_ref[ranks:], dot))
    most = jnp.max(jnp.max(gram, axis=1, keepdims=True), axis=0, keepdims=True)
    inverse = inverse_factor(gram * (1.0 / most)) * lax.rsqrt(most)
    inverse_stack = jnp.concatenate(split(inverse), axis=0)
    root = total_users ** 0.5
    scaled = thrice(inverse_stack, projected_high, projected_low, dot) * root
    for i in range(scaled.shape[1] // LANES):
        basis_ref[i * LANES : (i + 1) * LANES] = scaled[:, i * LANES : (i + 1) * LANES].T
    core_out_ref[...] = thrice(inverse_stack, crossed_high, crossed_low, dot_nt) * (1.0 / root)


def finish(me, stack, pieces, devices):
    ranks, users = stack.shape[0] // 2, stack.shape[1]
    return pl.pallas_call(
        functools.partial(finish_kernel, users * devices),
        out_shape=(
            jax.ShapeDtypeStruct((users, LANES), jnp.float32),
            jax.ShapeDtypeStruct((LANES, ranks), jnp.float32),
        ),
        in_specs=[SMEM] + [VMEM] * (1 + len(PIECES)),
        out_specs=(VMEM, VMEM),
        scratch_shapes=[
            pltpu.VMEM((pack_rows(ranks), LANES), jnp.float32),
            pltpu.VMEM((2 * ranks, ranks), jnp.bfloat16),
        ],
        compiler_params=limit(16),
        name="finish",
    )(me, stack, *[pieces[piece] for piece in PIECES])


def swap(value, mask, devices):
    return lax.ppermute(value, "users", [(i, i ^ mask) for i in range(devices)])


def encode(value):
    rows, lanes = value.shape
    groups = rows // GROUP
    parts = value.reshape(groups, GROUP, lanes)
    most = jnp.max(jnp.abs(parts), axis=1, keepdims=True)
    exponent = jnp.clip(jnp.floor(jnp.log2(most)) + 1.0, -110.0, 128.0)
    coded = jnp.clip(jnp.round(parts * jnp.exp2(14.0 - exponent)), -32767.0, 32767.0)
    extra = jnp.pad(exponent.reshape(groups, lanes), ((0, -groups % 16), (0, 0)))
    return jnp.concatenate([coded.reshape(rows, lanes), extra], axis=0).astype(jnp.int16)


def decode(coded, rows):
    lanes = coded.shape[1]
    groups = rows // GROUP
    scale = jnp.exp2(coded[rows : rows + groups].astype(jnp.float32) - 14.0)
    parts = coded[:rows].astype(jnp.float32).reshape(groups, GROUP, lanes)
    return (parts * scale.reshape(groups, 1, lanes)).reshape(rows, lanes)


def reduce_pieces(pieces, devices):
    rows = pieces[0, 0].shape[0]
    got = {plane: swap(pieces[1, plane], 1, devices) for plane in (3, 1, 2, 0)}
    total = pieces[0, 0] + got[0]
    for plane in (3, 1, 2):
        coded = encode(pieces[0, plane] + got[plane])
        total = total + decode(swap(coded, 2 * plane, devices), rows)
    mask = CHUNKS
    while mask < devices:
        coded = encode(total)
        total = decode(coded, rows) + decode(swap(coded, mask, devices), rows)
        mask *= 2
    return encode(total)


def spread_pieces(total, devices, rows):
    coded = {(0, 0): total}
    for plane in (3, 1, 2):
        coded[0, plane] = swap(total, 2 * plane, devices)
    for plane in (0, 3, 1, 2):
        coded[1, plane] = swap(coded[0, plane], 1, devices)
    return {piece: decode(value, rows) for piece, value in coded.items()}


def body(
    tile_owner, tile_slot, tile_cblock, tile_context, tile_weights,
    item_factors, context_factors, user_basis, user_counts,
):
    devices = lax.axis_size("users")
    half = devices // 2
    rank_c = context_factors.shape[0]
    me = lax.axis_index("users").astype(jnp.int32).reshape(1)

    mirror = swap(item_factors, half, devices)
    requests, where, own = route(me, tile_owner[:, 0], tile_slot, item_factors, half)
    sides = [list(range(half)), list(range(half, devices))]
    asked = lax.all_to_all(requests, "users", 0, 0, axis_index_groups=sides, tiled=True)
    found = collect(asked, own, mirror)
    found, cblock, factors = lax.optimization_barrier((found, tile_cblock, context_factors))
    blocks = lax.all_to_all(found, "users", 0, 0, axis_index_groups=sides, tiled=True)

    table = factors.astype(jnp.float32).reshape(rank_c, -1, CB).transpose(1, 0, 2)
    contexts = context_values(cblock, table, tile_context)
    pieces, stack = tile_sums(
        where, user_counts, me, blocks, tile_weights, contexts, user_basis
    )
    rows = pieces[0, 0].shape[0]
    pieces = spread_pieces(reduce_pieces(pieces, devices), devices, rows)
    return finish(me, stack, pieces, devices)


def solution(mesh):
    return jax.shard_map(
        body,
        mesh=mesh,
        in_specs=(
            P("users", None), P("users"), P("users"), P("users", None), P("users", None, None),
            P("users", None, None), P(), P("users", None), P("users"),
        ),
        out_specs=(P("users", None), P()),
        check_vma=False,
    )
```

```python
import functools

import jax
import jax.numpy as jnp
from jax import lax
from jax.experimental import pallas as pl
from jax.experimental.pallas import tpu as pltpu
from jax.sharding import PartitionSpec as P

CB = 8
SLOTS = 2
PLACES = 2 * SLOTS
LANES = 128
ROWS = 8
BATCH = 8
CHUNKS = 8
GROUP = 32
MIB = 2**20

SMEM = pl.BlockSpec(memory_space=pltpu.SMEM)
VMEM = pl.BlockSpec(memory_space=pltpu.VMEM)
ANY = pl.BlockSpec(memory_space=pl.ANY)


def in_hbm(value):
    return pltpu.with_memory_space_constraint(value, pltpu.HBM)


def limit(mib):
    return pltpu.CompilerParams(vmem_limit_bytes=mib * MIB)


def dot(lhs, rhs):
    return jnp.dot(lhs, rhs, preferred_element_type=jnp.float32)


def dot_nt(lhs, rhs):
    return lax.dot_general(lhs, rhs, (((1,), (1,)), ((), ())), preferred_element_type=jnp.float32)


def split(value):
    high = value.astype(jnp.bfloat16)
    return high, (value - high.astype(jnp.float32)).astype(jnp.bfloat16)


def quarters(value):
    rows, lanes = value.shape[0] // 2, value.shape[1] // 2
    return (value[:rows, :lanes] + value[:rows, lanes:]) + (value[rows:, :lanes] + value[rows:, lanes:])


def thrice(stack, high, low, product):
    rows = stack.shape[0] // 2
    first = product(stack, high)
    return first[:rows] + (first[rows:] + product(stack[:rows], low))


def route_kernel(half, me_ref, owner_ref, slot_ref, own_ref, request_ref, where_ref, held_ref, used_ref, sem_ref):
    copy = pltpu.make_async_copy(own_ref, held_ref, sem_ref)
    copy.start()
    side = me_ref[0] // half
    lane = lax.broadcasted_iota(jnp.int32, (1, LANES), 1)

    def clear(place, _):
        used_ref[place] = 0
        return 0

    lax.fori_loop(0, 2 * half, clear, 0, unroll=8)
    request_ref[...] = jnp.zeros_like(request_ref)

    def assign(tile, _):
        owner = owner_ref[tile]
        taken = used_ref[owner]
        used_ref[owner] = taken + 1
        low = lax.rem(owner, half)
        place = jnp.where(owner // half == side, 0, SLOTS) + taken
        request_ref[low] = jnp.where(lane == place, slot_ref[tile], request_ref[low])
        where_ref[tile] = low * PLACES + place
        return 0

    lax.fori_loop(0, owner_ref.shape[0], assign, 0, unroll=4)
    copy.wait()


def route(me, owners, slots, own, half):
    return pl.pallas_call(
        functools.partial(route_kernel, half),
        out_shape=(
            jax.ShapeDtypeStruct((half, 1, LANES), jnp.int32),
            jax.ShapeDtypeStruct(owners.shape, jnp.int32),
            jax.ShapeDtypeStruct(own.shape, own.dtype),
        ),
        in_specs=[SMEM, SMEM, SMEM, ANY],
        out_specs=(VMEM, SMEM, VMEM),
        scratch_shapes=[pltpu.SMEM((2 * half,), jnp.int32), pltpu.SemaphoreType.DMA],
        compiler_params=limit(4),
        name="route",
    )(me, in_hbm(owners), in_hbm(slots), in_hbm(own))


def collect_kernel(asked_ref, own_ref, mirror_ref, out_ref):
    for peer in range(asked_ref.shape[0]):
        for place in range(PLACES):
            source = own_ref if place < SLOTS else mirror_ref
            out_ref[peer * PLACES + place] = source[asked_ref[peer, 0, place]]


def collect(asked, own, mirror):
    return pl.pallas_call(
        collect_kernel,
        out_shape=jax.ShapeDtypeStruct((asked.shape[0] * PLACES,) + own.shape[1:], own.dtype),
        in_specs=[SMEM, VMEM, VMEM],
        out_specs=VMEM,
        compiler_params=limit(4),
        name="collect",
    )(asked, own, mirror)


def context_kernel(cblock_ref, table_ref, marks_ref, context_ref):
    tiles, users = marks_ref.shape

    def one(tile, _):
        table = table_ref[cblock_ref[tile]]
        marks = jnp.broadcast_to(marks_ref[pl.ds(tile, 1), :], (ROWS, users))
        total = jnp.zeros((ROWS, users), jnp.float32)
        for k in range(CB):
            column = jnp.broadcast_to(table[:, k : k + 1], (ROWS, users))
            total = jnp.where(marks == k, column, total)
        context_ref[tile] = total
        return 0

    lax.fori_loop(0, tiles, one, 0, unroll=2)


def context_values(cblock, table, marks):
    tiles, users = marks.shape
    return pl.pallas_call(
        context_kernel,
        out_shape=jax.ShapeDtypeStruct((tiles, ROWS, users), jnp.float32),
        in_specs=[SMEM, VMEM, VMEM],
        out_specs=VMEM,
        compiler_params=limit(4),
        cost_estimate=pl.CostEstimate(flops=10**7, bytes_accessed=2 * 10**7, transcendentals=0),
        name="contexts",
    )(in_hbm(cblock), table, marks)


def pack_places(me):
    return {
        (core, plane): jnp.bitwise_xor(lax.rem(me, CHUNKS), core + 2 * plane)
        for core in range(2)
        for plane in range(4)
    }


PIECES = [(core, plane) for core in (1, 0) for plane in (3, 1, 2, 0)]


def pack_rows(ranks):
    groups = ranks // LANES
    return (groups * (groups + 1) // 2 + groups) * LANES


def tiles_kernel(
    where_ref, count_ref, me_ref, blocks_ref, weights_ref, context_ref, basis_ref, *refs
):
    piece_refs, refs = refs[: len(PIECES)], refs[len(PIECES) :]
    stack_ref, y_ref, square_ref, pack_ref, even_ref, odd_ref = refs[:6]
    weights_held, context_held, basis_held, weights_sem, context_sem, basis_sem = refs[6:]
    rank_c, rank_i, users = y_ref.shape
    batches = weights_ref.shape[0] // BATCH
    half = rank_c // 2

    def copies(batch):
        rows = pl.ds(batch * BATCH, BATCH)
        return (
            pltpu.make_async_copy(weights_ref.at[rows], weights_held.at[rows], weights_sem.at[batch]),
            pltpu.make_async_copy(context_ref.at[rows], context_held.at[rows], context_sem.at[batch]),
        )

    def start(batch):
        for copy in copies(batch):
            copy.start()

    def wait(batch):
        for copy in copies(batch):
            copy.wait()

    start(0)

    def multiply(batch, place, into_ref):
        tile = batch * BATCH + place
        product = dot(blocks_ref[where_ref[tile]], weights_held[tile])
        into_ref[place] = product.astype(jnp.bfloat16).astype(jnp.float32)

    def add(batch, part, from_ref):
        lanes = slice(part // 2 * LANES, (part // 2 + 1) * LANES)
        ranks = range(part % 2 * half, (part % 2 + 1) * half)
        strips = [slice(i, i + ROWS) for i in range(0, rank_i, ROWS)]
        totals = [[y_ref[r, strip, lanes] for strip in strips] for r in ranks]
        for place in range(BATCH):
            parts_of = [from_ref[place, strip, lanes] for strip in strips]
            for i, r in enumerate(ranks):
                values = context_held[batch * BATCH + place, r : r + 1, lanes]
                values = jnp.broadcast_to(values, (ROWS, LANES))
                for j in range(len(strips)):
                    totals[i][j] = totals[i][j] + values * parts_of[j]
        for i, r in enumerate(ranks):
            for strip, total in zip(strips, totals[i]):
                y_ref[r, strip, lanes] = total

    y_ref[...] = jnp.zeros_like(y_ref)
    parts = 2 * users // LANES
    wait(0)
    start(1)
    for place in range(BATCH):
        multiply(0, place, even_ref)

    def turn(batch, from_ref, into_ref):
        wait(batch + 1)

        @pl.when(batch + 2 < batches)
        def _():
            start(batch + 2)

        for part in range(max(parts, BATCH)):
            if part < BATCH:
                multiply(batch + 1, part, into_ref)
            if part < parts:
                add(batch, part, from_ref)

    def pair(index, _):
        turn(2 * index, even_ref, odd_ref)
        turn(2 * index + 1, odd_ref, even_ref)
        return 0

    lax.fori_loop(0, batches // 2 - 1, pair, 0)
    basis_copy = pltpu.make_async_copy(basis_ref, basis_held, basis_sem)
    basis_copy.start()
    turn(batches - 2, even_ref, odd_ref)
    for part in range(parts):
        add(batches - 1, part, odd_ref)

    living = lax.broadcasted_iota(jnp.int32, (rank_i, users), 1) < count_ref[0]
    ranks = rank_c * rank_i
    for r in range(rank_c):
        high, low = split(jnp.where(living, y_ref[r], 0.0))
        stack_ref[r * rank_i : (r + 1) * rank_i] = high
        stack_ref[ranks + r * rank_i : ranks + (r + 1) * rank_i] = low
    square_ref[...] = dot_nt(stack_ref[...], stack_ref[:ranks])
    basis_copy.wait()
    projection = dot(stack_ref[...], jnp.concatenate(split(basis_held[...]), axis=1))
    groups = ranks // LANES
    place = 0
    for i in range(groups):
        rows = slice(i * LANES, (i + 1) * LANES)
        low_rows = slice(ranks + i * LANES, ranks + (i + 1) * LANES)
        for j in range(i, groups):
            lanes = slice(j * LANES, (j + 1) * LANES)
            low_lanes = slice(ranks + j * LANES, ranks + (j + 1) * LANES)
            block = square_ref[rows, lanes] + square_ref[low_rows, lanes] + square_ref[low_lanes, rows].T
            pack_ref[place * LANES : (place + 1) * LANES] = block
            place += 1
    pack_ref[place * LANES : (place + groups) * LANES] = quarters(projection)
    chunk = piece_refs[0].shape[0]
    places = pack_places(me_ref[0])
    for piece, ref in zip(PIECES, piece_refs):
        ref[...] = pack_ref[pl.ds(pl.multiple_of(places[piece] * chunk, ROWS), chunk)]


def tile_sums(where, count, me, blocks, weights, contexts, user_basis):
    tiles, _, users = weights.shape
    rank_i = blocks.shape[1]
    rank_c = contexts.shape[1]
    ranks = rank_c * rank_i
    rows = pack_rows(ranks)
    out_shape = (jax.ShapeDtypeStruct((rows // CHUNKS, LANES), jnp.float32),) * len(PIECES)
    out_shape += (jax.ShapeDtypeStruct((2 * ranks, users), jnp.bfloat16),)
    held = 3 * weights.size * 2 // (2 * MIB)
    out = pl.pallas_call(
        tiles_kernel,
        out_shape=out_shape,
        in_specs=[SMEM] * 3 + [VMEM] + [ANY] * 3,
        out_specs=(VMEM,) * len(out_shape),
        scratch_shapes=[
            pltpu.VMEM((rank_c, rank_i, users), jnp.float32),
            pltpu.VMEM((2 * ranks, ranks), jnp.float32),
            pltpu.VMEM((rows, LANES), jnp.float32),
            pltpu.VMEM((BATCH, rank_i, users), jnp.float32),
            pltpu.VMEM((BATCH, rank_i, users), jnp.float32),
            pltpu.VMEM(weights.shape, weights.dtype),
            pltpu.VMEM(contexts.shape, contexts.dtype),
            pltpu.VMEM(user_basis.shape, user_basis.dtype),
            pltpu.SemaphoreType.DMA((tiles // BATCH,)),
            pltpu.SemaphoreType.DMA((tiles // BATCH,)),
            pltpu.SemaphoreType.DMA,
        ],
        compiler_params=limit(12 + held),
        cost_estimate=pl.CostEstimate(flops=2 * 10**9, bytes_accessed=12 * 10**6, transcendentals=0),
        name="tile_sums",
    )(where, count, me, blocks, in_hbm(weights), in_hbm(contexts), in_hbm(user_basis))
    return dict(zip(PIECES, out[:-1])), out[-1]


def inverse_factor(gram, between):
    order = gram.shape[0]
    panels = order // ROWS
    sub = lax.broadcasted_iota(jnp.int32, (ROWS, order), 0)
    lane = lax.broadcasted_iota(jnp.int32, (ROWS, order), 1)
    left = [gram[ROWS * i : ROWS * (i + 1)] for i in range(panels)]
    right = [jnp.where(lane == sub + ROWS * i, 1.0, 0.0) for i in range(panels)]
    for k in range(panels):
        between(k)
        columns = {
            i: [
                jnp.broadcast_to(left[i][:, ROWS * k + j : ROWS * k + j + 1], (ROWS, order))
                for j in range(ROWS)
            ]
            for i in range(k, panels)
        }
        row, tail = left[k], right[k]
        scale = jnp.zeros((ROWS, order), jnp.float32)
        rows, tails = [], []
        for j in range(ROWS):
            head = columns[k][j]
            pivot = jnp.broadcast_to(head[j : j + 1], (ROWS, order))
            inverse = pl.reciprocal(pivot, approx=True)
            inverse = inverse * (2.0 - pivot * inverse)
            scale = jnp.where(sub == j, pivot, scale)
            rows.append(jnp.broadcast_to(row[j : j + 1], (ROWS, order)))
            tails.append(jnp.broadcast_to(tail[j : j + 1], (ROWS, order)))
            below = jnp.where(sub > j, head, 0.0) * inverse
            row = row - below * rows[j]
            tail = tail - below * tails[j]
            facts = {k: below}
            for i in range(k + 1, panels):
                facts[i] = columns[i][j] * inverse
            for c in range(j + 1, ROWS):
                crossing = jnp.broadcast_to(head[c : c + 1], (ROWS, order))
                for i in range(k, panels):
                    columns[i][c] = columns[i][c] - facts[i] * crossing
            for i in range(k + 1, panels):
                left[i] = left[i] - facts[i] * rows[j]
                right[i] = right[i] - facts[i] * tails[j]
        right[k] = tail * lax.rsqrt(scale)
    return jnp.concatenate(right, axis=0)


def finish_kernel(total_users, me_ref, stack_ref, *rest):
    piece_refs, rest = rest[: len(PIECES)], rest[len(PIECES) :]
    basis_ref, core_out_ref, pack_ref, full_ref, high_ref, low_ref = rest
    chunk = piece_refs[0].shape[0]
    places = pack_places(me_ref[0])
    for piece, ref in zip(PIECES, piece_refs):
        pack_ref[pl.ds(pl.multiple_of(places[piece] * chunk, ROWS), chunk)] = ref[...]
    ranks = full_ref.shape[1]
    groups = ranks // LANES
    place = 0
    for i in range(groups):
        for j in range(i, groups):
            block = pack_ref[place * LANES : (place + 1) * LANES]
            for row, lane, part in ((i, j, block), (j, i, block.T))[: 1 if i == j else 2]:
                lanes = slice(lane * LANES, (lane + 1) * LANES)
                high, low = split(part)
                full_ref[row * LANES : (row + 1) * LANES, lanes] = high
                full_ref[ranks + row * LANES : ranks + (row + 1) * LANES, lanes] = low
            place += 1
    projection = pack_ref[place * LANES : (place + groups) * LANES]
    crossed = quarters(dot(full_ref[...], jnp.concatenate(split(projection), axis=1)))
    crossed_high, crossed_low = split(crossed)
    turned = jnp.concatenate(
        [projection[i * LANES : (i + 1) * LANES].T for i in range(groups)], axis=1
    )
    turned_stack = jnp.concatenate(split(turned), axis=0)
    gram = quarters(dot(turned_stack, jnp.concatenate([crossed_high, crossed_low], axis=1)))
    strips = basis_ref.shape[0] // LANES

    def project(k):
        if k % 3 == 0 and k // 3 < strips:
            lanes = slice(k // 3 * LANES, (k // 3 + 1) * LANES)
            part = thrice(turned_stack, stack_ref[:ranks, lanes], stack_ref[ranks:, lanes], dot)
            high_ref[:, lanes], low_ref[:, lanes] = split(part)

    inverse_stack = jnp.concatenate(split(inverse_factor(gram, project)), axis=0)
    root = total_users ** 0.5
    scaled = thrice(inverse_stack, high_ref[...], low_ref[...], dot) * root
    for i in range(scaled.shape[1] // LANES):
        basis_ref[i * LANES : (i + 1) * LANES] = scaled[:, i * LANES : (i + 1) * LANES].T
    core_out_ref[...] = thrice(inverse_stack, crossed_high, crossed_low, dot_nt) * (1.0 / root)


def finish(me, stack, pieces, devices):
    ranks, users = stack.shape[0] // 2, stack.shape[1]
    return pl.pallas_call(
        functools.partial(finish_kernel, users * devices),
        out_shape=(
            jax.ShapeDtypeStruct((users, LANES), jnp.float32),
            jax.ShapeDtypeStruct((LANES, ranks), jnp.float32),
        ),
        in_specs=[SMEM] + [VMEM] * (1 + len(PIECES)),
        out_specs=(VMEM, VMEM),
        scratch_shapes=[
            pltpu.VMEM((pack_rows(ranks), LANES), jnp.float32),
            pltpu.VMEM((2 * ranks, ranks), jnp.bfloat16),
            pltpu.VMEM((LANES, users), jnp.bfloat16),
            pltpu.VMEM((LANES, users), jnp.bfloat16),
        ],
        compiler_params=limit(16),
        name="finish",
    )(me, stack, *[pieces[piece] for piece in PIECES])


def swap(value, mask, devices):
    return lax.ppermute(value, "users", [(i, i ^ mask) for i in range(devices)])


def encode(value):
    rows, lanes = value.shape
    groups = rows // GROUP
    parts = value.reshape(groups, GROUP, lanes)
    most = jnp.max(jnp.abs(parts), axis=1, keepdims=True)
    exponent = jnp.clip(jnp.floor(jnp.log2(most)) + 1.0, -110.0, 128.0)
    coded = jnp.clip(jnp.round(parts * jnp.exp2(14.0 - exponent)), -32767.0, 32767.0)
    extra = jnp.pad(exponent.reshape(groups, lanes), ((0, -groups % 16), (0, 0)))
    return jnp.concatenate([coded.reshape(rows, lanes), extra], axis=0).astype(jnp.int16)


def decode(coded, rows):
    lanes = coded.shape[1]
    groups = rows // GROUP
    scale = jnp.exp2(coded[rows : rows + groups].astype(jnp.float32) - 14.0)
    parts = coded[:rows].astype(jnp.float32).reshape(groups, GROUP, lanes)
    return (parts * scale.reshape(groups, 1, lanes)).reshape(rows, lanes)


def reduce_pieces(pieces, devices):
    rows = pieces[0, 0].shape[0]
    got = {plane: swap(pieces[1, plane], 1, devices) for plane in (3, 1, 2, 0)}
    total = pieces[0, 0] + got[0]
    for plane in (3, 1, 2):
        coded = encode(pieces[0, plane] + got[plane])
        total = total + decode(swap(coded, 2 * plane, devices), rows)
    mask = CHUNKS
    while mask < devices:
        coded = encode(total)
        total = decode(coded, rows) + decode(swap(coded, mask, devices), rows)
        mask *= 2
    return encode(total)


def spread_pieces(total, devices, rows):
    coded = {(0, 0): total}
    for plane in (3, 1, 2):
        coded[0, plane] = swap(total, 2 * plane, devices)
    for plane in (0, 3, 1, 2):
        coded[1, plane] = swap(coded[0, plane], 1, devices)
    return {piece: decode(value, rows) for piece, value in coded.items()}


def body(
    tile_owner, tile_slot, tile_cblock, tile_context, tile_weights,
    item_factors, context_factors, user_basis, user_counts,
):
    devices = lax.axis_size("users")
    half = devices // 2
    rank_c = context_factors.shape[0]
    me = lax.axis_index("users").astype(jnp.int32).reshape(1)

    mirror = swap(item_factors, half, devices)
    requests, where, own = route(me, tile_owner[:, 0], tile_slot, item_factors, half)
    sides = [list(range(half)), list(range(half, devices))]
    asked = lax.all_to_all(requests, "users", 0, 0, axis_index_groups=sides, tiled=True)
    found = collect(asked, own, mirror)
    found, cblock, factors = lax.optimization_barrier((found, tile_cblock, context_factors))
    blocks = lax.all_to_all(found, "users", 0, 0, axis_index_groups=sides, tiled=True)

    table = factors.astype(jnp.float32).reshape(rank_c, -1, CB).transpose(1, 0, 2)
    contexts = context_values(cblock, table, tile_context)
    pieces, stack = tile_sums(
        where, user_counts, me, blocks, tile_weights, contexts, user_basis
    )
    rows = pieces[0, 0].shape[0]
    pieces = spread_pieces(reduce_pieces(pieces, devices), devices, rows)
    return finish(me, stack, pieces, devices)


def solution(mesh):
    return jax.shard_map(
        body,
        mesh=mesh,
        in_specs=(
            P("users", None), P("users"), P("users"), P("users", None), P("users", None, None),
            P("users", None, None), P(), P("users", None), P("users"),
        ),
        out_specs=(P("users", None), P()),
        check_vma=False,
    )
```

```python
import functools

import jax
import jax.numpy as jnp
from jax import lax
from jax.experimental import pallas as pl
from jax.experimental.pallas import tpu as pltpu
from jax.sharding import PartitionSpec as P

CB = 8
SLOTS = 2
PLACES = 2 * SLOTS
LANES = 128
ROWS = 8
BATCH = 8
CHUNKS = 8
GROUP = 32
MIB = 2**20

SMEM = pl.BlockSpec(memory_space=pltpu.SMEM)
VMEM = pl.BlockSpec(memory_space=pltpu.VMEM)
ANY = pl.BlockSpec(memory_space=pl.ANY)


def in_hbm(value):
    return pltpu.with_memory_space_constraint(value, pltpu.HBM)


def limit(mib):
    return pltpu.CompilerParams(vmem_limit_bytes=mib * MIB)


def dot(lhs, rhs):
    return jnp.dot(lhs, rhs, preferred_element_type=jnp.float32)


def dot_nt(lhs, rhs):
    return lax.dot_general(lhs, rhs, (((1,), (1,)), ((), ())), preferred_element_type=jnp.float32)


def split(value):
    high = value.astype(jnp.bfloat16)
    return high, (value - high.astype(jnp.float32)).astype(jnp.bfloat16)


def quarters(value):
    rows, lanes = value.shape[0] // 2, value.shape[1] // 2
    return (value[:rows, :lanes] + value[:rows, lanes:]) + (value[rows:, :lanes] + value[rows:, lanes:])


def thrice(stack, high, low, product):
    rows = stack.shape[0] // 2
    first = product(stack, high)
    return first[:rows] + (first[rows:] + product(stack[:rows], low))


def route_kernel(half, me_ref, owner_ref, slot_ref, own_ref, request_ref, where_ref, held_ref, used_ref, sem_ref):
    copy = pltpu.make_async_copy(own_ref, held_ref, sem_ref)
    copy.start()
    side = me_ref[0] // half
    lane = lax.broadcasted_iota(jnp.int32, (1, LANES), 1)

    def clear(place, _):
        used_ref[place] = 0
        return 0

    lax.fori_loop(0, 2 * half, clear, 0, unroll=8)
    request_ref[...] = jnp.zeros_like(request_ref)

    def assign(tile, _):
        owner = owner_ref[tile]
        taken = used_ref[owner]
        used_ref[owner] = taken + 1
        low = lax.rem(owner, half)
        place = jnp.where(owner // half == side, 0, SLOTS) + taken
        request_ref[low] = jnp.where(lane == place, slot_ref[tile], request_ref[low])
        where_ref[tile] = low * PLACES + place
        return 0

    lax.fori_loop(0, owner_ref.shape[0], assign, 0, unroll=4)
    copy.wait()


def route(me, owners, slots, own, half):
    return pl.pallas_call(
        functools.partial(route_kernel, half),
        out_shape=(
            jax.ShapeDtypeStruct((half, 1, LANES), jnp.int32),
            jax.ShapeDtypeStruct(owners.shape, jnp.int32),
            jax.ShapeDtypeStruct(own.shape, own.dtype),
        ),
        in_specs=[SMEM, SMEM, SMEM, ANY],
        out_specs=(VMEM, SMEM, VMEM),
        scratch_shapes=[pltpu.SMEM((2 * half,), jnp.int32), pltpu.SemaphoreType.DMA],
        compiler_params=limit(4),
        name="route",
    )(me, in_hbm(owners), in_hbm(slots), in_hbm(own))


def collect_kernel(asked_ref, own_ref, mirror_ref, out_ref):
    for peer in range(asked_ref.shape[0]):
        for place in range(PLACES):
            source = own_ref if place < SLOTS else mirror_ref
            out_ref[peer * PLACES + place] = source[asked_ref[peer, 0, place]]


def collect(asked, own, mirror):
    return pl.pallas_call(
        collect_kernel,
        out_shape=jax.ShapeDtypeStruct((asked.shape[0] * PLACES,) + own.shape[1:], own.dtype),
        in_specs=[SMEM, VMEM, VMEM],
        out_specs=VMEM,
        compiler_params=limit(4),
        name="collect",
    )(asked, own, mirror)


def context_kernel(cblock_ref, table_ref, marks_ref, context_ref):
    tiles, users = marks_ref.shape

    def one(tile, _):
        table = table_ref[cblock_ref[tile]]
        marks = jnp.broadcast_to(marks_ref[pl.ds(tile, 1), :], (ROWS, users))
        total = jnp.zeros((ROWS, users), jnp.float32)
        for k in range(CB):
            column = jnp.broadcast_to(table[:, k : k + 1], (ROWS, users))
            total = jnp.where(marks == k, column, total)
        context_ref[tile] = total
        return 0

    lax.fori_loop(0, tiles, one, 0, unroll=2)


def context_values(cblock, table, marks):
    tiles, users = marks.shape
    return pl.pallas_call(
        context_kernel,
        out_shape=jax.ShapeDtypeStruct((tiles, ROWS, users), jnp.float32),
        in_specs=[SMEM, VMEM, VMEM],
        out_specs=VMEM,
        compiler_params=limit(4),
        cost_estimate=pl.CostEstimate(flops=10**7, bytes_accessed=2 * 10**7, transcendentals=0),
        name="contexts",
    )(in_hbm(cblock), table, marks)


def pack_places(me):
    return {
        (core, plane): jnp.bitwise_xor(lax.rem(me, CHUNKS), core + 2 * plane)
        for core in range(2)
        for plane in range(4)
    }


PIECES = [(core, plane) for core in (1, 0) for plane in (3, 1, 2, 0)]


def pack_rows(ranks):
    groups = ranks // LANES
    return (groups * (groups + 1) // 2 + groups) * LANES


def tiles_kernel(
    where_ref, count_ref, me_ref, blocks_ref, weights_ref, context_ref, basis_ref, *refs
):
    piece_refs, refs = refs[: len(PIECES)], refs[len(PIECES) :]
    stack_ref, y_ref, square_ref, pack_ref, even_ref, odd_ref = refs[:6]
    weights_held, context_held, basis_held, weights_sem, context_sem, basis_sem = refs[6:]
    rank_c, rank_i, users = y_ref.shape
    batches = weights_ref.shape[0] // BATCH
    half = rank_c // 2

    def copies(batch):
        rows = pl.ds(batch * BATCH, BATCH)
        tiles = [batch * BATCH + place for place in range(BATCH)]
        return [
            pltpu.make_async_copy(weights_ref.at[tile], weights_held.at[tile], weights_sem.at[tile]) for tile in tiles
        ] + [pltpu.make_async_copy(context_ref.at[rows], context_held.at[rows], context_sem.at[batch])]

    def start(batch):
        for copy in copies(batch):
            copy.start()

    def wait(batch):
        for copy in copies(batch):
            copy.wait()

    start(0)
    start(1)

    def multiply(batch, place, into_ref):
        tile = batch * BATCH + place
        product = dot(blocks_ref[where_ref[tile]], weights_held[tile])
        into_ref[place] = product.astype(jnp.bfloat16).astype(jnp.float32)

    def add(batch, part, from_ref):
        lanes = slice(part // 2 * LANES, (part // 2 + 1) * LANES)
        ranks = range(part % 2 * half, (part % 2 + 1) * half)
        strips = [slice(i, i + ROWS) for i in range(0, rank_i, ROWS)]
        totals = [[y_ref[r, strip, lanes] for strip in strips] for r in ranks]
        for place in range(BATCH):
            parts_of = [from_ref[place, strip, lanes] for strip in strips]
            for i, r in enumerate(ranks):
                values = context_held[batch * BATCH + place, r : r + 1, lanes]
                values = jnp.broadcast_to(values, (ROWS, LANES))
                for j in range(len(strips)):
                    totals[i][j] = totals[i][j] + values * parts_of[j]
        for i, r in enumerate(ranks):
            for strip, total in zip(strips, totals[i]):
                y_ref[r, strip, lanes] = total

    y_ref[...] = jnp.zeros_like(y_ref)
    parts = 2 * users // LANES
    wait(0)
    start(2)
    for place in range(BATCH):
        multiply(0, place, even_ref)

    def turn(batch, from_ref, into_ref):
        wait(batch + 1)

        @pl.when(batch + 3 < batches)
        def _():
            start(batch + 3)

        for part in range(max(parts, BATCH)):
            if part < BATCH:
                multiply(batch + 1, part, into_ref)
            if part < parts:
                add(batch, part, from_ref)

    def pair(index, _):
        turn(2 * index, even_ref, odd_ref)
        turn(2 * index + 1, odd_ref, even_ref)
        return 0

    lax.fori_loop(0, batches // 2 - 1, pair, 0)
    basis_copy = pltpu.make_async_copy(basis_ref, basis_held, basis_sem)
    basis_copy.start()
    turn(batches - 2, even_ref, odd_ref)
    for part in range(parts):
        add(batches - 1, part, odd_ref)

    living = lax.broadcasted_iota(jnp.int32, (rank_i, users), 1) < count_ref[0]
    ranks = rank_c * rank_i
    for r in range(rank_c):
        high, low = split(jnp.where(living, y_ref[r], 0.0))
        stack_ref[r * rank_i : (r + 1) * rank_i] = high
        stack_ref[ranks + r * rank_i : ranks + (r + 1) * rank_i] = low
    square_ref[...] = dot_nt(stack_ref[...], stack_ref[:ranks])
    basis_copy.wait()
    projection = dot(stack_ref[...], jnp.concatenate(split(basis_held[...]), axis=1))
    groups = ranks // LANES
    place = 0
    for i in range(groups):
        rows = slice(i * LANES, (i + 1) * LANES)
        low_rows = slice(ranks + i * LANES, ranks + (i + 1) * LANES)
        for j in range(i, groups):
            lanes = slice(j * LANES, (j + 1) * LANES)
            low_lanes = slice(ranks + j * LANES, ranks + (j + 1) * LANES)
            block = square_ref[rows, lanes] + square_ref[low_rows, lanes] + square_ref[low_lanes, rows].T
            pack_ref[place * LANES : (place + 1) * LANES] = block
            place += 1
    pack_ref[place * LANES : (place + groups) * LANES] = quarters(projection)
    chunk = piece_refs[0].shape[0]
    places = pack_places(me_ref[0])
    for piece, ref in zip(PIECES, piece_refs):
        ref[...] = pack_ref[pl.ds(pl.multiple_of(places[piece] * chunk, ROWS), chunk)]


def tile_sums(where, count, me, blocks, weights, contexts, user_basis):
    tiles, _, users = weights.shape
    rank_i = blocks.shape[1]
    rank_c = contexts.shape[1]
    ranks = rank_c * rank_i
    rows = pack_rows(ranks)
    out_shape = (jax.ShapeDtypeStruct((rows // CHUNKS, LANES), jnp.float32),) * len(PIECES)
    out_shape += (jax.ShapeDtypeStruct((2 * ranks, users), jnp.bfloat16),)
    held = 3 * weights.size * 2 // (2 * MIB)
    out = pl.pallas_call(
        tiles_kernel,
        out_shape=out_shape,
        in_specs=[SMEM] * 3 + [VMEM] + [ANY] * 3,
        out_specs=(VMEM,) * len(out_shape),
        scratch_shapes=[
            pltpu.VMEM((rank_c, rank_i, users), jnp.float32),
            pltpu.VMEM((2 * ranks, ranks), jnp.float32),
            pltpu.VMEM((rows, LANES), jnp.float32),
            pltpu.VMEM((BATCH, rank_i, users), jnp.float32),
            pltpu.VMEM((BATCH, rank_i, users), jnp.float32),
            pltpu.VMEM(weights.shape, weights.dtype),
            pltpu.VMEM(contexts.shape, contexts.dtype),
            pltpu.VMEM(user_basis.shape, user_basis.dtype),
            pltpu.SemaphoreType.DMA((tiles,)),
            pltpu.SemaphoreType.DMA((tiles // BATCH,)),
            pltpu.SemaphoreType.DMA,
        ],
        compiler_params=limit(12 + held),
        cost_estimate=pl.CostEstimate(flops=2 * 10**9, bytes_accessed=12 * 10**6, transcendentals=0),
        name="tile_sums",
    )(where, count, me, blocks, in_hbm(weights), in_hbm(contexts), in_hbm(user_basis))
    return dict(zip(PIECES, out[:-1])), out[-1]


def inverse_factor(gram, between):
    order = gram.shape[0]
    panels = order // ROWS
    sub = lax.broadcasted_iota(jnp.int32, (ROWS, order), 0)
    lane = lax.broadcasted_iota(jnp.int32, (ROWS, order), 1)
    left = [gram[ROWS * i : ROWS * (i + 1)] for i in range(panels)]
    right = [jnp.where(lane == sub + ROWS * i, 1.0, 0.0) for i in range(panels)]
    for k in range(panels):
        between(k)
        columns = {
            i: [
                jnp.broadcast_to(left[i][:, ROWS * k + j : ROWS * k + j + 1], (ROWS, order))
                for j in range(ROWS)
            ]
            for i in range(k, panels)
        }
        row, tail = left[k], right[k]
        scale = jnp.zeros((ROWS, order), jnp.float32)
        rows, tails = [], []
        for j in range(ROWS):
            head = columns[k][j]
            pivot = jnp.broadcast_to(head[j : j + 1], (ROWS, order))
            inverse = pl.reciprocal(pivot, approx=True)
            inverse = inverse * (2.0 - pivot * inverse)
            scale = jnp.where(sub == j, pivot, scale)
            rows.append(jnp.broadcast_to(row[j : j + 1], (ROWS, order)))
            tails.append(jnp.broadcast_to(tail[j : j + 1], (ROWS, order)))
            below = jnp.where(sub > j, head, 0.0) * inverse
            row = row - below * rows[j]
            tail = tail - below * tails[j]
            facts = {k: below}
            for i in range(k + 1, panels):
                facts[i] = columns[i][j] * inverse
            for c in range(j + 1, ROWS):
                crossing = jnp.broadcast_to(head[c : c + 1], (ROWS, order))
                for i in range(k, panels):
                    columns[i][c] = columns[i][c] - facts[i] * crossing
            for i in range(k + 1, panels):
                left[i] = left[i] - facts[i] * rows[j]
                right[i] = right[i] - facts[i] * tails[j]
        right[k] = tail * lax.rsqrt(scale)
    return jnp.concatenate(right, axis=0)


def finish_kernel(total_users, me_ref, stack_ref, *rest):
    piece_refs, rest = rest[: len(PIECES)], rest[len(PIECES) :]
    basis_ref, core_out_ref, pack_ref, full_ref, high_ref, low_ref = rest
    chunk = piece_refs[0].shape[0]
    places = pack_places(me_ref[0])
    for piece, ref in zip(PIECES, piece_refs):
        pack_ref[pl.ds(pl.multiple_of(places[piece] * chunk, ROWS), chunk)] = ref[...]
    ranks = full_ref.shape[1]
    groups = ranks // LANES
    place = 0
    for i in range(groups):
        for j in range(i, groups):
            block = pack_ref[place * LANES : (place + 1) * LANES]
            for row, lane, part in ((i, j, block), (j, i, block.T))[: 1 if i == j else 2]:
                lanes = slice(lane * LANES, (lane + 1) * LANES)
                high, low = split(part)
                full_ref[row * LANES : (row + 1) * LANES, lanes] = high
                full_ref[ranks + row * LANES : ranks + (row + 1) * LANES, lanes] = low
            place += 1
    projection = pack_ref[place * LANES : (place + groups) * LANES]
    crossed = quarters(dot(full_ref[...], jnp.concatenate(split(projection), axis=1)))
    crossed_high, crossed_low = split(crossed)
    turned = jnp.concatenate(
        [projection[i * LANES : (i + 1) * LANES].T for i in range(groups)], axis=1
    )
    turned_stack = jnp.concatenate(split(turned), axis=0)
    gram = quarters(dot(turned_stack, jnp.concatenate([crossed_high, crossed_low], axis=1)))
    strips = basis_ref.shape[0] // LANES

    def project(k):
        if k % 3 == 0 and k // 3 < strips:
            lanes = slice(k // 3 * LANES, (k // 3 + 1) * LANES)
            part = thrice(turned_stack, stack_ref[:ranks, lanes], stack_ref[ranks:, lanes], dot)
            high_ref[:, lanes], low_ref[:, lanes] = split(part)

    inverse_stack = jnp.concatenate(split(inverse_factor(gram, project)), axis=0)
    root = total_users ** 0.5
    scaled = thrice(inverse_stack, high_ref[...], low_ref[...], dot) * root
    for i in range(scaled.shape[1] // LANES):
        basis_ref[i * LANES : (i + 1) * LANES] = scaled[:, i * LANES : (i + 1) * LANES].T
    core_out_ref[...] = thrice(inverse_stack, crossed_high, crossed_low, dot_nt) * (1.0 / root)


def finish(me, stack, pieces, devices):
    ranks, users = stack.shape[0] // 2, stack.shape[1]
    return pl.pallas_call(
        functools.partial(finish_kernel, users * devices),
        out_shape=(
            jax.ShapeDtypeStruct((users, LANES), jnp.float32),
            jax.ShapeDtypeStruct((LANES, ranks), jnp.float32),
        ),
        in_specs=[SMEM] + [VMEM] * (1 + len(PIECES)),
        out_specs=(VMEM, VMEM),
        scratch_shapes=[
            pltpu.VMEM((pack_rows(ranks), LANES), jnp.float32),
            pltpu.VMEM((2 * ranks, ranks), jnp.bfloat16),
            pltpu.VMEM((LANES, users), jnp.bfloat16),
            pltpu.VMEM((LANES, users), jnp.bfloat16),
        ],
        compiler_params=limit(16),
        name="finish",
    )(me, stack, *[pieces[piece] for piece in PIECES])


def swap(value, mask, devices):
    return lax.ppermute(value, "users", [(i, i ^ mask) for i in range(devices)])


def encode(value):
    rows, lanes = value.shape
    groups = rows // GROUP
    parts = value.reshape(groups, GROUP, lanes)
    most = jnp.max(jnp.abs(parts), axis=1, keepdims=True)
    exponent = jnp.clip(jnp.floor(jnp.log2(most)) + 1.0, -110.0, 128.0)
    coded = jnp.clip(jnp.round(parts * jnp.exp2(14.0 - exponent)), -32767.0, 32767.0)
    extra = jnp.pad(exponent.reshape(groups, lanes), ((0, -groups % 16), (0, 0)))
    return jnp.concatenate([coded.reshape(rows, lanes), extra], axis=0).astype(jnp.int16)


def decode(coded, rows):
    lanes = coded.shape[1]
    groups = rows // GROUP
    scale = jnp.exp2(coded[rows : rows + groups].astype(jnp.float32) - 14.0)
    parts = coded[:rows].astype(jnp.float32).reshape(groups, GROUP, lanes)
    return (parts * scale.reshape(groups, 1, lanes)).reshape(rows, lanes)


def reduce_pieces(pieces, devices):
    rows = pieces[0, 0].shape[0]
    got = {plane: swap(pieces[1, plane], 1, devices) for plane in (3, 1, 2, 0)}
    total = pieces[0, 0] + got[0]
    for plane in (3, 1, 2):
        coded = encode(pieces[0, plane] + got[plane])
        total = total + decode(swap(coded, 2 * plane, devices), rows)
    mask = CHUNKS
    while mask < devices:
        coded = encode(total)
        total = decode(coded, rows) + decode(swap(coded, mask, devices), rows)
        mask *= 2
    return encode(total)


def spread_pieces(total, devices, rows):
    coded = {(0, 0): total}
    for plane in (3, 1, 2):
        coded[0, plane] = swap(total, 2 * plane, devices)
    for plane in (0, 3, 1, 2):
        coded[1, plane] = swap(coded[0, plane], 1, devices)
    return {piece: decode(value, rows) for piece, value in coded.items()}


def body(
    tile_owner, tile_slot, tile_cblock, tile_context, tile_weights,
    item_factors, context_factors, user_basis, user_counts,
):
    devices = lax.axis_size("users")
    half = devices // 2
    rank_c = context_factors.shape[0]
    me = lax.axis_index("users").astype(jnp.int32).reshape(1)

    mirror = swap(item_factors, half, devices)
    requests, where, own = route(me, tile_owner[:, 0], tile_slot, item_factors, half)
    sides = [list(range(half)), list(range(half, devices))]
    asked = lax.all_to_all(requests, "users", 0, 0, axis_index_groups=sides, tiled=True)
    found = collect(asked, own, mirror)
    found, cblock, factors = lax.optimization_barrier((found, tile_cblock, context_factors))
    blocks = lax.all_to_all(found, "users", 0, 0, axis_index_groups=sides, tiled=True)

    table = factors.astype(jnp.float32).reshape(rank_c, -1, CB).transpose(1, 0, 2)
    contexts = context_values(cblock, table, tile_context)
    pieces, stack = tile_sums(
        where, user_counts, me, blocks, tile_weights, contexts, user_basis
    )
    rows = pieces[0, 0].shape[0]
    pieces = spread_pieces(reduce_pieces(pieces, devices), devices, rows)
    return finish(me, stack, pieces, devices)


def solution(mesh):
    return jax.shard_map(
        body,
        mesh=mesh,
        in_specs=(
            P("users", None), P("users"), P("users"), P("users", None), P("users", None, None),
            P("users", None, None), P(), P("users", None), P("users"),
        ),
        out_specs=(P("users", None), P()),
        check_vma=False,
    )
```

```python
import functools

import jax
import jax.numpy as jnp
from jax import lax
from jax.experimental import pallas as pl
from jax.experimental.pallas import tpu as pltpu
from jax.sharding import PartitionSpec as P

CB = 8
SLOTS = 2
PLACES = 2 * SLOTS
LANES = 128
ROWS = 8
BATCH = 8
CHUNKS = 8
GROUP = 32
MIB = 2**20

SMEM = pl.BlockSpec(memory_space=pltpu.SMEM)
VMEM = pl.BlockSpec(memory_space=pltpu.VMEM)
ANY = pl.BlockSpec(memory_space=pl.ANY)


def in_hbm(value):
    return pltpu.with_memory_space_constraint(value, pltpu.HBM)


def limit(mib):
    return pltpu.CompilerParams(vmem_limit_bytes=mib * MIB)


def dot(lhs, rhs):
    return jnp.dot(lhs, rhs, preferred_element_type=jnp.float32)


def dot_nt(lhs, rhs):
    return lax.dot_general(lhs, rhs, (((1,), (1,)), ((), ())), preferred_element_type=jnp.float32)


def split(value):
    high = value.astype(jnp.bfloat16)
    return high, (value - high.astype(jnp.float32)).astype(jnp.bfloat16)


def quarters(value):
    rows, lanes = value.shape[0] // 2, value.shape[1] // 2
    return (value[:rows, :lanes] + value[:rows, lanes:]) + (value[rows:, :lanes] + value[rows:, lanes:])


def thrice(stack, high, low, product):
    rows = stack.shape[0] // 2
    first = product(stack, high)
    return first[:rows] + (first[rows:] + product(stack[:rows], low))


def route_kernel(half, me_ref, owner_ref, slot_ref, own_ref, request_ref, where_ref, held_ref, used_ref, sem_ref):
    copy = pltpu.make_async_copy(own_ref, held_ref, sem_ref)
    copy.start()
    side = me_ref[0] // half
    lane = lax.broadcasted_iota(jnp.int32, (1, LANES), 1)

    def clear(place, _):
        used_ref[place] = 0
        return 0

    lax.fori_loop(0, 2 * half, clear, 0, unroll=8)
    request_ref[...] = jnp.zeros_like(request_ref)

    def assign(tile, _):
        owner = owner_ref[tile]
        taken = used_ref[owner]
        used_ref[owner] = taken + 1
        low = lax.rem(owner, half)
        place = jnp.where(owner // half == side, 0, SLOTS) + taken
        request_ref[low] = jnp.where(lane == place, slot_ref[tile], request_ref[low])
        where_ref[tile] = low * PLACES + place
        return 0

    lax.fori_loop(0, owner_ref.shape[0], assign, 0, unroll=4)
    copy.wait()


def route(me, owners, slots, own, half):
    return pl.pallas_call(
        functools.partial(route_kernel, half),
        out_shape=(
            jax.ShapeDtypeStruct((half, 1, LANES), jnp.int32),
            jax.ShapeDtypeStruct(owners.shape, jnp.int32),
            jax.ShapeDtypeStruct(own.shape, own.dtype),
        ),
        in_specs=[SMEM, SMEM, SMEM, ANY],
        out_specs=(VMEM, SMEM, VMEM),
        scratch_shapes=[pltpu.SMEM((2 * half,), jnp.int32), pltpu.SemaphoreType.DMA],
        compiler_params=limit(4),
        name="route",
    )(me, in_hbm(owners), in_hbm(slots), in_hbm(own))


def collect_kernel(asked_ref, own_ref, mirror_ref, out_ref):
    for peer in range(asked_ref.shape[0]):
        for place in range(PLACES):
            source = own_ref if place < SLOTS else mirror_ref
            out_ref[peer * PLACES + place] = source[asked_ref[peer, 0, place]]


def collect(asked, own, mirror):
    return pl.pallas_call(
        collect_kernel,
        out_shape=jax.ShapeDtypeStruct((asked.shape[0] * PLACES,) + own.shape[1:], own.dtype),
        in_specs=[SMEM, VMEM, VMEM],
        out_specs=VMEM,
        compiler_params=limit(4),
        name="collect",
    )(asked, own, mirror)


def context_kernel(cblock_ref, table_ref, marks_ref, context_ref):
    tiles, users = marks_ref.shape

    def one(tile, _):
        table = table_ref[cblock_ref[tile]]
        marks = jnp.broadcast_to(marks_ref[pl.ds(tile, 1), :], (ROWS, users))
        total = jnp.zeros((ROWS, users), jnp.float32)
        for k in range(CB):
            column = jnp.broadcast_to(table[:, k : k + 1], (ROWS, users))
            total = jnp.where(marks == k, column, total)
        context_ref[tile] = total
        return 0

    lax.fori_loop(0, tiles, one, 0, unroll=2)


def context_values(cblock, table, marks):
    tiles, users = marks.shape
    return pl.pallas_call(
        context_kernel,
        out_shape=jax.ShapeDtypeStruct((tiles, ROWS, users), jnp.float32),
        in_specs=[SMEM, VMEM, VMEM],
        out_specs=VMEM,
        compiler_params=limit(4),
        cost_estimate=pl.CostEstimate(flops=10**7, bytes_accessed=2 * 10**7, transcendentals=0),
        name="contexts",
    )(in_hbm(cblock), table, marks)


def pack_places(me):
    return {
        (core, plane): jnp.bitwise_xor(lax.rem(me, CHUNKS), core + 2 * plane)
        for core in range(2)
        for plane in range(4)
    }


PIECES = [(core, plane) for core in (1, 0) for plane in (3, 1, 2, 0)]


def pack_rows(ranks):
    groups = ranks // LANES
    return (groups * (groups + 1) // 2 + groups) * LANES


def tiles_kernel(
    where_ref, count_ref, me_ref, blocks_ref, weights_ref, context_ref, basis_ref, *refs
):
    piece_refs, refs = refs[: len(PIECES)], refs[len(PIECES) :]
    stack_ref, y_ref, square_ref, pack_ref, even_ref, odd_ref = refs[:6]
    weights_held, context_held, basis_held, weights_sem, context_sem, basis_sem = refs[6:]
    rank_c, rank_i, users = y_ref.shape
    batches = weights_ref.shape[0] // BATCH
    half = rank_c // 2

    def copies(batch):
        rows = pl.ds(batch * BATCH, BATCH)
        tiles = [batch * BATCH + place for place in range(BATCH)]
        return [
            pltpu.make_async_copy(weights_ref.at[tile], weights_held.at[tile], weights_sem.at[tile]) for tile in tiles
        ] + [pltpu.make_async_copy(context_ref.at[rows], context_held.at[rows], context_sem.at[batch])]

    def start(batch):
        for copy in copies(batch):
            copy.start()

    def wait(batch):
        for copy in copies(batch):
            copy.wait()

    start(0)
    start(1)

    def multiply(batch, place, into_ref):
        tile = batch * BATCH + place
        into_ref[place] = dot(blocks_ref[where_ref[tile]], weights_held[tile])

    def add(batch, part, from_ref):
        lanes = slice(part // 2 * LANES, (part // 2 + 1) * LANES)
        ranks = range(part % 2 * half, (part % 2 + 1) * half)
        strips = [slice(i, i + ROWS) for i in range(0, rank_i, ROWS)]
        totals = [[y_ref[r, strip, lanes] for strip in strips] for r in ranks]
        for place in range(BATCH):
            parts_of = [from_ref[place, strip, lanes] for strip in strips]
            for i, r in enumerate(ranks):
                values = context_held[batch * BATCH + place, r : r + 1, lanes]
                values = jnp.broadcast_to(values, (ROWS, LANES))
                for j in range(len(strips)):
                    totals[i][j] = totals[i][j] + values * parts_of[j]
        for i, r in enumerate(ranks):
            for strip, total in zip(strips, totals[i]):
                y_ref[r, strip, lanes] = total

    y_ref[...] = jnp.zeros_like(y_ref)
    parts = 2 * users // LANES
    wait(0)
    start(2)
    for place in range(BATCH):
        multiply(0, place, even_ref)

    def turn(batch, from_ref, into_ref):
        wait(batch + 1)

        @pl.when(batch + 3 < batches)
        def _():
            start(batch + 3)

        for part in range(max(parts, BATCH)):
            if part < BATCH:
                multiply(batch + 1, part, into_ref)
            if part < parts:
                add(batch, part, from_ref)

    def pair(index, _):
        turn(2 * index, even_ref, odd_ref)
        turn(2 * index + 1, odd_ref, even_ref)
        return 0

    lax.fori_loop(0, batches // 2 - 1, pair, 0)
    basis_copy = pltpu.make_async_copy(basis_ref, basis_held, basis_sem)
    basis_copy.start()
    turn(batches - 2, even_ref, odd_ref)
    for part in range(parts):
        add(batches - 1, part, odd_ref)

    living = lax.broadcasted_iota(jnp.int32, (rank_i, users), 1) < count_ref[0]
    ranks = rank_c * rank_i
    for r in range(rank_c):
        high, low = split(jnp.where(living, y_ref[r], 0.0))
        stack_ref[r * rank_i : (r + 1) * rank_i] = high
        stack_ref[ranks + r * rank_i : ranks + (r + 1) * rank_i] = low
    square_ref[...] = dot_nt(stack_ref[...], stack_ref[:ranks])
    basis_copy.wait()
    projection = dot(stack_ref[...], jnp.concatenate(split(basis_held[...]), axis=1))
    groups = ranks // LANES
    place = 0
    for i in range(groups):
        rows = slice(i * LANES, (i + 1) * LANES)
        low_rows = slice(ranks + i * LANES, ranks + (i + 1) * LANES)
        for j in range(i, groups):
            lanes = slice(j * LANES, (j + 1) * LANES)
            low_lanes = slice(ranks + j * LANES, ranks + (j + 1) * LANES)
            block = square_ref[rows, lanes] + square_ref[low_rows, lanes] + square_ref[low_lanes, rows].T
            pack_ref[place * LANES : (place + 1) * LANES] = block
            place += 1
    pack_ref[place * LANES : (place + groups) * LANES] = quarters(projection)
    chunk = piece_refs[0].shape[0]
    places = pack_places(me_ref[0])
    for piece, ref in zip(PIECES, piece_refs):
        ref[...] = pack_ref[pl.ds(pl.multiple_of(places[piece] * chunk, ROWS), chunk)]


def tile_sums(where, count, me, blocks, weights, contexts, user_basis):
    tiles, _, users = weights.shape
    rank_i = blocks.shape[1]
    rank_c = contexts.shape[1]
    ranks = rank_c * rank_i
    rows = pack_rows(ranks)
    out_shape = (jax.ShapeDtypeStruct((rows // CHUNKS, LANES), jnp.float32),) * len(PIECES)
    out_shape += (jax.ShapeDtypeStruct((2 * ranks, users), jnp.bfloat16),)
    held = 3 * weights.size * 2 // (2 * MIB)
    out = pl.pallas_call(
        tiles_kernel,
        out_shape=out_shape,
        in_specs=[SMEM] * 3 + [VMEM] + [ANY] * 3,
        out_specs=(VMEM,) * len(out_shape),
        scratch_shapes=[
            pltpu.VMEM((rank_c, rank_i, users), jnp.float32),
            pltpu.VMEM((2 * ranks, ranks), jnp.float32),
            pltpu.VMEM((rows, LANES), jnp.float32),
            pltpu.VMEM((BATCH, rank_i, users), jnp.float32),
            pltpu.VMEM((BATCH, rank_i, users), jnp.float32),
            pltpu.VMEM(weights.shape, weights.dtype),
            pltpu.VMEM(contexts.shape, contexts.dtype),
            pltpu.VMEM(user_basis.shape, user_basis.dtype),
            pltpu.SemaphoreType.DMA((tiles,)),
            pltpu.SemaphoreType.DMA((tiles // BATCH,)),
            pltpu.SemaphoreType.DMA,
        ],
        compiler_params=limit(12 + held),
        cost_estimate=pl.CostEstimate(flops=2 * 10**9, bytes_accessed=12 * 10**6, transcendentals=0),
        name="tile_sums",
    )(where, count, me, blocks, in_hbm(weights), in_hbm(contexts), in_hbm(user_basis))
    return dict(zip(PIECES, out[:-1])), out[-1]


def inverse_factor(gram, between):
    order = gram.shape[0]
    panels = order // ROWS
    sub = lax.broadcasted_iota(jnp.int32, (ROWS, order), 0)
    lane = lax.broadcasted_iota(jnp.int32, (ROWS, order), 1)
    left = [gram[ROWS * i : ROWS * (i + 1)] for i in range(panels)]
    right = [jnp.where(lane == sub + ROWS * i, 1.0, 0.0) for i in range(panels)]
    for k in range(panels):
        between(k)
        columns = {
            i: [
                jnp.broadcast_to(left[i][:, ROWS * k + j : ROWS * k + j + 1], (ROWS, order))
                for j in range(ROWS)
            ]
            for i in range(k, panels)
        }
        row, tail = left[k], right[k]
        scale = jnp.zeros((ROWS, order), jnp.float32)
        rows, tails = [], []
        for j in range(ROWS):
            head = columns[k][j]
            pivot = jnp.broadcast_to(head[j : j + 1], (ROWS, order))
            inverse = pl.reciprocal(pivot, approx=True)
            inverse = inverse * (2.0 - pivot * inverse)
            scale = jnp.where(sub == j, pivot, scale)
            rows.append(jnp.broadcast_to(row[j : j + 1], (ROWS, order)))
            tails.append(jnp.broadcast_to(tail[j : j + 1], (ROWS, order)))
            below = jnp.where(sub > j, head, 0.0) * inverse
            row = row - below * rows[j]
            tail = tail - below * tails[j]
            facts = {k: below}
            for i in range(k + 1, panels):
                facts[i] = columns[i][j] * inverse
            for c in range(j + 1, ROWS):
                crossing = jnp.broadcast_to(head[c : c + 1], (ROWS, order))
                for i in range(k, panels):
                    columns[i][c] = columns[i][c] - facts[i] * crossing
            for i in range(k + 1, panels):
                left[i] = left[i] - facts[i] * rows[j]
                right[i] = right[i] - facts[i] * tails[j]
        right[k] = tail * lax.rsqrt(scale)
    return jnp.concatenate(right, axis=0)


def finish_kernel(total_users, me_ref, stack_ref, *rest):
    piece_refs, rest = rest[: len(PIECES)], rest[len(PIECES) :]
    basis_ref, core_out_ref, pack_ref, full_ref, high_ref, low_ref = rest
    chunk = piece_refs[0].shape[0]
    places = pack_places(me_ref[0])
    for piece, ref in zip(PIECES, piece_refs):
        pack_ref[pl.ds(pl.multiple_of(places[piece] * chunk, ROWS), chunk)] = ref[...]
    ranks = full_ref.shape[1]
    groups = ranks // LANES
    place = 0
    for i in range(groups):
        for j in range(i, groups):
            block = pack_ref[place * LANES : (place + 1) * LANES]
            for row, lane, part in ((i, j, block), (j, i, block.T))[: 1 if i == j else 2]:
                lanes = slice(lane * LANES, (lane + 1) * LANES)
                high, low = split(part)
                full_ref[row * LANES : (row + 1) * LANES, lanes] = high
                full_ref[ranks + row * LANES : ranks + (row + 1) * LANES, lanes] = low
            place += 1
    projection = pack_ref[place * LANES : (place + groups) * LANES]
    crossed = quarters(dot(full_ref[...], jnp.concatenate(split(projection), axis=1)))
    crossed_high, crossed_low = split(crossed)
    turned = jnp.concatenate(
        [projection[i * LANES : (i + 1) * LANES].T for i in range(groups)], axis=1
    )
    turned_stack = jnp.concatenate(split(turned), axis=0)
    gram = quarters(dot(turned_stack, jnp.concatenate([crossed_high, crossed_low], axis=1)))
    strips = basis_ref.shape[0] // LANES

    def project(k):
        if k % 3 == 0 and k // 3 < strips:
            lanes = slice(k // 3 * LANES, (k // 3 + 1) * LANES)
            part = thrice(turned_stack, stack_ref[:ranks, lanes], stack_ref[ranks:, lanes], dot)
            high_ref[:, lanes], low_ref[:, lanes] = split(part)

    inverse_stack = jnp.concatenate(split(inverse_factor(gram, project)), axis=0)
    root = total_users ** 0.5
    scaled = thrice(inverse_stack, high_ref[...], low_ref[...], dot) * root
    for i in range(scaled.shape[1] // LANES):
        basis_ref[i * LANES : (i + 1) * LANES] = scaled[:, i * LANES : (i + 1) * LANES].T
    core_out_ref[...] = thrice(inverse_stack, crossed_high, crossed_low, dot_nt) * (1.0 / root)


def finish(me, stack, pieces, devices):
    ranks, users = stack.shape[0] // 2, stack.shape[1]
    return pl.pallas_call(
        functools.partial(finish_kernel, users * devices),
        out_shape=(
            jax.ShapeDtypeStruct((users, LANES), jnp.float32),
            jax.ShapeDtypeStruct((LANES, ranks), jnp.float32),
        ),
        in_specs=[SMEM] + [VMEM] * (1 + len(PIECES)),
        out_specs=(VMEM, VMEM),
        scratch_shapes=[
            pltpu.VMEM((pack_rows(ranks), LANES), jnp.float32),
            pltpu.VMEM((2 * ranks, ranks), jnp.bfloat16),
            pltpu.VMEM((LANES, users), jnp.bfloat16),
            pltpu.VMEM((LANES, users), jnp.bfloat16),
        ],
        compiler_params=limit(16),
        name="finish",
    )(me, stack, *[pieces[piece] for piece in PIECES])


def swap(value, mask, devices):
    return lax.ppermute(value, "users", [(i, i ^ mask) for i in range(devices)])


def encode(value):
    rows, lanes = value.shape
    groups = rows // GROUP
    parts = value.reshape(groups, GROUP, lanes)
    most = jnp.max(jnp.abs(parts), axis=1, keepdims=True)
    exponent = jnp.clip(jnp.floor(jnp.log2(most)) + 1.0, -110.0, 128.0)
    coded = jnp.clip(jnp.round(parts * jnp.exp2(14.0 - exponent)), -32767.0, 32767.0)
    extra = jnp.pad(exponent.reshape(groups, lanes), ((0, -groups % 16), (0, 0)))
    return jnp.concatenate([coded.reshape(rows, lanes), extra], axis=0).astype(jnp.int16)


def decode(coded, rows):
    lanes = coded.shape[1]
    groups = rows // GROUP
    scale = jnp.exp2(coded[rows : rows + groups].astype(jnp.float32) - 14.0)
    parts = coded[:rows].astype(jnp.float32).reshape(groups, GROUP, lanes)
    return (parts * scale.reshape(groups, 1, lanes)).reshape(rows, lanes)


def reduce_pieces(pieces, devices):
    rows = pieces[0, 0].shape[0]
    got = {plane: swap(pieces[1, plane], 1, devices) for plane in (3, 1, 2, 0)}
    total = pieces[0, 0] + got[0]
    for plane in (3, 1, 2):
        coded = encode(pieces[0, plane] + got[plane])
        total = total + decode(swap(coded, 2 * plane, devices), rows)
    mask = CHUNKS
    while mask < devices:
        coded = encode(total)
        total = decode(coded, rows) + decode(swap(coded, mask, devices), rows)
        mask *= 2
    return encode(total)


def spread_pieces(total, devices, rows):
    coded = {(0, 0): total}
    for plane in (3, 1, 2):
        coded[0, plane] = swap(total, 2 * plane, devices)
    for plane in (0, 3, 1, 2):
        coded[1, plane] = swap(coded[0, plane], 1, devices)
    return {piece: decode(value, rows) for piece, value in coded.items()}


def body(
    tile_owner, tile_slot, tile_cblock, tile_context, tile_weights,
    item_factors, context_factors, user_basis, user_counts,
):
    devices = lax.axis_size("users")
    half = devices // 2
    rank_c = context_factors.shape[0]
    me = lax.axis_index("users").astype(jnp.int32).reshape(1)

    mirror = swap(item_factors, half, devices)
    requests, where, own = route(me, tile_owner[:, 0], tile_slot, item_factors, half)
    sides = [list(range(half)), list(range(half, devices))]
    asked = lax.all_to_all(requests, "users", 0, 0, axis_index_groups=sides, tiled=True)
    found = collect(asked, own, mirror)
    found, cblock, factors = lax.optimization_barrier((found, tile_cblock, context_factors))
    blocks = lax.all_to_all(found, "users", 0, 0, axis_index_groups=sides, tiled=True)

    table = factors.astype(jnp.float32).reshape(rank_c, -1, CB).transpose(1, 0, 2)
    contexts = context_values(cblock, table, tile_context)
    pieces, stack = tile_sums(
        where, user_counts, me, blocks, tile_weights, contexts, user_basis
    )
    rows = pieces[0, 0].shape[0]
    pieces = spread_pieces(reduce_pieces(pieces, devices), devices, rows)
    return finish(me, stack, pieces, devices)


def solution(mesh):
    return jax.shard_map(
        body,
        mesh=mesh,
        in_specs=(
            P("users", None), P("users"), P("users"), P("users", None), P("users", None, None),
            P("users", None, None), P(), P("users", None), P("users"),
        ),
        out_specs=(P("users", None), P()),
        check_vma=False,
    )
```

```python
import functools

import jax
import jax.numpy as jnp
from jax import lax
from jax.experimental import pallas as pl
from jax.experimental.pallas import tpu as pltpu
from jax.sharding import PartitionSpec as P

CB = 8
SLOTS = 2
PLACES = 2 * SLOTS
LANES = 128
ROWS = 8
BATCH = 8
CHUNKS = 8
GROUP = 32
MIB = 2**20

SMEM = pl.BlockSpec(memory_space=pltpu.SMEM)
VMEM = pl.BlockSpec(memory_space=pltpu.VMEM)
ANY = pl.BlockSpec(memory_space=pl.ANY)


def in_hbm(value):
    return pltpu.with_memory_space_constraint(value, pltpu.HBM)


def limit(mib):
    return pltpu.CompilerParams(vmem_limit_bytes=mib * MIB)


def dot(lhs, rhs):
    return jnp.dot(lhs, rhs, preferred_element_type=jnp.float32)


def dot_nt(lhs, rhs):
    return lax.dot_general(lhs, rhs, (((1,), (1,)), ((), ())), preferred_element_type=jnp.float32)


def split(value):
    high = value.astype(jnp.bfloat16)
    return high, (value - high.astype(jnp.float32)).astype(jnp.bfloat16)


def quarters(value):
    rows, lanes = value.shape[0] // 2, value.shape[1] // 2
    return (value[:rows, :lanes] + value[:rows, lanes:]) + (value[rows:, :lanes] + value[rows:, lanes:])


def thrice(stack, high, low, product):
    rows = stack.shape[0] // 2
    first = product(stack, high)
    return first[:rows] + (first[rows:] + product(stack[:rows], low))


def route_kernel(half, me_ref, owner_ref, slot_ref, own_ref, request_ref, where_ref, held_ref, used_ref, sem_ref):
    copy = pltpu.make_async_copy(own_ref, held_ref, sem_ref)
    copy.start()
    side = me_ref[0] // half
    lane = lax.broadcasted_iota(jnp.int32, (1, LANES), 1)

    def clear(place, _):
        used_ref[place] = 0
        return 0

    lax.fori_loop(0, 2 * half, clear, 0, unroll=8)
    request_ref[...] = jnp.zeros_like(request_ref)

    def assign(tile, _):
        owner = owner_ref[tile]
        taken = used_ref[owner]
        used_ref[owner] = taken + 1
        low = lax.rem(owner, half)
        place = jnp.where(owner // half == side, 0, SLOTS) + taken
        request_ref[low] = jnp.where(lane == place, slot_ref[tile], request_ref[low])
        where_ref[tile] = low * PLACES + place
        return 0

    lax.fori_loop(0, owner_ref.shape[0], assign, 0, unroll=4)
    copy.wait()


def route(me, owners, slots, own, half):
    return pl.pallas_call(
        functools.partial(route_kernel, half),
        out_shape=(
            jax.ShapeDtypeStruct((half, 1, LANES), jnp.int32),
            jax.ShapeDtypeStruct(owners.shape, jnp.int32),
            jax.ShapeDtypeStruct(own.shape, own.dtype),
        ),
        in_specs=[SMEM, SMEM, SMEM, ANY],
        out_specs=(VMEM, SMEM, VMEM),
        scratch_shapes=[pltpu.SMEM((2 * half,), jnp.int32), pltpu.SemaphoreType.DMA],
        compiler_params=limit(4),
        name="route",
    )(me, in_hbm(owners), in_hbm(slots), in_hbm(own))


def collect_kernel(asked_ref, own_ref, mirror_ref, out_ref):
    for peer in range(asked_ref.shape[0]):
        for place in range(PLACES):
            source = own_ref if place < SLOTS else mirror_ref
            out_ref[peer * PLACES + place] = source[asked_ref[peer, 0, place]]


def collect(asked, own, mirror):
    return pl.pallas_call(
        collect_kernel,
        out_shape=jax.ShapeDtypeStruct((asked.shape[0] * PLACES,) + own.shape[1:], own.dtype),
        in_specs=[SMEM, VMEM, VMEM],
        out_specs=VMEM,
        compiler_params=limit(4),
        name="collect",
    )(asked, own, mirror)


def context_kernel(cblock_ref, table_ref, marks_ref, context_ref):
    tiles, users = marks_ref.shape

    def one(tile, _):
        table = table_ref[cblock_ref[tile]]
        marks = jnp.broadcast_to(marks_ref[pl.ds(tile, 1), :], (ROWS, users))
        total = jnp.zeros((ROWS, users), jnp.float32)
        for k in range(CB):
            column = jnp.broadcast_to(table[:, k : k + 1], (ROWS, users))
            total = jnp.where(marks == k, column, total)
        context_ref[tile] = total
        return 0

    lax.fori_loop(0, tiles, one, 0, unroll=2)


def context_values(cblock, table, marks):
    tiles, users = marks.shape
    return pl.pallas_call(
        context_kernel,
        out_shape=jax.ShapeDtypeStruct((tiles, ROWS, users), jnp.float32),
        in_specs=[SMEM, VMEM, VMEM],
        out_specs=VMEM,
        compiler_params=limit(4),
        cost_estimate=pl.CostEstimate(flops=10**7, bytes_accessed=2 * 10**7, transcendentals=0),
        name="contexts",
    )(in_hbm(cblock), table, marks)


def pack_places(me):
    return {
        (core, plane): jnp.bitwise_xor(lax.rem(me, CHUNKS), core + 2 * plane)
        for core in range(2)
        for plane in range(4)
    }


PIECES = [(core, plane) for core in (1, 0) for plane in (3, 1, 2, 0)]


def pack_rows(ranks):
    groups = ranks // LANES
    return (groups * (groups + 1) // 2 + groups) * LANES


def tiles_kernel(
    where_ref, count_ref, me_ref, blocks_ref, weights_ref, context_ref, basis_ref, *refs
):
    piece_refs, refs = refs[: len(PIECES)], refs[len(PIECES) :]
    stack_ref, y_ref, square_ref, pack_ref, even_ref, odd_ref = refs[:6]
    weights_held, context_held, basis_held, weights_sem, context_sem, basis_sem = refs[6:]
    rank_c, rank_i, users = y_ref.shape
    batches = weights_ref.shape[0] // BATCH
    half = rank_c // 2

    def copies(batch):
        rows = pl.ds(batch * BATCH, BATCH)
        tiles = [batch * BATCH + place for place in range(BATCH)]
        return [
            pltpu.make_async_copy(weights_ref.at[tile], weights_held.at[tile], weights_sem.at[tile]) for tile in tiles
        ] + [pltpu.make_async_copy(context_ref.at[rows], context_held.at[rows], context_sem.at[batch])]

    def start(batch):
        for copy in copies(batch):
            copy.start()

    def wait(batch):
        for copy in copies(batch):
            copy.wait()

    start(0)
    start(1)

    def multiply(batch, place, into_ref):
        tile = batch * BATCH + place
        product = dot(blocks_ref[where_ref[tile]], weights_held[tile])
        into_ref[place] = product.astype(jnp.bfloat16).astype(jnp.float32)

    def add(batch, part, from_ref):
        lanes = slice(part // 2 * LANES, (part // 2 + 1) * LANES)
        ranks = range(part % 2 * half, (part % 2 + 1) * half)
        strips = [slice(i, i + ROWS) for i in range(0, rank_i, ROWS)]
        totals = [[y_ref[r, strip, lanes] for strip in strips] for r in ranks]
        for place in range(BATCH):
            parts_of = [from_ref[place, strip, lanes] for strip in strips]
            for i, r in enumerate(ranks):
                values = context_held[batch * BATCH + place, r : r + 1, lanes]
                values = jnp.broadcast_to(values, (ROWS, LANES))
                for j in range(len(strips)):
                    totals[i][j] = totals[i][j] + values * parts_of[j]
        for i, r in enumerate(ranks):
            for strip, total in zip(strips, totals[i]):
                y_ref[r, strip, lanes] = total

    y_ref[...] = jnp.zeros_like(y_ref)
    parts = 2 * users // LANES
    wait(0)
    start(2)
    for place in range(BATCH):
        multiply(0, place, even_ref)

    def turn(batch, from_ref, into_ref):
        wait(batch + 1)

        @pl.when(batch + 3 < batches)
        def _():
            start(batch + 3)

        for place in range(BATCH):
            multiply(batch + 1, place, into_ref)
        for part in range(parts):
            add(batch, part, from_ref)

    def pair(index, _):
        turn(2 * index, even_ref, odd_ref)
        turn(2 * index + 1, odd_ref, even_ref)
        return 0

    lax.fori_loop(0, batches // 2 - 1, pair, 0)
    basis_copy = pltpu.make_async_copy(basis_ref, basis_held, basis_sem)
    basis_copy.start()
    turn(batches - 2, even_ref, odd_ref)
    for part in range(parts):
        add(batches - 1, part, odd_ref)

    living = lax.broadcasted_iota(jnp.int32, (rank_i, users), 1) < count_ref[0]
    ranks = rank_c * rank_i
    for r in range(rank_c):
        high, low = split(jnp.where(living, y_ref[r], 0.0))
        stack_ref[r * rank_i : (r + 1) * rank_i] = high
        stack_ref[ranks + r * rank_i : ranks + (r + 1) * rank_i] = low
    square_ref[...] = dot_nt(stack_ref[...], stack_ref[:ranks])
    basis_copy.wait()
    projection = dot(stack_ref[...], jnp.concatenate(split(basis_held[...]), axis=1))
    groups = ranks // LANES
    place = 0
    for i in range(groups):
        rows = slice(i * LANES, (i + 1) * LANES)
        low_rows = slice(ranks + i * LANES, ranks + (i + 1) * LANES)
        for j in range(i, groups):
            lanes = slice(j * LANES, (j + 1) * LANES)
            low_lanes = slice(ranks + j * LANES, ranks + (j + 1) * LANES)
            block = square_ref[rows, lanes] + square_ref[low_rows, lanes] + square_ref[low_lanes, rows].T
            pack_ref[place * LANES : (place + 1) * LANES] = block
            place += 1
    pack_ref[place * LANES : (place + groups) * LANES] = quarters(projection)
    chunk = piece_refs[0].shape[0]
    places = pack_places(me_ref[0])
    for piece, ref in zip(PIECES, piece_refs):
        ref[...] = pack_ref[pl.ds(pl.multiple_of(places[piece] * chunk, ROWS), chunk)]


def tile_sums(where, count, me, blocks, weights, contexts, user_basis):
    tiles, _, users = weights.shape
    rank_i = blocks.shape[1]
    rank_c = contexts.shape[1]
    ranks = rank_c * rank_i
    rows = pack_rows(ranks)
    out_shape = (jax.ShapeDtypeStruct((rows // CHUNKS, LANES), jnp.float32),) * len(PIECES)
    out_shape += (jax.ShapeDtypeStruct((2 * ranks, users), jnp.bfloat16),)
    held = 3 * weights.size * 2 // (2 * MIB)
    out = pl.pallas_call(
        tiles_kernel,
        out_shape=out_shape,
        in_specs=[SMEM] * 3 + [VMEM] + [ANY] * 3,
        out_specs=(VMEM,) * len(out_shape),
        scratch_shapes=[
            pltpu.VMEM((rank_c, rank_i, users), jnp.float32),
            pltpu.VMEM((2 * ranks, ranks), jnp.float32),
            pltpu.VMEM((rows, LANES), jnp.float32),
            pltpu.VMEM((BATCH, rank_i, users), jnp.float32),
            pltpu.VMEM((BATCH, rank_i, users), jnp.float32),
            pltpu.VMEM(weights.shape, weights.dtype),
            pltpu.VMEM(contexts.shape, contexts.dtype),
            pltpu.VMEM(user_basis.shape, user_basis.dtype),
            pltpu.SemaphoreType.DMA((tiles,)),
            pltpu.SemaphoreType.DMA((tiles // BATCH,)),
            pltpu.SemaphoreType.DMA,
        ],
        compiler_params=limit(12 + held),
        cost_estimate=pl.CostEstimate(flops=2 * 10**9, bytes_accessed=12 * 10**6, transcendentals=0),
        name="tile_sums",
    )(where, count, me, blocks, in_hbm(weights), in_hbm(contexts), in_hbm(user_basis))
    return dict(zip(PIECES, out[:-1])), out[-1]


def inverse_factor(gram, between):
    order = gram.shape[0]
    panels = order // ROWS
    sub = lax.broadcasted_iota(jnp.int32, (ROWS, order), 0)
    lane = lax.broadcasted_iota(jnp.int32, (ROWS, order), 1)
    left = [gram[ROWS * i : ROWS * (i + 1)] for i in range(panels)]
    right = [jnp.where(lane == sub + ROWS * i, 1.0, 0.0) for i in range(panels)]
    for k in range(panels):
        between(k)
        columns = {
            i: [
                jnp.broadcast_to(left[i][:, ROWS * k + j : ROWS * k + j + 1], (ROWS, order))
                for j in range(ROWS)
            ]
            for i in range(k, panels)
        }
        row, tail = left[k], right[k]
        scale = jnp.zeros((ROWS, order), jnp.float32)
        rows, tails = [], []
        for j in range(ROWS):
            head = columns[k][j]
            pivot = jnp.broadcast_to(head[j : j + 1], (ROWS, order))
            inverse = pl.reciprocal(pivot, approx=True)
            inverse = inverse * (2.0 - pivot * inverse)
            scale = jnp.where(sub == j, pivot, scale)
            rows.append(jnp.broadcast_to(row[j : j + 1], (ROWS, order)))
            tails.append(jnp.broadcast_to(tail[j : j + 1], (ROWS, order)))
            below = jnp.where(sub > j, head, 0.0) * inverse
            row = row - below * rows[j]
            tail = tail - below * tails[j]
            facts = {k: below}
            for i in range(k + 1, panels):
                facts[i] = columns[i][j] * inverse
            for c in range(j + 1, ROWS):
                crossing = jnp.broadcast_to(head[c : c + 1], (ROWS, order))
                for i in range(k, panels):
                    columns[i][c] = columns[i][c] - facts[i] * crossing
            for i in range(k + 1, panels):
                left[i] = left[i] - facts[i] * rows[j]
                right[i] = right[i] - facts[i] * tails[j]
        right[k] = tail * lax.rsqrt(scale)
    return jnp.concatenate(right, axis=0)


def finish_kernel(total_users, me_ref, stack_ref, *rest):
    piece_refs, rest = rest[: len(PIECES)], rest[len(PIECES) :]
    basis_ref, core_out_ref, pack_ref, full_ref, high_ref, low_ref = rest
    chunk = piece_refs[0].shape[0]
    places = pack_places(me_ref[0])
    for piece, ref in zip(PIECES, piece_refs):
        pack_ref[pl.ds(pl.multiple_of(places[piece] * chunk, ROWS), chunk)] = ref[...]
    ranks = full_ref.shape[1]
    groups = ranks // LANES
    place = 0
    for i in range(groups):
        for j in range(i, groups):
            block = pack_ref[place * LANES : (place + 1) * LANES]
            for row, lane, part in ((i, j, block), (j, i, block.T))[: 1 if i == j else 2]:
                lanes = slice(lane * LANES, (lane + 1) * LANES)
                high, low = split(part)
                full_ref[row * LANES : (row + 1) * LANES, lanes] = high
                full_ref[ranks + row * LANES : ranks + (row + 1) * LANES, lanes] = low
            place += 1
    projection = pack_ref[place * LANES : (place + groups) * LANES]
    crossed = quarters(dot(full_ref[...], jnp.concatenate(split(projection), axis=1)))
    crossed_high, crossed_low = split(crossed)
    turned = jnp.concatenate(
        [projection[i * LANES : (i + 1) * LANES].T for i in range(groups)], axis=1
    )
    turned_stack = jnp.concatenate(split(turned), axis=0)
    gram = quarters(dot(turned_stack, jnp.concatenate([crossed_high, crossed_low], axis=1)))
    strips = basis_ref.shape[0] // LANES

    def project(k):
        if k % 3 == 0 and k // 3 < strips:
            lanes = slice(k // 3 * LANES, (k // 3 + 1) * LANES)
            part = thrice(turned_stack, stack_ref[:ranks, lanes], stack_ref[ranks:, lanes], dot)
            high_ref[:, lanes], low_ref[:, lanes] = split(part)

    inverse_stack = jnp.concatenate(split(inverse_factor(gram, project)), axis=0)
    root = total_users ** 0.5
    scaled = thrice(inverse_stack, high_ref[...], low_ref[...], dot) * root
    for i in range(scaled.shape[1] // LANES):
        basis_ref[i * LANES : (i + 1) * LANES] = scaled[:, i * LANES : (i + 1) * LANES].T
    core_out_ref[...] = thrice(inverse_stack, crossed_high, crossed_low, dot_nt) * (1.0 / root)


def finish(me, stack, pieces, devices):
    ranks, users = stack.shape[0] // 2, stack.shape[1]
    return pl.pallas_call(
        functools.partial(finish_kernel, users * devices),
        out_shape=(
            jax.ShapeDtypeStruct((users, LANES), jnp.float32),
            jax.ShapeDtypeStruct((LANES, ranks), jnp.float32),
        ),
        in_specs=[SMEM] + [VMEM] * (1 + len(PIECES)),
        out_specs=(VMEM, VMEM),
        scratch_shapes=[
            pltpu.VMEM((pack_rows(ranks), LANES), jnp.float32),
            pltpu.VMEM((2 * ranks, ranks), jnp.bfloat16),
            pltpu.VMEM((LANES, users), jnp.bfloat16),
            pltpu.VMEM((LANES, users), jnp.bfloat16),
        ],
        compiler_params=limit(16),
        name="finish",
    )(me, stack, *[pieces[piece] for piece in PIECES])


def swap(value, mask, devices):
    return lax.ppermute(value, "users", [(i, i ^ mask) for i in range(devices)])


def encode(value):
    rows, lanes = value.shape
    groups = rows // GROUP
    parts = value.reshape(groups, GROUP, lanes)
    most = jnp.max(jnp.abs(parts), axis=1, keepdims=True)
    exponent = jnp.clip(jnp.floor(jnp.log2(most)) + 1.0, -110.0, 128.0)
    coded = jnp.clip(jnp.round(parts * jnp.exp2(14.0 - exponent)), -32767.0, 32767.0)
    extra = jnp.pad(exponent.reshape(groups, lanes), ((0, -groups % 16), (0, 0)))
    return jnp.concatenate([coded.reshape(rows, lanes), extra], axis=0).astype(jnp.int16)


def decode(coded, rows):
    lanes = coded.shape[1]
    groups = rows // GROUP
    scale = jnp.exp2(coded[rows : rows + groups].astype(jnp.float32) - 14.0)
    parts = coded[:rows].astype(jnp.float32).reshape(groups, GROUP, lanes)
    return (parts * scale.reshape(groups, 1, lanes)).reshape(rows, lanes)


def reduce_pieces(pieces, devices):
    rows = pieces[0, 0].shape[0]
    got = {plane: swap(pieces[1, plane], 1, devices) for plane in (3, 1, 2, 0)}
    total = pieces[0, 0] + got[0]
    for plane in (3, 1, 2):
        coded = encode(pieces[0, plane] + got[plane])
        total = total + decode(swap(coded, 2 * plane, devices), rows)
    mask = CHUNKS
    while mask < devices:
        coded = encode(total)
        total = decode(coded, rows) + decode(swap(coded, mask, devices), rows)
        mask *= 2
    return encode(total)


def spread_pieces(total, devices, rows):
    coded = {(0, 0): total}
    for plane in (3, 1, 2):
        coded[0, plane] = swap(total, 2 * plane, devices)
    for plane in (0, 3, 1, 2):
        coded[1, plane] = swap(coded[0, plane], 1, devices)
    return {piece: decode(value, rows) for piece, value in coded.items()}


def body(
    tile_owner, tile_slot, tile_cblock, tile_context, tile_weights,
    item_factors, context_factors, user_basis, user_counts,
):
    devices = lax.axis_size("users")
    half = devices // 2
    rank_c = context_factors.shape[0]
    me = lax.axis_index("users").astype(jnp.int32).reshape(1)

    mirror = swap(item_factors, half, devices)
    requests, where, own = route(me, tile_owner[:, 0], tile_slot, item_factors, half)
    sides = [list(range(half)), list(range(half, devices))]
    asked = lax.all_to_all(requests, "users", 0, 0, axis_index_groups=sides, tiled=True)
    found = collect(asked, own, mirror)
    found, cblock, factors = lax.optimization_barrier((found, tile_cblock, context_factors))
    blocks = lax.all_to_all(found, "users", 0, 0, axis_index_groups=sides, tiled=True)

    table = factors.astype(jnp.float32).reshape(rank_c, -1, CB).transpose(1, 0, 2)
    contexts = context_values(cblock, table, tile_context)
    pieces, stack = tile_sums(
        where, user_counts, me, blocks, tile_weights, contexts, user_basis
    )
    rows = pieces[0, 0].shape[0]
    pieces = spread_pieces(reduce_pieces(pieces, devices), devices, rows)
    return finish(me, stack, pieces, devices)


def solution(mesh):
    return jax.shard_map(
        body,
        mesh=mesh,
        in_specs=(
            P("users", None), P("users"), P("users"), P("users", None), P("users", None, None),
            P("users", None, None), P(), P("users", None), P("users"),
        ),
        out_specs=(P("users", None), P()),
        check_vma=False,
    )
```

```python
import functools

import jax
import jax.numpy as jnp
from jax import lax
from jax.experimental import pallas as pl
from jax.experimental.pallas import tpu as pltpu
from jax.sharding import PartitionSpec as P

CB = 8
SLOTS = 2
PLACES = 2 * SLOTS
LANES = 128
ROWS = 8
BATCH = 8
CHUNKS = 8
GROUP = 32
MIB = 2**20

SMEM = pl.BlockSpec(memory_space=pltpu.SMEM)
VMEM = pl.BlockSpec(memory_space=pltpu.VMEM)
ANY = pl.BlockSpec(memory_space=pl.ANY)


def in_hbm(value):
    return pltpu.with_memory_space_constraint(value, pltpu.HBM)


def limit(mib):
    return pltpu.CompilerParams(vmem_limit_bytes=mib * MIB)


def dot(lhs, rhs):
    return jnp.dot(lhs, rhs, preferred_element_type=jnp.float32)


def dot_nt(lhs, rhs):
    return lax.dot_general(lhs, rhs, (((1,), (1,)), ((), ())), preferred_element_type=jnp.float32)


def split(value):
    high = value.astype(jnp.bfloat16)
    return high, (value - high.astype(jnp.float32)).astype(jnp.bfloat16)


def quarters(value):
    rows, lanes = value.shape[0] // 2, value.shape[1] // 2
    return (value[:rows, :lanes] + value[:rows, lanes:]) + (value[rows:, :lanes] + value[rows:, lanes:])


def thrice(stack, high, low, product):
    rows = stack.shape[0] // 2
    first = product(stack, high)
    return first[:rows] + (first[rows:] + product(stack[:rows], low))


def route_kernel(half, me_ref, owner_ref, slot_ref, own_ref, request_ref, where_ref, held_ref, used_ref, sem_ref):
    copy = pltpu.make_async_copy(own_ref, held_ref, sem_ref)
    copy.start()
    side = me_ref[0] // half
    lane = lax.broadcasted_iota(jnp.int32, (1, LANES), 1)

    def clear(place, _):
        used_ref[place] = 0
        return 0

    lax.fori_loop(0, 2 * half, clear, 0, unroll=8)
    request_ref[...] = jnp.zeros_like(request_ref)

    def assign(tile, _):
        owner = owner_ref[tile]
        taken = used_ref[owner]
        used_ref[owner] = taken + 1
        low = lax.rem(owner, half)
        place = jnp.where(owner // half == side, 0, SLOTS) + taken
        request_ref[low] = jnp.where(lane == place, slot_ref[tile], request_ref[low])
        where_ref[tile] = low * PLACES + place
        return 0

    lax.fori_loop(0, owner_ref.shape[0], assign, 0, unroll=4)
    copy.wait()


def route(me, owners, slots, own, half):
    return pl.pallas_call(
        functools.partial(route_kernel, half),
        out_shape=(
            jax.ShapeDtypeStruct((half, 1, LANES), jnp.int32),
            jax.ShapeDtypeStruct(owners.shape, jnp.int32),
            jax.ShapeDtypeStruct(own.shape, own.dtype),
        ),
        in_specs=[SMEM, SMEM, SMEM, ANY],
        out_specs=(VMEM, SMEM, VMEM),
        scratch_shapes=[pltpu.SMEM((2 * half,), jnp.int32), pltpu.SemaphoreType.DMA],
        compiler_params=limit(4),
        name="route",
    )(me, in_hbm(owners), in_hbm(slots), in_hbm(own))


def collect_kernel(asked_ref, own_ref, mirror_ref, out_ref):
    for peer in range(asked_ref.shape[0]):
        for place in range(PLACES):
            source = own_ref if place < SLOTS else mirror_ref
            out_ref[peer * PLACES + place] = source[asked_ref[peer, 0, place]]


def collect(asked, own, mirror):
    return pl.pallas_call(
        collect_kernel,
        out_shape=jax.ShapeDtypeStruct((asked.shape[0] * PLACES,) + own.shape[1:], own.dtype),
        in_specs=[SMEM, VMEM, VMEM],
        out_specs=VMEM,
        compiler_params=limit(4),
        name="collect",
    )(asked, own, mirror)


def context_kernel(cblock_ref, table_ref, marks_ref, context_ref):
    tiles, users = marks_ref.shape

    def one(tile, _):
        table = table_ref[cblock_ref[tile]]
        marks = jnp.broadcast_to(marks_ref[pl.ds(tile, 1), :], (ROWS, users))
        total = jnp.zeros((ROWS, users), jnp.float32)
        for k in range(CB):
            column = jnp.broadcast_to(table[:, k : k + 1], (ROWS, users))
            total = jnp.where(marks == k, column, total)
        context_ref[tile] = total
        return 0

    lax.fori_loop(0, tiles, one, 0, unroll=2)


def context_values(cblock, table, marks):
    tiles, users = marks.shape
    return pl.pallas_call(
        context_kernel,
        out_shape=jax.ShapeDtypeStruct((tiles, ROWS, users), jnp.float32),
        in_specs=[SMEM, VMEM, VMEM],
        out_specs=VMEM,
        compiler_params=limit(4),
        cost_estimate=pl.CostEstimate(flops=10**7, bytes_accessed=2 * 10**7, transcendentals=0),
        name="contexts",
    )(in_hbm(cblock), table, marks)


def pack_places(me):
    return {
        (core, plane): jnp.bitwise_xor(lax.rem(me, CHUNKS), core + 2 * plane)
        for core in range(2)
        for plane in range(4)
    }


PIECES = [(core, plane) for core in (1, 0) for plane in (3, 1, 2, 0)]


def pack_rows(ranks):
    groups = ranks // LANES
    return (groups * (groups + 1) // 2 + groups) * LANES


def tiles_kernel(
    where_ref, count_ref, me_ref, blocks_ref, weights_ref, context_ref, basis_ref, *refs
):
    piece_refs, refs = refs[: len(PIECES)], refs[len(PIECES) :]
    stack_ref, y_ref, square_ref, pack_ref, even_ref, odd_ref = refs[:6]
    weights_held, context_held, basis_held, weights_sem, context_sem, basis_sem = refs[6:]
    rank_c, rank_i, users = y_ref.shape
    batches = weights_ref.shape[0] // BATCH
    half = rank_c // 2

    def copies(batch):
        rows = pl.ds(batch * BATCH, BATCH)
        tiles = [batch * BATCH + place for place in range(BATCH)]
        return [
            pltpu.make_async_copy(weights_ref.at[tile], weights_held.at[tile], weights_sem.at[tile]) for tile in tiles
        ] + [pltpu.make_async_copy(context_ref.at[rows], context_held.at[rows], context_sem.at[batch])]

    def start(batch):
        for copy in copies(batch):
            copy.start()

    def wait(batch):
        for copy in copies(batch):
            copy.wait()

    start(0)
    start(1)

    def multiply(batch, place, into_ref):
        tile = batch * BATCH + place
        into_ref[place] = dot(blocks_ref[where_ref[tile]], weights_held[tile]).astype(into_ref.dtype)

    def add(batch, part, from_ref):
        lanes = slice(part // 2 * LANES, (part // 2 + 1) * LANES)
        ranks = range(part % 2 * half, (part % 2 + 1) * half)
        strips = [slice(i, i + ROWS) for i in range(0, rank_i, ROWS)]
        totals = [[y_ref[r, strip, lanes] for strip in strips] for r in ranks]
        for place in range(BATCH):
            parts_of = []
            for i in range(0, rank_i, 2 * ROWS):
                wide = from_ref[place, i : i + 2 * ROWS, lanes].astype(jnp.float32)
                parts_of += [wide[:ROWS], wide[ROWS:]]
            for i, r in enumerate(ranks):
                values = context_held[batch * BATCH + place, r : r + 1, lanes]
                values = jnp.broadcast_to(values, (ROWS, LANES))
                for j in range(len(strips)):
                    totals[i][j] = totals[i][j] + values * parts_of[j]
        for i, r in enumerate(ranks):
            for strip, total in zip(strips, totals[i]):
                y_ref[r, strip, lanes] = total

    y_ref[...] = jnp.zeros_like(y_ref)
    parts = 2 * users // LANES
    wait(0)
    start(2)
    for place in range(BATCH):
        multiply(0, place, even_ref)

    def turn(batch, from_ref, into_ref):
        wait(batch + 1)

        @pl.when(batch + 3 < batches)
        def _():
            start(batch + 3)

        for place in range(BATCH):
            multiply(batch + 1, place, into_ref)
        for part in range(parts):
            add(batch, part, from_ref)

    def pair(index, _):
        turn(2 * index, even_ref, odd_ref)
        turn(2 * index + 1, odd_ref, even_ref)
        return 0

    lax.fori_loop(0, batches // 2 - 1, pair, 0)
    basis_copy = pltpu.make_async_copy(basis_ref, basis_held, basis_sem)
    basis_copy.start()
    turn(batches - 2, even_ref, odd_ref)
    for part in range(parts):
        add(batches - 1, part, odd_ref)

    living = lax.broadcasted_iota(jnp.int32, (rank_i, users), 1) < count_ref[0]
    ranks = rank_c * rank_i
    for r in range(rank_c):
        high, low = split(jnp.where(living, y_ref[r], 0.0))
        stack_ref[r * rank_i : (r + 1) * rank_i] = high
        stack_ref[ranks + r * rank_i : ranks + (r + 1) * rank_i] = low
    square_ref[...] = dot_nt(stack_ref[...], stack_ref[:ranks])
    basis_copy.wait()
    projection = dot(stack_ref[...], jnp.concatenate(split(basis_held[...]), axis=1))
    groups = ranks // LANES
    place = 0
    for i in range(groups):
        rows = slice(i * LANES, (i + 1) * LANES)
        low_rows = slice(ranks + i * LANES, ranks + (i + 1) * LANES)
        for j in range(i, groups):
            lanes = slice(j * LANES, (j + 1) * LANES)
            low_lanes = slice(ranks + j * LANES, ranks + (j + 1) * LANES)
            block = square_ref[rows, lanes] + square_ref[low_rows, lanes] + square_ref[low_lanes, rows].T
            pack_ref[place * LANES : (place + 1) * LANES] = block
            place += 1
    pack_ref[place * LANES : (place + groups) * LANES] = quarters(projection)
    chunk = piece_refs[0].shape[0]
    places = pack_places(me_ref[0])
    for piece, ref in zip(PIECES, piece_refs):
        ref[...] = pack_ref[pl.ds(pl.multiple_of(places[piece] * chunk, ROWS), chunk)]


def tile_sums(where, count, me, blocks, weights, contexts, user_basis):
    tiles, _, users = weights.shape
    rank_i = blocks.shape[1]
    rank_c = contexts.shape[1]
    ranks = rank_c * rank_i
    rows = pack_rows(ranks)
    out_shape = (jax.ShapeDtypeStruct((rows // CHUNKS, LANES), jnp.float32),) * len(PIECES)
    out_shape += (jax.ShapeDtypeStruct((2 * ranks, users), jnp.bfloat16),)
    held = 3 * weights.size * 2 // (2 * MIB)
    out = pl.pallas_call(
        tiles_kernel,
        out_shape=out_shape,
        in_specs=[SMEM] * 3 + [VMEM] + [ANY] * 3,
        out_specs=(VMEM,) * len(out_shape),
        scratch_shapes=[
            pltpu.VMEM((rank_c, rank_i, users), jnp.float32),
            pltpu.VMEM((2 * ranks, ranks), jnp.float32),
            pltpu.VMEM((rows, LANES), jnp.float32),
            pltpu.VMEM((BATCH, rank_i, users), jnp.bfloat16),
            pltpu.VMEM((BATCH, rank_i, users), jnp.bfloat16),
            pltpu.VMEM(weights.shape, weights.dtype),
            pltpu.VMEM(contexts.shape, contexts.dtype),
            pltpu.VMEM(user_basis.shape, user_basis.dtype),
            pltpu.SemaphoreType.DMA((tiles,)),
            pltpu.SemaphoreType.DMA((tiles // BATCH,)),
            pltpu.SemaphoreType.DMA,
        ],
        compiler_params=limit(12 + held),
        cost_estimate=pl.CostEstimate(flops=2 * 10**9, bytes_accessed=12 * 10**6, transcendentals=0),
        name="tile_sums",
    )(where, count, me, blocks, in_hbm(weights), in_hbm(contexts), in_hbm(user_basis))
    return dict(zip(PIECES, out[:-1])), out[-1]


def inverse_factor(gram, between):
    order = gram.shape[0]
    panels = order // ROWS
    sub = lax.broadcasted_iota(jnp.int32, (ROWS, order), 0)
    lane = lax.broadcasted_iota(jnp.int32, (ROWS, order), 1)
    left = [gram[ROWS * i : ROWS * (i + 1)] for i in range(panels)]
    right = [jnp.where(lane == sub + ROWS * i, 1.0, 0.0) for i in range(panels)]
    for k in range(panels):
        between(k)
        columns = {
            i: [
                jnp.broadcast_to(left[i][:, ROWS * k + j : ROWS * k + j + 1], (ROWS, order))
                for j in range(ROWS)
            ]
            for i in range(k, panels)
        }
        row, tail = left[k], right[k]
        scale = jnp.zeros((ROWS, order), jnp.float32)
        rows, tails = [], []
        for j in range(ROWS):
            head = columns[k][j]
            pivot = jnp.broadcast_to(head[j : j + 1], (ROWS, order))
            inverse = pl.reciprocal(pivot, approx=True)
            inverse = inverse * (2.0 - pivot * inverse)
            scale = jnp.where(sub == j, pivot, scale)
            rows.append(jnp.broadcast_to(row[j : j + 1], (ROWS, order)))
            tails.append(jnp.broadcast_to(tail[j : j + 1], (ROWS, order)))
            below = jnp.where(sub > j, head, 0.0) * inverse
            row = row - below * rows[j]
            tail = tail - below * tails[j]
            facts = {k: below}
            for i in range(k + 1, panels):
                facts[i] = columns[i][j] * inverse
            for c in range(j + 1, ROWS):
                crossing = jnp.broadcast_to(head[c : c + 1], (ROWS, order))
                for i in range(k, panels):
                    columns[i][c] = columns[i][c] - facts[i] * crossing
            for i in range(k + 1, panels):
                left[i] = left[i] - facts[i] * rows[j]
                right[i] = right[i] - facts[i] * tails[j]
        right[k] = tail * lax.rsqrt(scale)
    return jnp.concatenate(right, axis=0)


def finish_kernel(total_users, me_ref, stack_ref, *rest):
    piece_refs, rest = rest[: len(PIECES)], rest[len(PIECES) :]
    basis_ref, core_out_ref, pack_ref, full_ref, high_ref, low_ref = rest
    chunk = piece_refs[0].shape[0]
    places = pack_places(me_ref[0])
    for piece, ref in zip(PIECES, piece_refs):
        pack_ref[pl.ds(pl.multiple_of(places[piece] * chunk, ROWS), chunk)] = ref[...]
    ranks = full_ref.shape[1]
    groups = ranks // LANES
    place = 0
    for i in range(groups):
        for j in range(i, groups):
            block = pack_ref[place * LANES : (place + 1) * LANES]
            for row, lane, part in ((i, j, block), (j, i, block.T))[: 1 if i == j else 2]:
                lanes = slice(lane * LANES, (lane + 1) * LANES)
                high, low = split(part)
                full_ref[row * LANES : (row + 1) * LANES, lanes] = high
                full_ref[ranks + row * LANES : ranks + (row + 1) * LANES, lanes] = low
            place += 1
    projection = pack_ref[place * LANES : (place + groups) * LANES]
    crossed = quarters(dot(full_ref[...], jnp.concatenate(split(projection), axis=1)))
    crossed_high, crossed_low = split(crossed)
    turned = jnp.concatenate(
        [projection[i * LANES : (i + 1) * LANES].T for i in range(groups)], axis=1
    )
    turned_stack = jnp.concatenate(split(turned), axis=0)
    gram = quarters(dot(turned_stack, jnp.concatenate([crossed_high, crossed_low], axis=1)))
    strips = basis_ref.shape[0] // LANES

    def project(k):
        if k % 3 == 0 and k // 3 < strips:
            lanes = slice(k // 3 * LANES, (k // 3 + 1) * LANES)
            part = thrice(turned_stack, stack_ref[:ranks, lanes], stack_ref[ranks:, lanes], dot)
            high_ref[:, lanes], low_ref[:, lanes] = split(part)

    inverse_stack = jnp.concatenate(split(inverse_factor(gram, project)), axis=0)
    root = total_users ** 0.5
    scaled = thrice(inverse_stack, high_ref[...], low_ref[...], dot) * root
    for i in range(scaled.shape[1] // LANES):
        basis_ref[i * LANES : (i + 1) * LANES] = scaled[:, i * LANES : (i + 1) * LANES].T
    core_out_ref[...] = thrice(inverse_stack, crossed_high, crossed_low, dot_nt) * (1.0 / root)


def finish(me, stack, pieces, devices):
    ranks, users = stack.shape[0] // 2, stack.shape[1]
    return pl.pallas_call(
        functools.partial(finish_kernel, users * devices),
        out_shape=(
            jax.ShapeDtypeStruct((users, LANES), jnp.float32),
            jax.ShapeDtypeStruct((LANES, ranks), jnp.float32),
        ),
        in_specs=[SMEM] + [VMEM] * (1 + len(PIECES)),
        out_specs=(VMEM, VMEM),
        scratch_shapes=[
            pltpu.VMEM((pack_rows(ranks), LANES), jnp.float32),
            pltpu.VMEM((2 * ranks, ranks), jnp.bfloat16),
            pltpu.VMEM((LANES, users), jnp.bfloat16),
            pltpu.VMEM((LANES, users), jnp.bfloat16),
        ],
        compiler_params=limit(16),
        name="finish",
    )(me, stack, *[pieces[piece] for piece in PIECES])


def swap(value, mask, devices):
    return lax.ppermute(value, "users", [(i, i ^ mask) for i in range(devices)])


def encode(value):
    rows, lanes = value.shape
    groups = rows // GROUP
    parts = value.reshape(groups, GROUP, lanes)
    most = jnp.max(jnp.abs(parts), axis=1, keepdims=True)
    exponent = jnp.clip(jnp.floor(jnp.log2(most)) + 1.0, -110.0, 128.0)
    coded = jnp.clip(jnp.round(parts * jnp.exp2(14.0 - exponent)), -32767.0, 32767.0)
    extra = jnp.pad(exponent.reshape(groups, lanes), ((0, -groups % 16), (0, 0)))
    return jnp.concatenate([coded.reshape(rows, lanes), extra], axis=0).astype(jnp.int16)


def decode(coded, rows):
    lanes = coded.shape[1]
    groups = rows // GROUP
    scale = jnp.exp2(coded[rows : rows + groups].astype(jnp.float32) - 14.0)
    parts = coded[:rows].astype(jnp.float32).reshape(groups, GROUP, lanes)
    return (parts * scale.reshape(groups, 1, lanes)).reshape(rows, lanes)


def reduce_pieces(pieces, devices):
    rows = pieces[0, 0].shape[0]
    got = {plane: swap(pieces[1, plane], 1, devices) for plane in (3, 1, 2, 0)}
    total = pieces[0, 0] + got[0]
    for plane in (3, 1, 2):
        coded = encode(pieces[0, plane] + got[plane])
        total = total + decode(swap(coded, 2 * plane, devices), rows)
    mask = CHUNKS
    while mask < devices:
        coded = encode(total)
        total = decode(coded, rows) + decode(swap(coded, mask, devices), rows)
        mask *= 2
    return encode(total)


def spread_pieces(total, devices, rows):
    coded = {(0, 0): total}
    for plane in (3, 1, 2):
        coded[0, plane] = swap(total, 2 * plane, devices)
    for plane in (0, 3, 1, 2):
        coded[1, plane] = swap(coded[0, plane], 1, devices)
    return {piece: decode(value, rows) for piece, value in coded.items()}


def body(
    tile_owner, tile_slot, tile_cblock, tile_context, tile_weights,
    item_factors, context_factors, user_basis, user_counts,
):
    devices = lax.axis_size("users")
    half = devices // 2
    rank_c = context_factors.shape[0]
    me = lax.axis_index("users").astype(jnp.int32).reshape(1)

    mirror = swap(item_factors, half, devices)
    requests, where, own = route(me, tile_owner[:, 0], tile_slot, item_factors, half)
    sides = [list(range(half)), list(range(half, devices))]
    asked = lax.all_to_all(requests, "users", 0, 0, axis_index_groups=sides, tiled=True)
    found = collect(asked, own, mirror)
    found, cblock, factors = lax.optimization_barrier((found, tile_cblock, context_factors))
    blocks = lax.all_to_all(found, "users", 0, 0, axis_index_groups=sides, tiled=True)

    table = factors.astype(jnp.float32).reshape(rank_c, -1, CB).transpose(1, 0, 2)
    contexts = context_values(cblock, table, tile_context)
    pieces, stack = tile_sums(
        where, user_counts, me, blocks, tile_weights, contexts, user_basis
    )
    rows = pieces[0, 0].shape[0]
    pieces = spread_pieces(reduce_pieces(pieces, devices), devices, rows)
    return finish(me, stack, pieces, devices)


def solution(mesh):
    return jax.shard_map(
        body,
        mesh=mesh,
        in_specs=(
            P("users", None), P("users"), P("users"), P("users", None), P("users", None, None),
            P("users", None, None), P(), P("users", None), P("users"),
        ),
        out_specs=(P("users", None), P()),
        check_vma=False,
    )
```

```python
import functools

import jax
import jax.numpy as jnp
from jax import lax
from jax.experimental import pallas as pl
from jax.experimental.pallas import tpu as pltpu
from jax.sharding import PartitionSpec as P

CB = 8
SLOTS = 2
PLACES = 2 * SLOTS
LANES = 128
ROWS = 8
BATCH = 8
CHUNKS = 8
GROUP = 32
MIB = 2**20

SMEM = pl.BlockSpec(memory_space=pltpu.SMEM)
VMEM = pl.BlockSpec(memory_space=pltpu.VMEM)
ANY = pl.BlockSpec(memory_space=pl.ANY)


def in_hbm(value):
    return pltpu.with_memory_space_constraint(value, pltpu.HBM)


def limit(mib):
    return pltpu.CompilerParams(vmem_limit_bytes=mib * MIB)


def dot(lhs, rhs):
    return jnp.dot(lhs, rhs, preferred_element_type=jnp.float32)


def dot_nt(lhs, rhs):
    return lax.dot_general(lhs, rhs, (((1,), (1,)), ((), ())), preferred_element_type=jnp.float32)


def split(value):
    high = value.astype(jnp.bfloat16)
    return high, (value - high.astype(jnp.float32)).astype(jnp.bfloat16)


def quarters(value):
    rows, lanes = value.shape[0] // 2, value.shape[1] // 2
    return (value[:rows, :lanes] + value[:rows, lanes:]) + (value[rows:, :lanes] + value[rows:, lanes:])


def thrice(stack, high, low, product):
    rows = stack.shape[0] // 2
    first = product(stack, high)
    return first[:rows] + (first[rows:] + product(stack[:rows], low))


def route_kernel(half, me_ref, owner_ref, slot_ref, own_ref, request_ref, where_ref, held_ref, used_ref, sem_ref):
    copy = pltpu.make_async_copy(own_ref, held_ref, sem_ref)
    copy.start()
    side = me_ref[0] // half
    lane = lax.broadcasted_iota(jnp.int32, (1, LANES), 1)

    def clear(place, _):
        used_ref[place] = 0
        return 0

    lax.fori_loop(0, 2 * half, clear, 0, unroll=8)
    request_ref[...] = jnp.zeros_like(request_ref)

    def assign(tile, _):
        owner = owner_ref[tile]
        taken = used_ref[owner]
        used_ref[owner] = taken + 1
        low = lax.rem(owner, half)
        place = jnp.where(owner // half == side, 0, SLOTS) + taken
        request_ref[low] = jnp.where(lane == place, slot_ref[tile], request_ref[low])
        where_ref[tile] = low * PLACES + place
        return 0

    lax.fori_loop(0, owner_ref.shape[0], assign, 0, unroll=4)
    copy.wait()


def route(me, owners, slots, own, half):
    return pl.pallas_call(
        functools.partial(route_kernel, half),
        out_shape=(
            jax.ShapeDtypeStruct((half, 1, LANES), jnp.int32),
            jax.ShapeDtypeStruct(owners.shape, jnp.int32),
            jax.ShapeDtypeStruct(own.shape, own.dtype),
        ),
        in_specs=[SMEM, SMEM, SMEM, ANY],
        out_specs=(VMEM, SMEM, VMEM),
        scratch_shapes=[pltpu.SMEM((2 * half,), jnp.int32), pltpu.SemaphoreType.DMA],
        compiler_params=limit(4),
        name="route",
    )(me, in_hbm(owners), in_hbm(slots), in_hbm(own))


def collect_kernel(asked_ref, own_ref, mirror_ref, out_ref):
    for peer in range(asked_ref.shape[0]):
        for place in range(PLACES):
            source = own_ref if place < SLOTS else mirror_ref
            out_ref[peer * PLACES + place] = source[asked_ref[peer, 0, place]]


def collect(asked, own, mirror):
    return pl.pallas_call(
        collect_kernel,
        out_shape=jax.ShapeDtypeStruct((asked.shape[0] * PLACES,) + own.shape[1:], own.dtype),
        in_specs=[SMEM, VMEM, VMEM],
        out_specs=VMEM,
        compiler_params=limit(4),
        name="collect",
    )(asked, own, mirror)


def context_kernel(cblock_ref, table_ref, marks_ref, context_ref):
    tiles, users = marks_ref.shape

    def one(tile, _):
        table = table_ref[cblock_ref[tile]]
        marks = jnp.broadcast_to(marks_ref[pl.ds(tile, 1), :], (ROWS, users))
        total = jnp.zeros((ROWS, users), jnp.float32)
        for k in range(CB):
            column = jnp.broadcast_to(table[:, k : k + 1], (ROWS, users))
            total = jnp.where(marks == k, column, total)
        context_ref[tile] = jnp.broadcast_to(total[:, None, :], (ROWS, ROWS, users))
        return 0

    lax.fori_loop(0, tiles, one, 0, unroll=2)


def context_values(cblock, table, marks):
    tiles, users = marks.shape
    return pl.pallas_call(
        context_kernel,
        out_shape=jax.ShapeDtypeStruct((tiles, ROWS, ROWS, users), jnp.float32),
        in_specs=[SMEM, VMEM, VMEM],
        out_specs=VMEM,
        compiler_params=limit(4),
        cost_estimate=pl.CostEstimate(flops=10**7, bytes_accessed=2 * 10**7, transcendentals=0),
        name="contexts",
    )(in_hbm(cblock), table, marks)


def pack_places(me):
    return {
        (core, plane): jnp.bitwise_xor(lax.rem(me, CHUNKS), core + 2 * plane)
        for core in range(2)
        for plane in range(4)
    }


PIECES = [(core, plane) for core in (1, 0) for plane in (3, 1, 2, 0)]


def pack_rows(ranks):
    groups = ranks // LANES
    return (groups * (groups + 1) // 2 + groups) * LANES


def tiles_kernel(
    where_ref, count_ref, me_ref, blocks_ref, weights_ref, context_ref, basis_ref, *refs
):
    piece_refs, refs = refs[: len(PIECES)], refs[len(PIECES) :]
    stack_ref, y_ref, square_ref, pack_ref, even_ref, odd_ref = refs[:6]
    weights_held, context_held, basis_held, weights_sem, context_sem, basis_sem = refs[6:]
    rank_c, rank_i, users = y_ref.shape
    batches = weights_ref.shape[0] // BATCH
    half = rank_c // 2

    def copies(batch):
        rows = pl.ds(batch * BATCH, BATCH)
        tiles = [batch * BATCH + place for place in range(BATCH)]
        return [
            pltpu.make_async_copy(weights_ref.at[tile], weights_held.at[tile], weights_sem.at[tile]) for tile in tiles
        ] + [pltpu.make_async_copy(context_ref.at[rows], context_held.at[rows], context_sem.at[batch])]

    def start(batch):
        for copy in copies(batch):
            copy.start()

    def wait(batch):
        for copy in copies(batch):
            copy.wait()

    start(0)
    start(1)

    def multiply(batch, place, into_ref):
        tile = batch * BATCH + place
        into_ref[place] = dot(blocks_ref[where_ref[tile]], weights_held[tile]).astype(into_ref.dtype)

    def add(batch, part, from_ref):
        lanes = slice(part // 2 * LANES, (part // 2 + 1) * LANES)
        ranks = range(part % 2 * half, (part % 2 + 1) * half)
        strips = [slice(i, i + ROWS) for i in range(0, rank_i, ROWS)]
        totals = [[y_ref[r, strip, lanes] for strip in strips] for r in ranks]
        for place in range(BATCH):
            parts_of = []
            for i in range(0, rank_i, 2 * ROWS):
                wide = from_ref[place, i : i + 2 * ROWS, lanes].astype(jnp.float32)
                parts_of += [wide[:ROWS], wide[ROWS:]]
            for i, r in enumerate(ranks):
                values = context_held[batch * BATCH + place, r, :, lanes]
                for j in range(len(strips)):
                    totals[i][j] = totals[i][j] + values * parts_of[j]
        for i, r in enumerate(ranks):
            for strip, total in zip(strips, totals[i]):
                y_ref[r, strip, lanes] = total

    y_ref[...] = jnp.zeros_like(y_ref)
    parts = 2 * users // LANES
    wait(0)
    start(2)
    for place in range(BATCH):
        multiply(0, place, even_ref)

    def turn(batch, from_ref, into_ref):
        wait(batch + 1)

        @pl.when(batch + 3 < batches)
        def _():
            start(batch + 3)

        for place in range(BATCH):
            multiply(batch + 1, place, into_ref)
        for part in range(parts):
            add(batch, part, from_ref)

    def pair(index, _):
        turn(2 * index, even_ref, odd_ref)
        turn(2 * index + 1, odd_ref, even_ref)
        return 0

    lax.fori_loop(0, batches // 2 - 1, pair, 0)
    basis_copy = pltpu.make_async_copy(basis_ref, basis_held, basis_sem)
    basis_copy.start()
    turn(batches - 2, even_ref, odd_ref)
    for part in range(parts):
        add(batches - 1, part, odd_ref)

    living = lax.broadcasted_iota(jnp.int32, (rank_i, users), 1) < count_ref[0]
    ranks = rank_c * rank_i
    for r in range(rank_c):
        high, low = split(jnp.where(living, y_ref[r], 0.0))
        stack_ref[r * rank_i : (r + 1) * rank_i] = high
        stack_ref[ranks + r * rank_i : ranks + (r + 1) * rank_i] = low
    square_ref[...] = dot_nt(stack_ref[...], stack_ref[:ranks])
    basis_copy.wait()
    projection = dot(stack_ref[...], jnp.concatenate(split(basis_held[...]), axis=1))
    groups = ranks // LANES
    place = 0
    for i in range(groups):
        rows = slice(i * LANES, (i + 1) * LANES)
        low_rows = slice(ranks + i * LANES, ranks + (i + 1) * LANES)
        for j in range(i, groups):
            lanes = slice(j * LANES, (j + 1) * LANES)
            low_lanes = slice(ranks + j * LANES, ranks + (j + 1) * LANES)
            block = square_ref[rows, lanes] + square_ref[low_rows, lanes] + square_ref[low_lanes, rows].T
            pack_ref[place * LANES : (place + 1) * LANES] = block
            place += 1
    pack_ref[place * LANES : (place + groups) * LANES] = quarters(projection)
    chunk = piece_refs[0].shape[0]
    places = pack_places(me_ref[0])
    for piece, ref in zip(PIECES, piece_refs):
        ref[...] = pack_ref[pl.ds(pl.multiple_of(places[piece] * chunk, ROWS), chunk)]


def tile_sums(where, count, me, blocks, weights, contexts, user_basis):
    tiles, _, users = weights.shape
    rank_i = blocks.shape[1]
    rank_c = contexts.shape[1]
    ranks = rank_c * rank_i
    rows = pack_rows(ranks)
    out_shape = (jax.ShapeDtypeStruct((rows // CHUNKS, LANES), jnp.float32),) * len(PIECES)
    out_shape += (jax.ShapeDtypeStruct((2 * ranks, users), jnp.bfloat16),)
    held = 3 * weights.size * 2 // (2 * MIB)
    out = pl.pallas_call(
        tiles_kernel,
        out_shape=out_shape,
        in_specs=[SMEM] * 3 + [VMEM] + [ANY] * 3,
        out_specs=(VMEM,) * len(out_shape),
        scratch_shapes=[
            pltpu.VMEM((rank_c, rank_i, users), jnp.float32),
            pltpu.VMEM((2 * ranks, ranks), jnp.float32),
            pltpu.VMEM((rows, LANES), jnp.float32),
            pltpu.VMEM((BATCH, rank_i, users), jnp.bfloat16),
            pltpu.VMEM((BATCH, rank_i, users), jnp.bfloat16),
            pltpu.VMEM(weights.shape, weights.dtype),
            pltpu.VMEM(contexts.shape, contexts.dtype),
            pltpu.VMEM(user_basis.shape, user_basis.dtype),
            pltpu.SemaphoreType.DMA((tiles,)),
            pltpu.SemaphoreType.DMA((tiles // BATCH,)),
            pltpu.SemaphoreType.DMA,
        ],
        compiler_params=limit(12 + held + contexts.size * 4 // MIB),
        cost_estimate=pl.CostEstimate(flops=2 * 10**9, bytes_accessed=12 * 10**6, transcendentals=0),
        name="tile_sums",
    )(where, count, me, blocks, in_hbm(weights), in_hbm(contexts), in_hbm(user_basis))
    return dict(zip(PIECES, out[:-1])), out[-1]


def inverse_factor(gram, between):
    order = gram.shape[0]
    panels = order // ROWS
    sub = lax.broadcasted_iota(jnp.int32, (ROWS, order), 0)
    lane = lax.broadcasted_iota(jnp.int32, (ROWS, order), 1)
    left = [gram[ROWS * i : ROWS * (i + 1)] for i in range(panels)]
    right = [jnp.where(lane == sub + ROWS * i, 1.0, 0.0) for i in range(panels)]
    for k in range(panels):
        between(k)
        columns = {
            i: [
                jnp.broadcast_to(left[i][:, ROWS * k + j : ROWS * k + j + 1], (ROWS, order))
                for j in range(ROWS)
            ]
            for i in range(k, panels)
        }
        row, tail = left[k], right[k]
        scale = jnp.zeros((ROWS, order), jnp.float32)
        rows, tails = [], []
        for j in range(ROWS):
            head = columns[k][j]
            pivot = jnp.broadcast_to(head[j : j + 1], (ROWS, order))
            inverse = pl.reciprocal(pivot, approx=True)
            inverse = inverse * (2.0 - pivot * inverse)
            scale = jnp.where(sub == j, pivot, scale)
            rows.append(jnp.broadcast_to(row[j : j + 1], (ROWS, order)))
            tails.append(jnp.broadcast_to(tail[j : j + 1], (ROWS, order)))
            below = jnp.where(sub > j, head, 0.0) * inverse
            row = row - below * rows[j]
            tail = tail - below * tails[j]
            facts = {k: below}
            for i in range(k + 1, panels):
                facts[i] = columns[i][j] * inverse
            for c in range(j + 1, ROWS):
                crossing = jnp.broadcast_to(head[c : c + 1], (ROWS, order))
                for i in range(k, panels):
                    columns[i][c] = columns[i][c] - facts[i] * crossing
            for i in range(k + 1, panels):
                left[i] = left[i] - facts[i] * rows[j]
                right[i] = right[i] - facts[i] * tails[j]
        right[k] = tail * lax.rsqrt(scale)
    return jnp.concatenate(right, axis=0)


def finish_kernel(total_users, me_ref, stack_ref, *rest):
    piece_refs, rest = rest[: len(PIECES)], rest[len(PIECES) :]
    basis_ref, core_out_ref, pack_ref, full_ref, high_ref, low_ref = rest
    chunk = piece_refs[0].shape[0]
    places = pack_places(me_ref[0])
    for piece, ref in zip(PIECES, piece_refs):
        pack_ref[pl.ds(pl.multiple_of(places[piece] * chunk, ROWS), chunk)] = ref[...]
    ranks = full_ref.shape[1]
    groups = ranks // LANES
    place = 0
    for i in range(groups):
        for j in range(i, groups):
            block = pack_ref[place * LANES : (place + 1) * LANES]
            for row, lane, part in ((i, j, block), (j, i, block.T))[: 1 if i == j else 2]:
                lanes = slice(lane * LANES, (lane + 1) * LANES)
                high, low = split(part)
                full_ref[row * LANES : (row + 1) * LANES, lanes] = high
                full_ref[ranks + row * LANES : ranks + (row + 1) * LANES, lanes] = low
            place += 1
    projection = pack_ref[place * LANES : (place + groups) * LANES]
    crossed = quarters(dot(full_ref[...], jnp.concatenate(split(projection), axis=1)))
    crossed_high, crossed_low = split(crossed)
    turned = jnp.concatenate(
        [projection[i * LANES : (i + 1) * LANES].T for i in range(groups)], axis=1
    )
    turned_stack = jnp.concatenate(split(turned), axis=0)
    gram = quarters(dot(turned_stack, jnp.concatenate([crossed_high, crossed_low], axis=1)))
    strips = basis_ref.shape[0] // LANES

    def project(k):
        if k % 3 == 0 and k // 3 < strips:
            lanes = slice(k // 3 * LANES, (k // 3 + 1) * LANES)
            part = thrice(turned_stack, stack_ref[:ranks, lanes], stack_ref[ranks:, lanes], dot)
            high_ref[:, lanes], low_ref[:, lanes] = split(part)

    inverse_stack = jnp.concatenate(split(inverse_factor(gram, project)), axis=0)
    root = total_users ** 0.5
    scaled = thrice(inverse_stack, high_ref[...], low_ref[...], dot) * root
    for i in range(scaled.shape[1] // LANES):
        basis_ref[i * LANES : (i + 1) * LANES] = scaled[:, i * LANES : (i + 1) * LANES].T
    core_out_ref[...] = thrice(inverse_stack, crossed_high, crossed_low, dot_nt) * (1.0 / root)


def finish(me, stack, pieces, devices):
    ranks, users = stack.shape[0] // 2, stack.shape[1]
    return pl.pallas_call(
        functools.partial(finish_kernel, users * devices),
        out_shape=(
            jax.ShapeDtypeStruct((users, LANES), jnp.float32),
            jax.ShapeDtypeStruct((LANES, ranks), jnp.float32),
        ),
        in_specs=[SMEM] + [VMEM] * (1 + len(PIECES)),
        out_specs=(VMEM, VMEM),
        scratch_shapes=[
            pltpu.VMEM((pack_rows(ranks), LANES), jnp.float32),
            pltpu.VMEM((2 * ranks, ranks), jnp.bfloat16),
            pltpu.VMEM((LANES, users), jnp.bfloat16),
            pltpu.VMEM((LANES, users), jnp.bfloat16),
        ],
        compiler_params=limit(16),
        name="finish",
    )(me, stack, *[pieces[piece] for piece in PIECES])


def swap(value, mask, devices):
    return lax.ppermute(value, "users", [(i, i ^ mask) for i in range(devices)])


def encode(value):
    rows, lanes = value.shape
    groups = rows // GROUP
    parts = value.reshape(groups, GROUP, lanes)
    most = jnp.max(jnp.abs(parts), axis=1, keepdims=True)
    exponent = jnp.clip(jnp.floor(jnp.log2(most)) + 1.0, -110.0, 128.0)
    coded = jnp.clip(jnp.round(parts * jnp.exp2(14.0 - exponent)), -32767.0, 32767.0)
    extra = jnp.pad(exponent.reshape(groups, lanes), ((0, -groups % 16), (0, 0)))
    return jnp.concatenate([coded.reshape(rows, lanes), extra], axis=0).astype(jnp.int16)


def decode(coded, rows):
    lanes = coded.shape[1]
    groups = rows // GROUP
    scale = jnp.exp2(coded[rows : rows + groups].astype(jnp.float32) - 14.0)
    parts = coded[:rows].astype(jnp.float32).reshape(groups, GROUP, lanes)
    return (parts * scale.reshape(groups, 1, lanes)).reshape(rows, lanes)


def reduce_pieces(pieces, devices):
    rows = pieces[0, 0].shape[0]
    got = {plane: swap(pieces[1, plane], 1, devices) for plane in (3, 1, 2, 0)}
    total = pieces[0, 0] + got[0]
    for plane in (3, 1, 2):
        coded = encode(pieces[0, plane] + got[plane])
        total = total + decode(swap(coded, 2 * plane, devices), rows)
    mask = CHUNKS
    while mask < devices:
        coded = encode(total)
        total = decode(coded, rows) + decode(swap(coded, mask, devices), rows)
        mask *= 2
    return encode(total)


def spread_pieces(total, devices, rows):
    coded = {(0, 0): total}
    for plane in (3, 1, 2):
        coded[0, plane] = swap(total, 2 * plane, devices)
    for plane in (0, 3, 1, 2):
        coded[1, plane] = swap(coded[0, plane], 1, devices)
    return {piece: decode(value, rows) for piece, value in coded.items()}


def body(
    tile_owner, tile_slot, tile_cblock, tile_context, tile_weights,
    item_factors, context_factors, user_basis, user_counts,
):
    devices = lax.axis_size("users")
    half = devices // 2
    rank_c = context_factors.shape[0]
    me = lax.axis_index("users").astype(jnp.int32).reshape(1)

    mirror = swap(item_factors, half, devices)
    requests, where, own = route(me, tile_owner[:, 0], tile_slot, item_factors, half)
    sides = [list(range(half)), list(range(half, devices))]
    asked = lax.all_to_all(requests, "users", 0, 0, axis_index_groups=sides, tiled=True)
    found = collect(asked, own, mirror)
    found, cblock, factors = lax.optimization_barrier((found, tile_cblock, context_factors))
    blocks = lax.all_to_all(found, "users", 0, 0, axis_index_groups=sides, tiled=True)

    table = factors.astype(jnp.float32).reshape(rank_c, -1, CB).transpose(1, 0, 2)
    contexts = context_values(cblock, table, tile_context)
    pieces, stack = tile_sums(
        where, user_counts, me, blocks, tile_weights, contexts, user_basis
    )
    rows = pieces[0, 0].shape[0]
    pieces = spread_pieces(reduce_pieces(pieces, devices), devices, rows)
    return finish(me, stack, pieces, devices)


def solution(mesh):
    return jax.shard_map(
        body,
        mesh=mesh,
        in_specs=(
            P("users", None), P("users"), P("users"), P("users", None), P("users", None, None),
            P("users", None, None), P(), P("users", None), P("users"),
        ),
        out_specs=(P("users", None), P()),
        check_vma=False,
    )
```
